256 devices in a mesh: lat: 16 (over x_hi, z), lon: 16 (over x_lo, y, core).
Axes of the slice: x: 4 (x_hi: 2, x_lo: 2; x = x_hi * 2 + x_lo), y: 4, z: 8, core: 2. Of those that a mesh axis runs over, the one named last changes fastest.
Arguments:
- fields: bfloat16 [2, 192, 288, 384], P(None, 'lat', 'lon'), may hold values from -6 to 6
- cotangent: bfloat16 [2, 192, 288, 384], P(None, 'lat', 'lon'), may hold values from -6 to 6
- norm_gain: float32 [384], replicated, may hold values from 0.5 to 1.5
- w_query: bfloat16 [384, 384], P('lat', 'lon'), may hold values from -0.3125 to 0.3125
- w_key: bfloat16 [384, 384], P('lat', 'lon'), may hold values from -0.3125 to 0.3125
- w_value: bfloat16 [384, 384], P('lat', 'lon'), may hold values from -0.3125 to 0.3125
- w_out: bfloat16 [384, 384], P('lat', 'lon'), may hold values from -0.3125 to 0.3125
- rel_table: float32 [16, 12, 6336], P('lat'), may hold values from -4 to 304
Outputs:
- grad_fields: bfloat16 [2, 192, 288, 384], P(None, 'lat', 'lon')
- grad_query: float32 [384, 384], P('lat', 'lon')
- grad_key: float32 [384, 384], P('lat', 'lon')
- grad_value: float32 [384, 384], P('lat', 'lon')
- grad_out: float32 [384, 384], P('lat', 'lon')
- grad_table: float32 [16, 12, 6336], P('lat', None, 'lon')
- grad_gain: float32 [384], replicated
The draws below stay inside these ranges and needn't reach their ends.
All inputs are finite; a program needn't handle non-finite values.
Results may differ from the reference program's by a relative error of at most 0.03.
Values may be sent and summed in bfloat16 or wider, within the bound.
No kernel may reach another device: no remote copies, remote signals or barrier semaphores. Data moves between devices by JAX's collectives and lax.ppermute only.
A program may use at most 128 MiB of HBM per device.

```python
import math
import jax
import jax.numpy as jnp
from jax import lax

D = 384
H = 12
LEV = 2
WLAT = 12
WLON = 6
HW = 384
RELS = 11
PAIRS = 6336
NWLAT = 16
NLAT = 192
NLON = 288


def draw_rel_table(key, part):
    key = jax.random.fold_in(key, 7)
    key_base = jax.random.fold_in(key, 0)
    tab_shape = (NWLAT, H, LEV, LEV, WLAT, WLAT, RELS)
    base = jax.random.truncated_normal(key_base, -4.0, 4.0, tab_shape, jnp.float32)
    return base.reshape(NWLAT, H, PAIRS)


def spiked(result, rng, source, target, blocks, factor):
    def block_of(axis_at):
        return (jnp.arange(result.shape[axis_at]) // (result.shape[axis_at] // blocks)).reshape((-1,) + (1,) * (result.ndim - 1 - axis_at))

    near = jax.random.permutation(rng, blocks)[block_of(target)]
    second = (block_of(target) + blocks // 2) % blocks
    return jnp.where((block_of(source) == near) | (block_of(source) == second), factor * result, result)


def shard_levels(own_key, dims, pieces, least, largest):
    gain = 1.0
    for axis_at, parts in pieces:
        heights = jax.random.uniform(jax.random.fold_in(jax.random.fold_in(own_key, 6), axis_at), (parts,), jnp.float32, least / len(pieces), largest / len(pieces))
        gain = gain * jnp.repeat(jnp.exp(heights), dims[axis_at] // parts).reshape((-1,) + (1,) * (len(dims) - 1 - axis_at))
    return gain


def bell_draw(stream_key, extent, deviation, bound, shards=(), kind=jnp.bfloat16):
    loudness = shard_levels(stream_key, extent, shards, -0.22, 0.18) if shards else 1.0
    entries = jax.random.normal(stream_key, extent, jnp.float32) * deviation * loudness
    return jnp.minimum(jnp.maximum(entries, -bound), bound).astype(kind)


def bell_draw_with(key, extent, width, bound, shards, heavy, kind=jnp.bfloat16):
    entries = width * jax.random.normal(key, extent, jnp.float32)
    if shards:
        entries = entries * shard_levels(key, extent, shards, -0.22, 0.18)
    return jnp.clip(spiked(entries, jax.random.fold_in(key, 3), *heavy), -bound, bound).astype(kind)


def setup_inputs(seed: int = 0) -> dict:
    keys = jax.random.split(jax.random.key(seed), 9)
    fields = bell_draw(keys[0], (LEV, NLAT, NLON, D), 1.0, 6.0, ((1, 16), (2, 16)))
    cotangent = bell_draw_with(keys[1], (LEV, NLAT, NLON, D), 1.0, 6.0, ((1, 16), (2, 16)), (2, 3, 16, 2.0))
    norm_gain = jnp.clip(1.0 + 0.1 * jax.random.normal(keys[2], (D,), jnp.float32), 0.5, 1.5)
    w_query = bell_draw(keys[3], (D, HW), D ** -0.5, 0.3125, ((0, 16), (1, 16)))
    w_key = bell_draw(keys[4], (D, HW), D ** -0.5, 0.3125, ((0, 16), (1, 16)))
    w_value = bell_draw(keys[5], (D, HW), D ** -0.5, 0.3125, ((0, 16), (1, 16)))
    w_out = bell_draw(keys[6], (HW, D), HW ** -0.5, 0.3125, ((0, 16), (1, 16)))
    rel_table = draw_rel_table(jax.random.fold_in(keys[8], 71), 0)
    return {"fields": fields, "cotangent": cotangent, "norm_gain": norm_gain, "w_query": w_query, "w_key": w_key, "w_value": w_value, "w_out": w_out, "rel_table": rel_table}


EPSILON = 1e-05
MASKED = -1000000000.0
HIGHEST = lax.Precision.HIGHEST

def relative_table(rel_count, lon_width):
    rel_ids = jnp.arange(rel_count)[:, None, None]
    lon_query = jnp.arange(lon_width)[None, :, None]
    lon_key = jnp.arange(lon_width)[None, None, :]
    return (lon_query - lon_key + (lon_width - 1) == rel_ids).astype(jnp.float32)

def expand_bias(rel_tab, spread, levels, lat_rows):
    head_count = rel_tab.shape[0]
    lon_width = spread.shape[1]
    shaped = rel_tab.reshape(head_count, levels, levels, lat_rows, lat_rows, spread.shape[0])
    expanded = jnp.einsum('hzwabr,rpq->hzapwbq', shaped, spread, precision=HIGHEST)
    win_size = levels * lat_rows * lon_width
    return expanded.reshape(head_count, win_size, win_size)

def fold_bias(d_bias, spread, levels, lat_rows):
    head_count = d_bias.shape[0]
    lon_width = spread.shape[1]
    grid_ds = d_bias.reshape(head_count, levels, lat_rows, lon_width, levels, lat_rows, lon_width)
    folded = jnp.einsum('hzapwbq,rpq->hzwabr', grid_ds, spread, precision=HIGHEST)
    return folded.reshape(head_count, -1)

def cross_mask(levels, lat_rows, lon_width):
    token_ids = jnp.arange(levels * lat_rows * lon_width)
    northern = token_ids // lon_width % lat_rows < lat_rows // 2
    return northern[:, None] != northern[None, :]

def to_windows(tensor, lat_rows, lon_width):
    levels, lat_all, lon_all, features = tensor.shape
    blocks = tensor.reshape(levels, lat_all // lat_rows, lat_rows, lon_all // lon_width, lon_width, features)
    blocks = blocks.transpose(1, 3, 0, 2, 4, 5)
    return blocks.reshape(lat_all // lat_rows, lon_all // lon_width, levels * lat_rows * lon_width, features)

def from_windows(blocks, levels, lat_rows, lon_width):
    lat_count, lon_count, win_size, features = blocks.shape
    grid_back = blocks.reshape(lat_count, lon_count, levels, lat_rows, lon_width, features)
    grid_back = grid_back.transpose(2, 0, 3, 1, 4, 5)
    return grid_back.reshape(levels, lat_count * lat_rows, lon_count * lon_width, features)

def layer_norm(flat_raw, norm_gain):
    values_f = flat_raw.astype(jnp.float32)
    row_mean = lax.optimization_barrier(jnp.mean(values_f, axis=-1, keepdims=True))
    centred = values_f - row_mean
    row_var = lax.optimization_barrier(jnp.mean(centred * centred, axis=-1, keepdims=True))
    inv_std = 1.0 / jnp.sqrt(row_var + EPSILON)
    standard = centred * inv_std
    normed = (standard * norm_gain).astype(jnp.bfloat16)
    return (normed, standard, inv_std)

def attend(queries, keys_in, values_in, d_context, rel_tab, is_last, head_count, levels, lat_rows, lon_width):
    win_count, win_size, hidden = queries.shape
    head_dim = hidden // head_count
    score_scale = 1.0 / math.sqrt(head_dim)
    spread = relative_table(2 * lon_width - 1, lon_width)

    def heads_of(tensor):
        return tensor.reshape(win_count, win_size, head_count, head_dim).astype(jnp.float32)
    query_h = heads_of(queries)
    key_h = heads_of(keys_in)
    value_h = heads_of(values_in)
    dctx_h = heads_of(d_context)
    scores = jnp.einsum('nqhd,nkhd->nhqk', query_h, key_h) * score_scale
    scores = scores + expand_bias(rel_tab, spread, levels, lat_rows)[None]
    blocked = jnp.logical_and(is_last, cross_mask(levels, lat_rows, lon_width))
    scores = jnp.where(blocked[None, None], MASKED, scores)
    row_max = lax.optimization_barrier(jnp.max(scores, axis=-1, keepdims=True))
    expos = jnp.exp(scores - row_max)
    probs = expos / lax.optimization_barrier(jnp.sum(expos, axis=-1, keepdims=True))
    probs_low = lax.optimization_barrier(probs.astype(jnp.bfloat16)).astype(jnp.float32)
    context = jnp.einsum('nhqk,nkhd->nqhd', probs_low, value_h).astype(jnp.bfloat16).reshape(win_count, win_size, hidden)
    d_probs = jnp.einsum('nqhd,nkhd->nhqk', dctx_h, value_h)
    d_value = jnp.einsum('nhqk,nqhd->nkhd', probs_low, dctx_h).astype(jnp.bfloat16).reshape(win_count, win_size, hidden)
    d_scores = probs * (d_probs - lax.optimization_barrier(jnp.sum(probs * d_probs, axis=-1, keepdims=True)))
    d_table = fold_bias(lax.optimization_barrier(jnp.sum(d_scores, axis=0)), spread, levels, lat_rows)
    d_low = lax.optimization_barrier((d_scores * score_scale).astype(jnp.bfloat16)).astype(jnp.float32)
    d_query = jnp.einsum('nhqk,nkhd->nqhd', d_low, key_h).astype(jnp.bfloat16).reshape(win_count, win_size, hidden)
    d_key = jnp.einsum('nhqk,nqhd->nkhd', d_low, query_h).astype(jnp.bfloat16).reshape(win_count, win_size, hidden)
    return (context, d_query, d_key, d_value, d_table)

def reference(fields, cotangent, norm_gain, w_query, w_key, w_value, w_out, rel_table):
    half_rows = WLAT // 2
    half_cols = WLON // 2
    shifted = jnp.roll(fields, (-half_rows, -half_cols), axis=(1, 2))
    cot_shift = jnp.roll(cotangent, (-half_rows, -half_cols), axis=(1, 2))
    normed, standard, inv_std = layer_norm(shifted.reshape(-1, D), norm_gain)
    queries = jnp.dot(normed, w_query, preferred_element_type=jnp.float32).astype(jnp.bfloat16)
    keys_all = jnp.dot(normed, w_key, preferred_element_type=jnp.float32).astype(jnp.bfloat16)
    values_all = jnp.dot(normed, w_value, preferred_element_type=jnp.float32).astype(jnp.bfloat16)
    flat_cot = cot_shift.reshape(-1, D)
    d_context = jnp.dot(flat_cot, w_out.T, preferred_element_type=jnp.float32).astype(jnp.bfloat16)

    def window_of(tensor):
        return to_windows(tensor.reshape(LEV, NLAT, NLON, -1), WLAT, WLON)

    def per_row(packed):
        q_row, k_row, v_row, d_row, tab_row, lat_window = packed
        return attend(q_row, k_row, v_row, d_row, tab_row, lat_window == NWLAT - 1, H, LEV, WLAT, WLON)
    results = lax.map(per_row, (window_of(queries), window_of(keys_all), window_of(values_all), window_of(d_context), rel_table, jnp.arange(NWLAT, dtype=jnp.int32)))
    context, d_query, d_key, d_value, grad_table = results

    def flat_of(blocks):
        return from_windows(blocks, LEV, WLAT, WLON).reshape(-1, blocks.shape[-1])
    context = flat_of(context)
    d_query = flat_of(d_query)
    d_key = flat_of(d_key)
    d_value = flat_of(d_value)
    grad_out = jnp.dot(context.T, flat_cot, preferred_element_type=jnp.float32)
    d_normed = jnp.dot(d_query, w_query.T, preferred_element_type=jnp.float32)
    d_normed = d_normed + jnp.dot(d_key, w_key.T, preferred_element_type=jnp.float32)
    d_normed = d_normed + jnp.dot(d_value, w_value.T, preferred_element_type=jnp.float32)
    grad_query = jnp.dot(normed.T, d_query, preferred_element_type=jnp.float32)
    grad_key = jnp.dot(normed.T, d_key, preferred_element_type=jnp.float32)
    grad_value = jnp.dot(normed.T, d_value, preferred_element_type=jnp.float32)
    grad_gain = lax.optimization_barrier(jnp.sum(d_normed * standard, axis=0))
    d_standard = d_normed * norm_gain
    d_input = inv_std * (d_standard - lax.optimization_barrier(jnp.mean(d_standard, axis=-1, keepdims=True)) - standard * lax.optimization_barrier(jnp.mean(d_standard * standard, axis=-1, keepdims=True)))
    d_input = d_input.astype(jnp.bfloat16).reshape(LEV, NLAT, NLON, D)
    back = jnp.roll(d_input, (half_rows, half_cols), axis=(1, 2))
    grad_fields = (cotangent.astype(jnp.float32) + back.astype(jnp.float32)).astype(jnp.bfloat16)
    return (grad_fields, grad_query, grad_key, grad_value, grad_out, grad_table, grad_gain)
```

```python
import functools
import math

import jax
import jax.numpy as jnp
from jax import lax
from jax.experimental import pallas as pl
from jax.experimental.pallas import tpu as pltpu
from jax.sharding import PartitionSpec as P

EPSILON = 1e-05
MASKED = -1000000000.0
F32 = jnp.float32
BF16 = jnp.bfloat16
NN = (((1,), (0,)), ((), ()))
NT = (((1,), (1,)), ((), ()))
TN = (((0,), (0,)), ((), ()))


def mm(a, b, dims):
    return lax.dot_general(a, b, dims, preferred_element_type=F32)


def block_kernel(
    me_ref, x_ref, c_ref, gain_ref, w_ref, bias_ref,
    din_ref, gw_ref, gtab_ref, ggain_ref,
    w_s, gw_s, std_s, inv_s, normed_s, qkv_t, dctx_t, ktok, vtok, dqkv_t, ctx_t, bias_s, dsum_s,
    *, heads, windows, tokens, lon_width,
):
    feat = x_ref.shape[1]
    dim = feat // heads
    group = 128 // dim
    cell = tokens // lon_width
    scale = 1.0 / math.sqrt(dim)
    lanes = bias_ref.shape[2]
    sectors, packed, _ = w_ref.shape
    part = packed // 4
    me = me_ref[0]

    for r in range(sectors):
        block = w_ref[r].astype(F32)
        owner = jnp.bitwise_xor(me, r)
        start = pl.multiple_of(owner * part, part)
        for i in range(4):
            w_s[i, pl.ds(start, part), :] = block[i * part:(i + 1) * part]

    xf = x_ref[...].astype(F32)
    mean = jnp.mean(xf, axis=1, keepdims=True)
    centred = xf - mean
    var = jnp.mean(centred * centred, axis=1, keepdims=True)
    inv = 1.0 / jnp.sqrt(var + EPSILON)
    std = centred * inv
    std_s[...] = std
    inv_s[...] = inv
    normed_s[...] = (std * gain_ref[...]).astype(BF16)
    w_out = w_s[3].T.astype(BF16)
    w_qkv = w_s[0:3].reshape(3 * feat, feat).astype(BF16)
    w_key = w_qkv[feat:2 * feat]
    w_value = w_qkv[2 * feat:]
    for w in range(windows):
        rows = slice(w * tokens, (w + 1) * tokens)
        nw = normed_s[rows]
        qkv_t[w] = mm(w_qkv, nw, NT).astype(BF16)
        dctx_t[w] = mm(w_out, c_ref[rows], NT).astype(BF16)
        kt = mm(nw, w_key, NT).astype(BF16)
        vt = mm(nw, w_value, NT).astype(BF16)
        for g in range(feat // 128):
            ktok[g, w] = kt[:, g * 128:(g + 1) * 128]
            vtok[g, w] = vt[:, g * 128:(g + 1) * 128]

    sub = lax.broadcasted_iota(jnp.int32, (128, tokens), 0) // dim
    dsum_s[...] = jnp.zeros_like(dsum_s)

    def head(h, carry):
        strip = bias_ref[h]
        for q in range(lon_width):
            off = (lon_width - 1 - q) * cell
            rolled = pltpu.roll(strip, lanes - off, 1) if off else strip
            bias_s[q * cell:(q + 1) * cell, :] = rolled[:, :tokens]
        g = h // group
        inside = sub == h % group
        gbase = pl.multiple_of(g * 128, 128)
        qbase = pl.multiple_of(h * dim, dim)
        kbase = pl.multiple_of(feat + h * dim, dim)
        vbase = pl.multiple_of(2 * feat + h * dim, dim)
        total = jnp.zeros((tokens, tokens), F32)
        for w in range(windows):
            q_grp = qkv_t[w, pl.ds(gbase, 128), :]
            d_grp = dctx_t[w, pl.ds(gbase, 128), :]
            zero = jnp.zeros_like(q_grp)
            score = mm(ktok[g, w], jnp.where(inside, q_grp, zero), NN) * scale + bias_s[...]
            d_prob = mm(vtok[g, w], jnp.where(inside, d_grp, zero), NN)
            top = jnp.max(score, axis=0, keepdims=True)
            expo = jnp.exp(score - top)
            prob = expo * (1.0 / jnp.sum(expo, axis=0, keepdims=True))
            low = prob.astype(BF16)
            qh = qkv_t[w, pl.ds(qbase, dim), :]
            kh = qkv_t[w, pl.ds(kbase, dim), :]
            vh = qkv_t[w, pl.ds(vbase, dim), :]
            dh = dctx_t[w, pl.ds(qbase, dim), :]
            ctx_t[w, pl.ds(qbase, dim), :] = mm(vh, low, NN).astype(BF16)
            dqkv_t[w, pl.ds(vbase, dim), :] = mm(dh, low, NT).astype(BF16)
            inner = jnp.sum(prob * d_prob, axis=0, keepdims=True)
            d_score = prob * (d_prob - inner)
            total = total + d_score
            d_low = (d_score * scale).astype(BF16)
            dqkv_t[w, pl.ds(qbase, dim), :] = mm(kh, d_low, NN).astype(BF16)
            dqkv_t[w, pl.ds(kbase, dim), :] = mm(qh, d_low, NT).astype(BF16)
        dsum_s[:, :tokens] = total.T
        folded = jnp.zeros((cell, lanes), F32)
        for p in range(lon_width):
            off = (lon_width - 1 - p) * cell
            piece = dsum_s[p * cell:(p + 1) * cell, :]
            folded = folded + (pltpu.roll(piece, off, 1) if off else piece)
        gtab_ref[h] = folded
        return carry

    lax.fori_loop(0, heads, head, 0)

    g_qkv = jnp.zeros((3 * feat, feat), F32)
    g_out = jnp.zeros((feat, feat), F32)
    g_gain = jnp.zeros((1, feat), F32)
    for w in range(windows):
        rows = slice(w * tokens, (w + 1) * tokens)
        g_qkv = g_qkv + mm(dqkv_t[w], normed_s[rows], NN)
        g_out = g_out + mm(ctx_t[w], c_ref[rows], NN)
        d_normed = mm(dqkv_t[w], w_qkv, TN)
        std = std_s[rows]
        prod = d_normed * std
        g_gain = g_gain + jnp.sum(prod, axis=0, keepdims=True)
        g = d_normed * gain_ref[...]
        d_in = inv_s[rows] * (
            g - jnp.mean(g, axis=1, keepdims=True)
            - std * jnp.mean(prod * gain_ref[...], axis=1, keepdims=True)
        )
        din_ref[rows] = d_in.astype(BF16)
    gw_s[0:3] = g_qkv.reshape(3, feat, feat)
    gw_s[3] = g_out.T
    for r in range(sectors):
        owner = jnp.bitwise_xor(me, r)
        start = pl.multiple_of(owner * part, part)
        block = jnp.concatenate([gw_s[i, pl.ds(start, part), :] for i in range(4)], axis=0)
        gw_ref[r] = block.astype(BF16)
    ggain_ref[...] = g_gain


def run_block(me, x, c, gain, w_all, strips, heads, windows, lon_width, interpret=False):
    rows, feat = x.shape
    tokens = rows // windows
    cell = tokens // lon_width
    lanes = strips.shape[2]
    vmem = pl.BlockSpec(memory_space=pltpu.VMEM)
    return pl.pallas_call(
        functools.partial(block_kernel, heads=heads, windows=windows, tokens=tokens, lon_width=lon_width),
        out_shape=(
            jax.ShapeDtypeStruct((rows, feat), BF16),
            jax.ShapeDtypeStruct(w_all.shape, BF16),
            jax.ShapeDtypeStruct((heads, cell, lanes), F32),
            jax.ShapeDtypeStruct((1, feat), F32),
        ),
        in_specs=[pl.BlockSpec(memory_space=pltpu.SMEM)] + [vmem] * 5,
        out_specs=[vmem] * 4,
        scratch_shapes=[
            pltpu.VMEM((4, feat, feat), F32),
            pltpu.VMEM((4, feat, feat), F32),
            pltpu.VMEM((rows, feat), F32),
            pltpu.VMEM((rows, 1), F32),
            pltpu.VMEM((rows, feat), BF16),
            pltpu.VMEM((windows, 3 * feat, tokens), BF16),
            pltpu.VMEM((windows, feat, tokens), BF16),
            pltpu.VMEM((feat // 128, windows, tokens, 128), BF16),
            pltpu.VMEM((feat // 128, windows, tokens, 128), BF16),
            pltpu.VMEM((windows, 3 * feat, tokens), BF16),
            pltpu.VMEM((windows, feat, tokens), BF16),
            pltpu.VMEM((tokens, tokens), F32),
            pltpu.VMEM((tokens, lanes), F32),
        ],
        compiler_params=pltpu.CompilerParams(vmem_limit_bytes=48 * 1024 * 1024),
        interpret=interpret,
    )(me, x, c, gain, w_all, strips)


def swap(x, axis, bit):
    n = lax.axis_size(axis)
    return lax.ppermute(x, axis, [(i, i ^ bit) for i in range(n)])


def shift(x, lat_by, lon_by):
    lats, lons = lax.axis_size("lat"), lax.axis_size("lon")
    if lon_by == 0:
        return lax.ppermute(x, "lat", [(i, (i + lat_by) % lats) for i in range(lats)])
    if lat_by == 0:
        return lax.ppermute(x, "lon", [(i, (i + lon_by) % lons) for i in range(lons)])
    pairs = [
        (a * lons + b, (a + lat_by) % lats * lons + (b + lon_by) % lons)
        for a in range(lats)
        for b in range(lons)
    ]
    return lax.ppermute(x, ("lat", "lon"), pairs)


def gather_relative(x, axis):
    held = x[None]
    bit = 1
    while bit < lax.axis_size(axis):
        held = jnp.concatenate([held, swap(held, axis, bit)], axis=0)
        bit *= 2
    return held


def scatter_relative(x, axis):
    total = x
    bit = lax.axis_size(axis) // 2
    while bit:
        sent = total[bit:].astype(BF16)
        total = total[:bit].astype(F32) + swap(sent, axis, bit).astype(F32)
        bit //= 2
    return total[0]


def relative(x, me):
    n = x.shape[0]
    bit = 1
    while bit < n:
        y = x.reshape((n // (2 * bit), 2, bit) + x.shape[1:])
        x = jnp.where((me & bit) != 0, y[:, ::-1], y).reshape(x.shape)
        bit *= 2
    return x


def local(fields, cotangent, norm_gain, w_query, w_key, w_value, w_out, rel_table):
    levels, lat_rows, lon_cols, feat = fields.shape
    heads = rel_table.shape[1]
    rels = rel_table.shape[2] // (levels * levels * lat_rows * lat_rows)
    lon_width = (rels + 1) // 2
    half_rows = lat_rows // 2
    half_cols = lon_width // 2
    windows = lon_cols // lon_width
    cell = levels * lat_rows
    lats = lax.axis_size("lat")
    lons = lax.axis_size("lon")
    me_lat = lax.axis_index("lat")
    me_lon = lax.axis_index("lon")

    mine = jnp.concatenate([w_query, w_key, w_value, w_out], axis=1)
    rows_all = relative(gather_relative(mine, "lat"), me_lat)
    turned = rows_all.reshape(feat, mine.shape[1]).T
    w_all = gather_relative(turned, "lon")

    both = jnp.stack([fields, cotangent]).transpose(3, 0, 1, 2, 4)
    own = both[half_cols:, :, :, half_rows:]
    south = shift(both[half_cols:, :, :, :half_rows], -1, 0)
    east = shift(both[:half_cols, :, :, half_rows:], 0, -1)
    corner = shift(both[:half_cols, :, :, :half_rows], -1, -1)
    moved = jnp.concatenate(
        [jnp.concatenate([own, south], axis=3), jnp.concatenate([east, corner], axis=3)], axis=0
    )
    shifted = moved[:, 0].reshape(-1, feat)
    cot_shift = moved[:, 1].reshape(-1, feat)

    table = rel_table[0].reshape(heads, levels, levels, lat_rows, lat_rows, rels)
    strips = table.transpose(0, 2, 4, 5, 1, 3)
    northern = jnp.arange(lat_rows) < half_rows
    crossing = northern[:, None, None, None] != northern[None, None, None, :]
    strips = jnp.where(jnp.logical_and(me_lat == lats - 1, crossing), MASKED, strips)
    strips = strips.reshape(heads, cell, rels * cell)
    pad = -(rels * cell) % 128
    strips = jnp.pad(strips, ((0, 0), (0, 0), (0, pad)))

    d_input, g_weights, g_table, g_gain = run_block(
        me_lon.reshape(1), shifted, cot_shift, norm_gain[None], w_all, strips, heads, windows, lon_width
    )

    part = scatter_relative(g_weights, "lon")
    part = part.T.reshape(lats, feat // lats, -1)
    part = scatter_relative(relative(part, me_lat), "lat")
    grad_query, grad_key, grad_value, grad_out = jnp.split(part, 4, axis=1)

    per = lons // (levels * levels)
    rows = lat_rows // per
    sent = g_table[:, :, : rels * cell].reshape(heads, levels, per, rows, rels, levels, lat_rows)
    sent = sent.transpose(1, 5, 2, 0, 3, 6, 4)[..., ::-1]
    sent = sent.reshape(lons, heads, rows * lat_rows * rels).astype(BF16)
    grad_table = scatter_relative(relative(sent, me_lon), "lon")[None]

    gain_sum = g_gain[0]
    for axis in ("lon", "lat"):
        bit = 1
        while bit < lax.axis_size(axis):
            gain_sum = gain_sum + swap(gain_sum, axis, bit)
            bit *= 2

    d_in = d_input.reshape(lon_cols, levels, lat_rows, feat)
    stay = lon_cols - half_cols
    west = shift(d_in[stay:, :, :half_rows], 0, 1)
    north = shift(d_in[:stay, :, half_rows:], 1, 0)
    corner = shift(d_in[stay:, :, half_rows:], 1, 1)
    back = jnp.concatenate(
        [jnp.concatenate([corner, west], axis=2), jnp.concatenate([north, d_in[:stay, :, :half_rows]], axis=2)],
        axis=0,
    ).transpose(1, 2, 0, 3)
    grad_fields = (cotangent.astype(F32) + back.astype(F32)).astype(BF16)
    return (grad_fields, grad_query, grad_key, grad_value, grad_out, grad_table, gain_sum)


def solution(mesh):
    return jax.shard_map(
        local,
        mesh=mesh,
        in_specs=(
            P(None, "lat", "lon", None),
            P(None, "lat", "lon", None),
            P(),
            P("lat", "lon"),
            P("lat", "lon"),
            P("lat", "lon"),
            P("lat", "lon"),
            P("lat", None, None),
        ),
        out_specs=(
            P(None, "lat", "lon", None),
            P("lat", "lon"),
            P("lat", "lon"),
            P("lat", "lon"),
            P("lat", "lon"),
            P("lat", None, "lon"),
            P(),
        ),
        check_vma=False,
    )
```

```python
import functools
import math

import jax
import jax.numpy as jnp
import numpy as np
from jax import lax
from jax.experimental import pallas as pl
from jax.experimental.pallas import tpu as pltpu
from jax.sharding import PartitionSpec as P

EPSILON = 1e-05
MASKED = -1000000000.0
F32 = jnp.float32
BF16 = jnp.bfloat16
NN = (((1,), (0,)), ((), ()))
NT = (((1,), (1,)), ((), ()))
TN = (((0,), (0,)), ((), ()))


def mm(a, b, dims):
    return lax.dot_general(a, b, dims, preferred_element_type=F32)


def offset_order(rels, levels, lat_rows, group):
    lanes = rels * levels * lat_rows
    order = np.zeros((levels * group, lanes + -lanes % 128), np.float32)
    for level in range(levels):
        for lat in range(lat_rows):
            for rel in range(rels):
                order[level * group + lat * rels + rel, ((rels - 1 - rel) * levels + level) * lat_rows + lat] = 1.0
    return order


def strips_kernel(last_ref, table_ref, order_ref, out_ref, table_s, *, levels, lat_rows, rels):
    heads = table_ref.shape[0]
    slots = table_s.shape[1]
    cell = levels * lat_rows
    width = lat_rows * rels
    group = table_s.shape[2] // levels
    table_s[...] = jnp.zeros_like(table_s)
    table = table_ref[...]
    for z in range(levels):
        for w in range(levels):
            for a in range(lat_rows):
                at = ((z * levels + w) * lat_rows + a) * width
                table_s[z * lat_rows + a, 0:heads, w * group:w * group + width] = table[:, at:at + width]
    full = table_s[...].reshape(cell * slots, levels * group)
    order = order_ref[...]
    high = full.astype(BF16)
    rest = full - high.astype(F32)
    mid = rest.astype(BF16)
    low = (rest - mid.astype(F32)).astype(BF16)
    strips = mm(high, order, NN) + mm(mid, order, NN) + mm(low, order, NN)
    row = lax.broadcasted_iota(jnp.int32, (cell * slots, 1), 0) // slots
    lane = lax.broadcasted_iota(jnp.int32, (1, strips.shape[1]), 1)
    row_north = (row % lat_rows < lat_rows // 2).astype(F32)
    lane_north = (lane % lat_rows < lat_rows // 2).astype(F32)
    crossing = (row_north != lane_north) & (last_ref[0] != 0)
    strips = jnp.where(crossing, MASKED, strips)
    for g in range(out_ref.shape[0]):
        out_ref[g] = strips[:, g * 128:(g + 1) * 128]


def make_strips(last, table, order, levels, lat_rows, rels, slots):
    heads = table.shape[0]
    vmem = pl.BlockSpec(memory_space=pltpu.VMEM)
    return pl.pallas_call(
        functools.partial(strips_kernel, levels=levels, lat_rows=lat_rows, rels=rels),
        out_shape=jax.ShapeDtypeStruct((order.shape[1] // 128, levels * lat_rows * slots, 128), F32),
        in_specs=[pl.BlockSpec(memory_space=pltpu.SMEM), vmem, vmem],
        out_specs=vmem,
        scratch_shapes=[pltpu.VMEM((levels * lat_rows, slots, order.shape[0]), F32)],
        compiler_params=pltpu.CompilerParams(vmem_limit_bytes=32 * 1024 * 1024),
        name="bias_strips",
    )(last, table, order)


def turn_kernel(x_ref, out_ref):
    blocks, rows, lanes = x_ref.shape
    turned = x_ref[...].astype(F32).reshape(blocks * rows, lanes).T.astype(BF16)
    for i in range(out_ref.shape[0]):
        out_ref[i] = turned


def turn(x, copies):
    blocks, rows, lanes = x.shape
    vmem = pl.BlockSpec(memory_space=pltpu.VMEM)
    return pl.pallas_call(
        turn_kernel,
        out_shape=jax.ShapeDtypeStruct((copies, lanes, blocks * rows), BF16),
        in_specs=[vmem],
        out_specs=vmem,
        name="turn_weights",
    )(x)


def block_kernel(
    me_ref, x_ref, c_ref, gain_ref, w_same_ref, w_other_ref, strips_ref, order_ref,
    din_ref, same_ref, other_ref, ggain_ref,
    w_s, gw_s, std_s, inv_s, normed_s, qkv_t, dctx_t, ktok, vtok, dqkv_t, ctx_t, bias_s, dsum_s, fold_s,
    *, heads, windows, tokens, lon_width, levels, lat_rows, rels,
):
    feat = x_ref.shape[1]
    dim = feat // heads
    group = 128 // dim
    cell = tokens // lon_width
    scale = 1.0 / math.sqrt(dim)
    tiles = strips_ref.shape[0]
    lanes = tiles * 128
    slots = strips_ref.shape[1] // cell
    pairs, packed, _ = w_same_ref.shape
    part = packed // 4
    parity = me_ref[0] % 2

    for ref, side in ((w_same_ref, parity), (w_other_ref, 1 - parity)):
        for i in range(pairs):
            block = ref[i].astype(F32)
            start = pl.multiple_of((2 * i + side) * part, part)
            for k in range(4):
                w_s[k, pl.ds(start, part), :] = block[k * part:(k + 1) * part]

    xf = x_ref[...].astype(F32)
    mean = jnp.mean(xf, axis=1, keepdims=True)
    centred = xf - mean
    var = jnp.mean(centred * centred, axis=1, keepdims=True)
    inv = 1.0 / jnp.sqrt(var + EPSILON)
    std = centred * inv
    std_s[...] = std
    inv_s[...] = inv
    normed_s[...] = (std * gain_ref[...]).astype(BF16)
    w_out = w_s[3].T.astype(BF16)
    w_qkv = w_s[0:3].reshape(3 * feat, feat).astype(BF16)
    w_key = w_qkv[feat:2 * feat]
    w_value = w_qkv[2 * feat:]
    for w in range(windows):
        rows = slice(w * tokens, (w + 1) * tokens)
        nw = normed_s[rows]
        qkv_t[w] = mm(w_qkv, nw, NT).astype(BF16)
        dctx_t[w] = mm(w_out, c_ref[rows], NT).astype(BF16)
        kt = mm(nw, w_key, NT).astype(BF16)
        vt = mm(nw, w_value, NT).astype(BF16)
        for g in range(feat // 128):
            ktok[g, w] = kt[:, g * 128:(g + 1) * 128]
            vtok[g, w] = vt[:, g * 128:(g + 1) * 128]

    sub = lax.broadcasted_iota(jnp.int32, (128, tokens), 0) // dim
    dsum_s[...] = jnp.zeros_like(dsum_s)
    fold_s[...] = jnp.zeros_like(fold_s)

    def head(h, carry):
        strip = jnp.concatenate([strips_ref[g, pl.ds(h, cell, stride=slots), :] for g in range(tiles)], axis=1)
        for p in range(lon_width):
            off = (lon_width - 1 - p) * cell
            rolled = pltpu.roll(strip, lanes - off, 1) if off else strip
            bias_s[p * cell:(p + 1) * cell, :] = rolled[:, :tokens]
        bias = bias_s[...].T
        g = h // group
        inside = sub == h % group
        gbase = pl.multiple_of(g * 128, 128)
        qbase = pl.multiple_of(h * dim, dim)
        kbase = pl.multiple_of(feat + h * dim, dim)
        vbase = pl.multiple_of(2 * feat + h * dim, dim)
        total = jnp.zeros((tokens, tokens), F32)
        for w in range(windows):
            q_grp = qkv_t[w, pl.ds(gbase, 128), :]
            d_grp = dctx_t[w, pl.ds(gbase, 128), :]
            zero = jnp.zeros_like(q_grp)
            score = mm(ktok[g, w], jnp.where(inside, q_grp, zero), NN) * scale + bias
            d_prob = mm(vtok[g, w], jnp.where(inside, d_grp, zero), NN)
            top = jnp.max(score, axis=0, keepdims=True)
            expo = jnp.exp(score - top)
            prob = expo * (1.0 / jnp.sum(expo, axis=0, keepdims=True))
            low = prob.astype(BF16)
            qh = qkv_t[w, pl.ds(qbase, dim), :]
            kh = qkv_t[w, pl.ds(kbase, dim), :]
            vh = qkv_t[w, pl.ds(vbase, dim), :]
            dh = dctx_t[w, pl.ds(qbase, dim), :]
            ctx_t[w, pl.ds(qbase, dim), :] = mm(vh, low, NN).astype(BF16)
            dqkv_t[w, pl.ds(vbase, dim), :] = mm(dh, low, NT).astype(BF16)
            inner = jnp.sum(prob * d_prob, axis=0, keepdims=True)
            d_score = prob * (d_prob - inner)
            total = total + d_score
            d_low = (d_score * scale).astype(BF16)
            dqkv_t[w, pl.ds(qbase, dim), :] = mm(kh, d_low, NN).astype(BF16)
            dqkv_t[w, pl.ds(kbase, dim), :] = mm(qh, d_low, NT).astype(BF16)
        dsum_s[:, :tokens] = total.T
        folded = jnp.zeros((cell, lanes), F32)
        for p in range(lon_width):
            off = (lon_width - 1 - p) * cell
            piece = dsum_s[p * cell:(p + 1) * cell, :]
            folded = folded + (pltpu.roll(piece, off, 1) if off else piece)
        for g in range(tiles):
            fold_s[g, pl.ds(h, cell, stride=slots), :] = folded[:, g * 128:(g + 1) * 128]
        return carry

    lax.fori_loop(0, heads, head, 0)

    g_qkv = jnp.zeros((3 * feat, feat), F32)
    g_out = jnp.zeros((feat, feat), F32)
    g_gain = jnp.zeros((1, feat), F32)
    for w in range(windows):
        rows = slice(w * tokens, (w + 1) * tokens)
        g_qkv = g_qkv + mm(dqkv_t[w], normed_s[rows], NN)
        g_out = g_out + mm(ctx_t[w], c_ref[rows], NN)
        d_normed = mm(dqkv_t[w], w_qkv, TN)
        std = std_s[rows]
        prod = d_normed * std
        g_gain = g_gain + jnp.sum(prod, axis=0, keepdims=True)
        g = d_normed * gain_ref[...]
        d_in = inv_s[rows] * (
            g - jnp.mean(g, axis=1, keepdims=True)
            - std * jnp.mean(prod * gain_ref[...], axis=1, keepdims=True)
        )
        din_ref[rows] = d_in.astype(BF16)
    gw_s[0:3] = g_qkv.reshape(3, feat, feat)
    gw_s[3] = g_out.T
    ggain_ref[...] = g_gain

    fold = jnp.concatenate([fold_s[g] for g in range(tiles)], axis=1).astype(BF16)
    back = mm(fold, order_ref[...], NT)
    width = lat_rows * rels
    half = back.shape[1] // levels
    per = 2 * pairs // (levels * levels)
    run = lat_rows // per
    wide = -(-run * width // 128) * 128
    back = back.reshape(levels * per, run, slots, levels * half)
    full = []
    for w in range(levels):
        line = jnp.zeros((levels * per * slots, wide), F32)
        for k in range(run):
            piece = back[:, k, :, w * half:(w + 1) * half].reshape(levels * per * slots, half)
            piece = jnp.concatenate([piece, jnp.zeros((levels * per * slots, wide - half), F32)], axis=1)
            line = line + (pltpu.roll(piece, k * width, 1) if k else piece)
        full.append(line)

    lower = lax.broadcasted_iota(jnp.int32, (8, feat), 0) >= 4
    for ref, side in ((same_ref, parity), (other_ref, 1 - parity)):
        for i in range(pairs):
            start = pl.multiple_of((2 * i + side) * part, part)
            block = jnp.concatenate([gw_s[k, pl.ds(start, part), :] for k in range(4)], axis=0)
            ref[i, 0:packed, :] = block.astype(BF16)
    for j in range(2 * pairs):
        z, w, a = j // (levels * per), j // per % levels, j % per
        at = (z * per + a) * slots
        line = full[w][at:at + slots]
        tail = line[:, feat:]
        moved = jnp.concatenate([pltpu.roll(tail[:8], 4, 0), tail[:8], pltpu.roll(tail[8:], 4, 0)], axis=1)
        lines = jnp.concatenate([line[:8, :feat], jnp.where(lower, moved, line[8:, :feat])], axis=0).astype(BF16)

        @pl.when(parity == j % 2)
        def _():
            same_ref[j // 2, packed:, :] = lines

        @pl.when(parity != j % 2)
        def _():
            other_ref[j // 2, packed:, :] = lines


def run_block(me, x, c, gain, w_same, w_other, strips, order, heads, windows, lon_width, levels, lat_rows, rels):
    rows, feat = x.shape
    tokens = rows // windows
    lanes = strips.shape[0] * 128
    pairs, packed, _ = w_same.shape
    slots = strips.shape[1] // (levels * lat_rows)
    vmem = pl.BlockSpec(memory_space=pltpu.VMEM)
    sent = jax.ShapeDtypeStruct((pairs, packed + slots, feat), BF16)
    return pl.pallas_call(
        functools.partial(
            block_kernel, heads=heads, windows=windows, tokens=tokens, lon_width=lon_width,
            levels=levels, lat_rows=lat_rows, rels=rels,
        ),
        out_shape=(
            jax.ShapeDtypeStruct((rows, feat), BF16),
            sent,
            sent,
            jax.ShapeDtypeStruct((1, feat), F32),
        ),
        in_specs=[pl.BlockSpec(memory_space=pltpu.SMEM)] + [vmem] * 7,
        out_specs=[vmem] * 4,
        scratch_shapes=[
            pltpu.VMEM((4, feat, feat), F32),
            pltpu.VMEM((4, feat, feat), F32),
            pltpu.VMEM((rows, feat), F32),
            pltpu.VMEM((rows, 1), F32),
            pltpu.VMEM((rows, feat), BF16),
            pltpu.VMEM((windows, 3 * feat, tokens), BF16),
            pltpu.VMEM((windows, feat, tokens), BF16),
            pltpu.VMEM((feat // 128, windows, tokens, 128), BF16),
            pltpu.VMEM((feat // 128, windows, tokens, 128), BF16),
            pltpu.VMEM((windows, 3 * feat, tokens), BF16),
            pltpu.VMEM((windows, feat, tokens), BF16),
            pltpu.VMEM((tokens, tokens), F32),
            pltpu.VMEM((tokens, lanes), F32),
            pltpu.VMEM(strips.shape, F32),
        ],
        compiler_params=pltpu.CompilerParams(vmem_limit_bytes=48 * 1024 * 1024),
        name="window_block",
    )(me, x, c, gain, w_same, w_other, strips, order)


def sum_kernel(x_ref, gain_ref, out_ref, table_ref, *, packed):
    pieces, rows, feat = x_ref.shape
    total = x_ref[0].astype(F32)
    for i in range(1, pieces):
        total = total + x_ref[i].astype(F32)
    turned = total[:packed].T
    blocks = out_ref.shape[0]
    part = feat // blocks
    gain = gain_ref[...]
    high = gain.astype(BF16).astype(F32)
    gains = jnp.concatenate(
        [src[:, k * packed:(k + 1) * packed] for src in (high, gain - high) for k in range(feat // packed)], axis=0
    )
    for i in range(blocks):
        out_ref[i] = jnp.concatenate([turned[i * part:(i + 1) * part], gains], axis=0).astype(BF16)
    table_ref[...] = total[packed:]


def sum_and_turn(x, gain, blocks, packed):
    pieces, rows, feat = x.shape
    vmem = pl.BlockSpec(memory_space=pltpu.VMEM)
    return pl.pallas_call(
        functools.partial(sum_kernel, packed=packed),
        out_shape=(
            jax.ShapeDtypeStruct((blocks, feat // blocks + 2 * (feat // packed), packed), BF16),
            jax.ShapeDtypeStruct((rows - packed, feat), F32),
        ),
        in_specs=[vmem, vmem],
        out_specs=[vmem, vmem],
        name="sum_and_turn",
    )(x, gain)


def last_kernel(x_ref, query_ref, key_ref, value_ref, out_ref, gain_ref):
    total = x_ref[0].astype(F32)
    for i in range(1, x_ref.shape[0]):
        total = total + x_ref[i].astype(F32)
    part = query_ref.shape[0]
    for i, ref in enumerate((query_ref, key_ref, value_ref, out_ref)):
        ref[...] = total[:part, i * part:(i + 1) * part]
    count = (total.shape[0] - part) // 2
    gain_ref[...] = total[part:part + count] + total[part + count:]


def last_sum(x, part, feat):
    vmem = pl.BlockSpec(memory_space=pltpu.VMEM)
    block = jax.ShapeDtypeStruct((part, part), F32)
    lanes = x.shape[2]
    return pl.pallas_call(
        last_kernel,
        out_shape=(block, block, block, block, jax.ShapeDtypeStruct((feat // lanes, lanes), F32)),
        in_specs=[vmem],
        out_specs=[vmem] * 5,
        name="last_sum",
    )(x)


def swap(x, axis, bit):
    n = lax.axis_size(axis)
    return lax.ppermute(x, axis, [(i, i ^ bit) for i in range(n)])


def shift(x, lat_by, lon_by):
    lats, lons = lax.axis_size("lat"), lax.axis_size("lon")
    if lon_by == 0:
        return lax.ppermute(x, "lat", [(i, (i + lat_by) % lats) for i in range(lats)])
    if lat_by == 0:
        return lax.ppermute(x, "lon", [(i, (i + lon_by) % lons) for i in range(lons)])
    pairs = [
        (a * lons + b, (a + lat_by) % lats * lons + (b + lon_by) % lons)
        for a in range(lats)
        for b in range(lons)
    ]
    return lax.ppermute(x, ("lat", "lon"), pairs)


def spread_over_lat(x):
    return lax.all_to_all(x, "lat", 0, 0)


def spread_over_lon(x):
    n = lax.axis_size("lon")
    groups = [list(range(c, n, 2)) for c in range(2)]
    return lax.all_to_all(x, "lon", 0, 0, axis_index_groups=groups)


def local(fields, cotangent, norm_gain, w_query, w_key, w_value, w_out, rel_table):
    levels, lat_rows, lon_cols, feat = fields.shape
    heads = rel_table.shape[1]
    rels = rel_table.shape[2] // (levels * levels * lat_rows * lat_rows)
    lon_width = (rels + 1) // 2
    half_rows = lat_rows // 2
    half_cols = lon_width // 2
    windows = lon_cols // lon_width
    lats = lax.axis_size("lat")
    lons = lax.axis_size("lon")
    me_lat = lax.axis_index("lat")
    me_lon = lax.axis_index("lon")
    part = w_query.shape[0]

    both = jnp.stack([fields, cotangent]).transpose(3, 0, 1, 2, 4)
    own = both[half_cols:, :, :, half_rows:]
    south = shift(both[half_cols:, :, :, :half_rows], -1, 0)
    east = shift(both[:half_cols, :, :, half_rows:], 0, -1)
    corner = shift(both[:half_cols, :, :, :half_rows], -1, -1)
    moved = jnp.concatenate(
        [jnp.concatenate([own, south], axis=3), jnp.concatenate([east, corner], axis=3)], axis=0
    )
    shifted = moved[:, 0].reshape(-1, feat)
    cot_shift = moved[:, 1].reshape(-1, feat)

    mine = jnp.concatenate([w_query, w_key, w_value, w_out], axis=1)
    rows_all = spread_over_lat(jnp.broadcast_to(mine[None], (lats,) + mine.shape))
    w_same = spread_over_lon(turn(rows_all, lons // 2))
    w_other = swap(w_same, "lon", 1)

    order = jnp.asarray(offset_order(rels, levels, lat_rows, 256), BF16)
    last = (me_lat == lats - 1).astype(jnp.int32).reshape(1)
    slots = heads + -heads % 16
    strips = make_strips(last, rel_table[0], order, levels, lat_rows, rels, slots)

    d_input, g_same, g_other, g_gain = run_block(
        me_lon.reshape(1), shifted, cot_shift, norm_gain[None], w_same, w_other, strips, order,
        heads, windows, lon_width, levels, lat_rows, rels,
    )

    paired = (g_same.astype(F32) + swap(g_other, "lon", 1).astype(F32)).astype(BF16)
    arrived = spread_over_lon(paired)
    gain_sum = g_gain
    bit = 1
    while bit < lons:
        gain_sum = gain_sum + swap(gain_sum, "lon", bit)
        bit *= 2
    packed = 4 * part
    message, lines = sum_and_turn(arrived, gain_sum, lats, packed)
    grad_query, grad_key, grad_value, grad_out, grad_gain = last_sum(spread_over_lat(message), part, feat)

    over = rel_table.shape[2] // lons - feat
    groups = feat // 128
    tail = lines[heads:].reshape(slots - heads, groups, 128)[:, :, :over].transpose(1, 0, 2)
    grad_table = jnp.concatenate([lines[:heads], tail.reshape(heads, over)], axis=1)[None]

    d_in = d_input.reshape(lon_cols, levels, lat_rows, feat)
    stay = lon_cols - half_cols
    west = shift(d_in[stay:, :, :half_rows], 0, 1)
    north = shift(d_in[:stay, :, half_rows:], 1, 0)
    corner = shift(d_in[stay:, :, half_rows:], 1, 1)
    back = jnp.concatenate(
        [jnp.concatenate([corner, west], axis=2), jnp.concatenate([north, d_in[:stay, :, :half_rows]], axis=2)],
        axis=0,
    ).transpose(1, 2, 0, 3)
    grad_fields = (cotangent.astype(F32) + back.astype(F32)).astype(BF16)
    return (grad_fields, grad_query, grad_key, grad_value, grad_out, grad_table, grad_gain.reshape(feat))


def solution(mesh):
    return jax.shard_map(
        local,
        mesh=mesh,
        in_specs=(
            P(None, "lat", "lon", None),
            P(None, "lat", "lon", None),
            P(),
            P("lat", "lon"),
            P("lat", "lon"),
            P("lat", "lon"),
            P("lat", "lon"),
            P("lat", None, None),
        ),
        out_specs=(
            P(None, "lat", "lon", None),
            P("lat", "lon"),
            P("lat", "lon"),
            P("lat", "lon"),
            P("lat", "lon"),
            P("lat", None, "lon"),
            P(),
        ),
        check_vma=False,
    )
```

```python
import functools
import math

import jax
import jax.numpy as jnp
import numpy as np
from jax import lax
from jax.experimental import pallas as pl
from jax.experimental.pallas import tpu as pltpu
from jax.sharding import PartitionSpec as P

EPSILON = 1e-05
MASKED = -1000000000.0
LOG2E = math.log2(math.e)
UNROLL = 2
F32 = jnp.float32
BF16 = jnp.bfloat16
NN = (((1,), (0,)), ((), ()))
NT = (((1,), (1,)), ((), ()))
TN = (((0,), (0,)), ((), ()))


def mm(a, b, dims):
    return lax.dot_general(a, b, dims, preferred_element_type=F32)


def offset_order(rels, levels, lat_rows, group):
    lanes = rels * levels * lat_rows
    order = np.zeros((levels * group, lanes + -lanes % 128), np.float32)
    for level in range(levels):
        for lat in range(lat_rows):
            for rel in range(rels):
                order[level * group + lat * rels + rel, ((rels - 1 - rel) * levels + level) * lat_rows + lat] = 1.0
    return order


def bias_kernel(last_ref, table_ref, order_ref, out_ref, table_s, strips_s, bias_s, *, levels, lat_rows, rels, windows):
    heads = table_ref.shape[0]
    slots = table_s.shape[1]
    cell = levels * lat_rows
    width = lat_rows * rels
    group = table_s.shape[2] // levels
    tiles = strips_s.shape[0]
    lanes = tiles * 128
    lon_width = (rels + 1) // 2
    tokens = lon_width * cell
    table_s[...] = jnp.zeros_like(table_s)
    table = table_ref[...]
    for z in range(levels):
        for w in range(levels):
            for a in range(lat_rows):
                at = ((z * levels + w) * lat_rows + a) * width
                table_s[z * lat_rows + a, 0:heads, w * group:w * group + width] = table[:, at:at + width]
    full = table_s[...].reshape(cell * slots, levels * group)
    order = order_ref[...]
    high = full.astype(BF16)
    rest = full - high.astype(F32)
    mid = rest.astype(BF16)
    low = (rest - mid.astype(F32)).astype(BF16)
    strips = mm(high, order, NN) + mm(mid, order, NN) + mm(low, order, NN)
    row = lax.broadcasted_iota(jnp.int32, (cell * slots, 1), 0) // slots
    lane = lax.broadcasted_iota(jnp.int32, (1, lanes), 1)
    row_north = (row % lat_rows < lat_rows // 2).astype(F32)
    lane_north = (lane % lat_rows < lat_rows // 2).astype(F32)
    crossing = (row_north != lane_north) & (last_ref[0] != 0)
    strips = jnp.where(crossing, MASKED, strips) * LOG2E
    for g in range(tiles):
        strips_s[g] = strips[:, g * 128:(g + 1) * 128]

    def head(h, carry):
        strip = jnp.concatenate([strips_s[g, pl.ds(h, cell, stride=slots), :] for g in range(tiles)], axis=1)
        for p in range(lon_width):
            off = (lon_width - 1 - p) * cell
            rolled = pltpu.roll(strip, lanes - off, 1) if off else strip
            bias_s[p * cell:(p + 1) * cell, :] = rolled[:, :tokens]
        bias = bias_s[...].T
        out_ref[h] = jnp.concatenate([bias] * windows, axis=1)
        return carry

    lax.fori_loop(0, heads, head, 0)


def make_bias(last, table, order, levels, lat_rows, rels, slots, windows):
    heads = table.shape[0]
    cell = levels * lat_rows
    tokens = (rels + 1) // 2 * cell
    tiles = order.shape[1] // 128
    vmem = pl.BlockSpec(memory_space=pltpu.VMEM)
    return pl.pallas_call(
        functools.partial(bias_kernel, levels=levels, lat_rows=lat_rows, rels=rels, windows=windows),
        out_shape=jax.ShapeDtypeStruct((heads, tokens, windows * tokens), F32),
        in_specs=[pl.BlockSpec(memory_space=pltpu.SMEM), vmem, vmem],
        out_specs=vmem,
        scratch_shapes=[
            pltpu.VMEM((cell, slots, order.shape[0]), F32),
            pltpu.VMEM((tiles, cell * slots, 128), F32),
            pltpu.VMEM((tokens, tokens), F32),
        ],
        compiler_params=pltpu.CompilerParams(vmem_limit_bytes=32 * 1024 * 1024),
        name="make_bias",
    )(last, table, order)


def turn_kernel(x_ref, out_ref):
    blocks, rows, lanes = x_ref.shape
    turned = x_ref[...].astype(F32).reshape(blocks * rows, lanes).T.astype(BF16)
    for i in range(out_ref.shape[0]):
        out_ref[i] = turned


def turn(x, copies):
    blocks, rows, lanes = x.shape
    vmem = pl.BlockSpec(memory_space=pltpu.VMEM)
    return pl.pallas_call(
        turn_kernel,
        out_shape=jax.ShapeDtypeStruct((copies, lanes, blocks * rows), BF16),
        in_specs=[vmem],
        out_specs=vmem,
        name="turn_weights",
    )(x)


def load_weights(w_s, w_same_ref, w_other_ref, parity):
    pairs, packed, _ = w_same_ref.shape
    part = packed // 4
    for ref, side in ((w_same_ref, parity), (w_other_ref, 1 - parity)):
        for i in range(pairs):
            block = ref[i].astype(F32)
            start = pl.multiple_of((2 * i + side) * part, part)
            for k in range(w_s.shape[0]):
                w_s[k, pl.ds(start, part), :] = block[k * part:(k + 1) * part]


def normalise(x_ref):
    xf = x_ref[...].astype(F32)
    mean = jnp.mean(xf, axis=1, keepdims=True)
    centred = xf - mean
    var = jnp.mean(centred * centred, axis=1, keepdims=True)
    inv = 1.0 / jnp.sqrt(var + EPSILON)
    return centred * inv, inv


def block_kernel(
    me_ref, x_ref, c_ref, gain_ref, w_same_ref, w_other_ref, bias_ref, order_ref, pick_ref,
    same_ref, other_ref, dq_s, dk_s, dv_s,
    w_s, gw_s, normed_s, q_s, d_s, k_s, v_s, ctx_s, dsum_s, fold_s,
    *, heads, windows, levels, lat_rows, rels,
):
    feat = x_ref.shape[1]
    dim = feat // heads
    lon_width = (rels + 1) // 2
    cell = levels * lat_rows
    tokens = lon_width * cell
    scale = 1.0 / math.sqrt(dim)
    tiles = fold_s.shape[0]
    lanes = tiles * 128
    slots = fold_s.shape[1] // cell
    pairs, packed, _ = w_same_ref.shape
    part = packed // 4
    parity = me_ref[0] % 2

    load_weights(w_s, w_same_ref, w_other_ref, parity)
    std, _ = normalise(x_ref)
    normed_s[...] = (std * gain_ref[...]).astype(BF16)
    window = lax.broadcasted_iota(jnp.int32, (dim, windows * tokens), 1) // tokens

    def apart(x):
        x = x.astype(BF16).reshape(heads, dim, windows * tokens)
        return [jnp.where((window == w)[None], x, jnp.zeros_like(x)) for w in range(windows)]

    w_qry = w_s[0].astype(BF16)
    w_key = w_s[1].astype(BF16)
    w_val = w_s[2].astype(BF16)
    w_out = w_s[3].T.astype(BF16)
    for dst, x in ((q_s, mm(w_qry, normed_s[...], NT)), (d_s, mm(w_out, c_ref[...], NT))):
        for w, block in enumerate(apart(x)):
            dst[:, w * dim:(w + 1) * dim, :] = block
    for w in range(windows):
        nw = normed_s[w * tokens:(w + 1) * tokens]
        k_s[:, w * dim:(w + 1) * dim, :] = mm(w_key, nw, NT).astype(BF16).reshape(heads, dim, tokens)
        v_s[:, w * dim:(w + 1) * dim, :] = mm(w_val, nw, NT).astype(BF16).reshape(heads, dim, tokens)
    dsum_s[...] = jnp.zeros_like(dsum_s)
    fold_s[...] = jnp.zeros_like(fold_s)

    def own(x):
        out = x[:dim]
        for w in range(1, windows):
            out = jnp.where(window == w, x[w * dim:(w + 1) * dim], out)
        return out

    def head(h, carry):
        qh, dh, kh, vh = q_s[h], d_s[h], k_s[h], v_s[h]
        score = mm(kh, qh, TN) * (scale * LOG2E) + bias_ref[h]
        d_prob = mm(vh, dh, TN)
        expo = jnp.exp2(score - jnp.max(score, axis=0, keepdims=True))
        prob = expo * (1.0 / jnp.sum(expo, axis=0, keepdims=True))
        low = prob.astype(BF16)
        ctx = own(mm(vh, low, NN))
        ctx_s[h] = ctx.astype(BF16)
        dv_s[h] = mm(dh, low, NT).astype(BF16)
        d_ctx = dh[:dim].astype(F32)
        for w in range(1, windows):
            d_ctx = d_ctx + dh[w * dim:(w + 1) * dim].astype(F32)
        inner = jnp.sum(ctx * d_ctx, axis=0, keepdims=True)
        d_low = (prob * (d_prob - inner)).astype(BF16)
        dq_s[h] = (own(mm(kh, d_low, NN)) * scale).astype(BF16)
        both = mm(jnp.concatenate([qh, pick_ref[...]], axis=0), d_low, NT)
        dk_s[h] = (both[:windows * dim] * scale).astype(BF16)
        dsum_s[:, :tokens] = both[windows * dim:]
        folded = jnp.zeros((cell, lanes), F32)
        for p in range(lon_width):
            off = (lon_width - 1 - p) * cell
            piece = dsum_s[p * cell:(p + 1) * cell, :]
            folded = folded + (pltpu.roll(piece, off, 1) if off else piece)
        for g in range(tiles):
            fold_s[g, pl.ds(h, cell, stride=slots), :] = folded[:, g * 128:(g + 1) * 128]
        return carry

    if UNROLL:
        lax.fori_loop(0, heads, head, 0, unroll=UNROLL)

    def by_window(ref, w):
        return ref[:, w * dim:(w + 1) * dim, :].reshape(feat, tokens)

    gw_s[0] = mm(dq_s[...].reshape(feat, windows * tokens), normed_s[...], NN)
    gw_s[3] = mm(ctx_s[...].reshape(feat, windows * tokens), c_ref[...], NN).T
    for i, ref in ((1, dk_s), (2, dv_s)):
        total = jnp.zeros((feat, feat), F32)
        for w in range(windows):
            total = total + mm(by_window(ref, w), normed_s[w * tokens:(w + 1) * tokens], NN)
        gw_s[i] = total
    g_gain = jnp.zeros((1, feat), F32)
    for i in range(3):
        g_gain = g_gain + jnp.sum(gw_s[i] * w_s[i], axis=0, keepdims=True)
    g_gain = g_gain / gain_ref[...]

    fold = jnp.concatenate([fold_s[g] for g in range(tiles)], axis=1).astype(BF16)
    back = mm(fold, order_ref[...], NT)
    width = lat_rows * rels
    half = back.shape[1] // levels
    per = 2 * pairs // (levels * levels)
    run = lat_rows // per
    wide = -(-run * width // 128) * 128
    back = back.reshape(levels * per, run, slots, levels * half)
    full = []
    for w in range(levels):
        line = jnp.zeros((levels * per * slots, wide), F32)
        for k in range(run):
            piece = back[:, k, :, w * half:(w + 1) * half].reshape(levels * per * slots, half)
            piece = jnp.concatenate([piece, jnp.zeros((levels * per * slots, wide - half), F32)], axis=1)
            line = line + (pltpu.roll(piece, k * width, 1) if k else piece)
        full.append(line)

    lane = lax.broadcasted_iota(jnp.int32, (8, feat), 1) % 128
    row = lax.broadcasted_iota(jnp.int32, (8, feat), 0)
    gains = jnp.zeros((8, feat), F32)
    for i in range(4):
        turned = jnp.concatenate(
            [pltpu.roll(g_gain[:, g * 128:(g + 1) * 128], (160 - 32 * i) % 128, 1) for g in range(feat // 128)], axis=1
        )
        gains = jnp.where((row == 4 + i) & (lane >= 32) & (lane < 64), turned, gains)

    for ref, side in ((same_ref, parity), (other_ref, 1 - parity)):
        for i in range(pairs):
            start = pl.multiple_of((2 * i + side) * part, part)
            block = jnp.concatenate([gw_s[k, pl.ds(start, part), :] for k in range(4)], axis=0)
            ref[i, 0:packed, :] = block.astype(BF16)
    for j in range(2 * pairs):
        z, w, a = j // (levels * per), j // per % levels, j % per
        at = (z * per + a) * slots
        line = full[w][at:at + slots]
        tail = line[:, feat:]
        moved = jnp.concatenate([pltpu.roll(tail[:8], 4, 0), tail[:8], pltpu.roll(tail[8:], 4, 0)], axis=1)
        moved = jnp.where(lane < 32, moved, gains)
        lines = jnp.concatenate([line[:8, :feat], jnp.where(row >= 4, moved, line[8:, :feat])], axis=0).astype(BF16)

        @pl.when(parity == j % 2)
        def _():
            same_ref[j // 2, packed:, :] = lines

        @pl.when(parity != j % 2)
        def _():
            other_ref[j // 2, packed:, :] = lines


def run_block(me, x, c, gain, w_same, w_other, bias, order, pick, heads, windows, levels, lat_rows, rels):
    rows, feat = x.shape
    tokens = rows // windows
    dim = feat // heads
    cell = levels * lat_rows
    tiles = order.shape[1] // 128
    slots = heads + -heads % 16
    pairs, packed, _ = w_same.shape
    vmem = pl.BlockSpec(memory_space=pltpu.VMEM)
    sent = jax.ShapeDtypeStruct((pairs, packed + slots, feat), BF16)
    aligned = jax.ShapeDtypeStruct((heads, windows * dim, tokens), BF16)
    return pl.pallas_call(
        functools.partial(block_kernel, heads=heads, windows=windows, levels=levels, lat_rows=lat_rows, rels=rels),
        out_shape=(sent, sent, jax.ShapeDtypeStruct((heads, dim, rows), BF16), aligned, aligned),
        in_specs=[pl.BlockSpec(memory_space=pltpu.SMEM)] + [vmem] * 8,
        out_specs=[vmem] * 5,
        scratch_shapes=[
            pltpu.VMEM((4, feat, feat), F32),
            pltpu.VMEM((4, feat, feat), F32),
            pltpu.VMEM((rows, feat), BF16),
            pltpu.VMEM((heads, windows * dim, rows), BF16),
            pltpu.VMEM((heads, windows * dim, rows), BF16),
            pltpu.VMEM((heads, windows * dim, tokens), BF16),
            pltpu.VMEM((heads, windows * dim, tokens), BF16),
            pltpu.VMEM((heads, dim, rows), BF16),
            pltpu.VMEM((tokens, tiles * 128), F32),
            pltpu.VMEM((tiles, cell * slots, 128), F32),
        ],
        compiler_params=pltpu.CompilerParams(vmem_limit_bytes=48 * 1024 * 1024),
        name="window_block",
    )(me, x, c, gain, w_same, w_other, bias, order, pick)


def input_kernel(me_ref, x_ref, gain_ref, w_same_ref, w_other_ref, dq_ref, dk_ref, dv_ref, din_ref, w_s):
    heads, stacked, tokens = dk_ref.shape
    rows, feat = x_ref.shape
    windows = rows // tokens
    dim = stacked // windows
    load_weights(w_s, w_same_ref, w_other_ref, me_ref[0] % 2)
    std, inv = normalise(x_ref)
    gain = gain_ref[...]
    w_qry, w_key, w_val = (w_s[i].astype(BF16) for i in range(3))
    from_q = mm(dq_ref[...].reshape(feat, rows), w_qry, TN)
    for w in range(windows):
        at = slice(w * tokens, (w + 1) * tokens)
        d_normed = from_q[at]
        for ref, weight in ((dk_ref, w_key), (dv_ref, w_val)):
            d_normed = d_normed + mm(ref[:, w * dim:(w + 1) * dim, :].reshape(feat, tokens), weight, TN)
        g = d_normed * gain
        d_in = inv[at] * (
            g - jnp.mean(g, axis=1, keepdims=True) - std[at] * jnp.mean(g * std[at], axis=1, keepdims=True)
        )
        din_ref[at] = d_in.astype(BF16)


def input_gradient(me, x, gain, w_same, w_other, dq, dk, dv):
    feat = x.shape[1]
    vmem = pl.BlockSpec(memory_space=pltpu.VMEM)
    return pl.pallas_call(
        input_kernel,
        out_shape=jax.ShapeDtypeStruct(x.shape, BF16),
        in_specs=[pl.BlockSpec(memory_space=pltpu.SMEM)] + [vmem] * 7,
        out_specs=vmem,
        scratch_shapes=[pltpu.VMEM((3, feat, feat), F32)],
        compiler_params=pltpu.CompilerParams(vmem_limit_bytes=32 * 1024 * 1024),
        name="input_gradient",
    )(me, x, gain, w_same, w_other, dq, dk, dv)


def sum_kernel(x_ref, out_ref, table_ref, *, packed):
    pieces, rows, feat = x_ref.shape
    total = x_ref[0].astype(F32)
    for i in range(1, pieces):
        total = total + x_ref[i].astype(F32)
    turned = total[:packed].T
    blocks = out_ref.shape[0]
    part = feat // blocks
    lane = lax.broadcasted_iota(jnp.int32, (1, feat), 1) % 128
    gain = jnp.zeros((1, feat), F32)
    for i in range(4):
        line = total[rows - 4 + i:rows - 3 + i]
        moved = jnp.concatenate(
            [pltpu.roll(line[:, g * 128:(g + 1) * 128], (32 * i - 32) % 128, 1) for g in range(feat // 128)], axis=1
        )
        gain = jnp.where((lane >= 32 * i) & (lane < 32 * i + 32), moved, gain)
    high = gain.astype(BF16).astype(F32)
    gains = jnp.concatenate(
        [src[:, k * packed:(k + 1) * packed] for src in (high, gain - high) for k in range(feat // packed)], axis=0
    )
    for i in range(blocks):
        out_ref[i] = jnp.concatenate([turned[i * part:(i + 1) * part], gains], axis=0).astype(BF16)
    table_ref[...] = total[packed:]


def sum_and_turn(x, blocks, packed):
    pieces, rows, feat = x.shape
    vmem = pl.BlockSpec(memory_space=pltpu.VMEM)
    return pl.pallas_call(
        functools.partial(sum_kernel, packed=packed),
        out_shape=(
            jax.ShapeDtypeStruct((blocks, feat // blocks + 2 * (feat // packed), packed), BF16),
            jax.ShapeDtypeStruct((rows - packed, feat), F32),
        ),
        in_specs=[vmem],
        out_specs=[vmem, vmem],
        name="sum_and_turn",
    )(x)


def last_kernel(x_ref, query_ref, key_ref, value_ref, out_ref, gain_ref):
    total = x_ref[0].astype(F32)
    for i in range(1, x_ref.shape[0]):
        total = total + x_ref[i].astype(F32)
    part = query_ref.shape[0]
    for i, ref in enumerate((query_ref, key_ref, value_ref, out_ref)):
        ref[...] = total[:part, i * part:(i + 1) * part]
    count = (total.shape[0] - part) // 2
    gain_ref[...] = total[part:part + count] + total[part + count:]


def last_sum(x, part, feat):
    vmem = pl.BlockSpec(memory_space=pltpu.VMEM)
    block = jax.ShapeDtypeStruct((part, part), F32)
    lanes = x.shape[2]
    return pl.pallas_call(
        last_kernel,
        out_shape=(block, block, block, block, jax.ShapeDtypeStruct((feat // lanes, lanes), F32)),
        in_specs=[vmem],
        out_specs=[vmem] * 5,
        name="last_sum",
    )(x)


def swap(x, axis, bit):
    n = lax.axis_size(axis)
    return lax.ppermute(x, axis, [(i, i ^ bit) for i in range(n)])


def shift(x, lat_by, lon_by):
    lats, lons = lax.axis_size("lat"), lax.axis_size("lon")
    if lon_by == 0:
        return lax.ppermute(x, "lat", [(i, (i + lat_by) % lats) for i in range(lats)])
    if lat_by == 0:
        return lax.ppermute(x, "lon", [(i, (i + lon_by) % lons) for i in range(lons)])
    pairs = [
        (a * lons + b, (a + lat_by) % lats * lons + (b + lon_by) % lons)
        for a in range(lats)
        for b in range(lons)
    ]
    return lax.ppermute(x, ("lat", "lon"), pairs)


def spread_over_lat(x):
    return lax.all_to_all(x, "lat", 0, 0)


def spread_over_lon(x):
    n = lax.axis_size("lon")
    groups = [list(range(c, n, 2)) for c in range(2)]
    return lax.all_to_all(x, "lon", 0, 0, axis_index_groups=groups)


def local(fields, cotangent, norm_gain, w_query, w_key, w_value, w_out, rel_table):
    levels, lat_rows, lon_cols, feat = fields.shape
    heads = rel_table.shape[1]
    rels = rel_table.shape[2] // (levels * levels * lat_rows * lat_rows)
    lon_width = (rels + 1) // 2
    half_rows = lat_rows // 2
    half_cols = lon_width // 2
    windows = lon_cols // lon_width
    lats = lax.axis_size("lat")
    lons = lax.axis_size("lon")
    me_lat = lax.axis_index("lat")
    me_lon = lax.axis_index("lon")
    part = w_query.shape[0]

    both = jnp.stack([fields, cotangent]).transpose(3, 0, 1, 2, 4)

    mine = jnp.concatenate([w_query, w_key, w_value, w_out], axis=1)
    mine, both = lax.optimization_barrier((mine, both))
    rows_all = spread_over_lat(jnp.broadcast_to(mine[None], (lats,) + mine.shape))
    own = both[half_cols:, :, :, half_rows:]
    south = shift(both[half_cols:, :, :, :half_rows], -1, 0)
    east = shift(both[:half_cols, :, :, half_rows:], 0, -1)
    corner = shift(both[:half_cols, :, :, :half_rows], -1, -1)
    rows_all, south, east, corner = lax.optimization_barrier((rows_all, south, east, corner))
    w_same = spread_over_lon(turn(rows_all, lons // 2))
    w_other = swap(w_same, "lon", 1)
    moved = jnp.concatenate(
        [jnp.concatenate([own, south], axis=3), jnp.concatenate([east, corner], axis=3)], axis=0
    )
    shifted = moved[:, 0].reshape(-1, feat)
    cot_shift = moved[:, 1].reshape(-1, feat)

    order = jnp.asarray(offset_order(rels, levels, lat_rows, 256), BF16)
    last = (me_lat == lats - 1).astype(jnp.int32).reshape(1)
    slots = heads + -heads % 16
    bias = make_bias(last, rel_table[0], order, levels, lat_rows, rels, slots, windows)
    tokens = lon_width * levels * lat_rows
    pick = jnp.asarray(np.tile(np.eye(tokens, dtype=np.float32), (1, windows)), BF16)

    me = me_lon.reshape(1)
    gain = norm_gain[None]
    g_same, g_other, dq, dk, dv = run_block(
        me, shifted, cot_shift, gain, w_same, w_other, bias, order, pick, heads, windows, levels, lat_rows, rels
    )

    paired = (g_same.astype(F32) + swap(g_other, "lon", 1).astype(F32)).astype(BF16)
    paired, dq, dk, dv = lax.optimization_barrier((paired, dq, dk, dv))
    arrived = spread_over_lon(paired)
    message, lines = sum_and_turn(arrived, lats, 4 * part)
    grad_query, grad_key, grad_value, grad_out, grad_gain = last_sum(spread_over_lat(message), part, feat)
    d_input = input_gradient(me, shifted, gain, w_same, w_other, dq, dk, dv)

    over = rel_table.shape[2] // lons - feat
    groups = feat // 128
    tail = lines[heads:].reshape(slots - heads, groups, 128)[:, :, :over].transpose(1, 0, 2)
    grad_table = jnp.concatenate([lines[:heads], tail.reshape(heads, over)], axis=1)[None]

    d_in = d_input.reshape(lon_cols, levels, lat_rows, feat)
    stay = lon_cols - half_cols
    west = shift(d_in[stay:, :, :half_rows], 0, 1)
    north = shift(d_in[:stay, :, half_rows:], 1, 0)
    corner = shift(d_in[stay:, :, half_rows:], 1, 1)
    back = jnp.concatenate(
        [jnp.concatenate([corner, west], axis=2), jnp.concatenate([north, d_in[:stay, :, :half_rows]], axis=2)],
        axis=0,
    ).transpose(1, 2, 0, 3)
    grad_fields = (cotangent.astype(F32) + back.astype(F32)).astype(BF16)
    return (grad_fields, grad_query, grad_key, grad_value, grad_out, grad_table, grad_gain.reshape(feat))


def solution(mesh):
    return jax.shard_map(
        local,
        mesh=mesh,
        in_specs=(
            P(None, "lat", "lon", None),
            P(None, "lat", "lon", None),
            P(),
            P("lat", "lon"),
            P("lat", "lon"),
            P("lat", "lon"),
            P("lat", "lon"),
            P("lat", None, None),
        ),
        out_specs=(
            P(None, "lat", "lon", None),
            P("lat", "lon"),
            P("lat", "lon"),
            P("lat", "lon"),
            P("lat", "lon"),
            P("lat", None, "lon"),
            P(),
        ),
        check_vma=False,
    )
```

```python
import functools
import math

import jax
import jax.numpy as jnp
import numpy as np
from jax import lax
from jax.experimental import pallas as pl
from jax.experimental.pallas import tpu as pltpu
from jax.sharding import PartitionSpec as P

EPSILON = 1e-05
MASKED = -1000000000.0
LOG2E = math.log2(math.e)
UNROLL = 6
F32 = jnp.float32
BF16 = jnp.bfloat16
NN = (((1,), (0,)), ((), ()))
NT = (((1,), (1,)), ((), ()))
TN = (((0,), (0,)), ((), ()))


def mm(a, b, dims):
    return lax.dot_general(a, b, dims, preferred_element_type=F32)


def offset_order(rels, levels, lat_rows, group):
    lanes = rels * levels * lat_rows
    order = np.zeros((levels * group, lanes + -lanes % 128), np.float32)
    for level in range(levels):
        for lat in range(lat_rows):
            for rel in range(rels):
                order[level * group + lat * rels + rel, ((rels - 1 - rel) * levels + level) * lat_rows + lat] = 1.0
    return order


def bias_kernel(last_ref, table_ref, order_ref, out_ref, table_s, strips_s, bias_s, *, levels, lat_rows, rels, windows):
    heads = table_ref.shape[0]
    slots = table_s.shape[1]
    cell = levels * lat_rows
    width = lat_rows * rels
    group = table_s.shape[2] // levels
    tiles = strips_s.shape[0]
    lanes = tiles * 128
    lon_width = (rels + 1) // 2
    tokens = lon_width * cell
    table_s[...] = jnp.zeros_like(table_s)
    table = table_ref[...]
    for z in range(levels):
        for w in range(levels):
            for a in range(lat_rows):
                at = ((z * levels + w) * lat_rows + a) * width
                table_s[z * lat_rows + a, 0:heads, w * group:w * group + width] = table[:, at:at + width]
    full = table_s[...].reshape(cell * slots, levels * group)
    order = order_ref[...]
    high = full.astype(BF16)
    rest = full - high.astype(F32)
    mid = rest.astype(BF16)
    low = (rest - mid.astype(F32)).astype(BF16)
    strips = mm(high, order, NN) + mm(mid, order, NN) + mm(low, order, NN)
    row = lax.broadcasted_iota(jnp.int32, (cell * slots, 1), 0) // slots
    lane = lax.broadcasted_iota(jnp.int32, (1, lanes), 1)
    row_north = (row % lat_rows < lat_rows // 2).astype(F32)
    lane_north = (lane % lat_rows < lat_rows // 2).astype(F32)
    crossing = (row_north != lane_north) & (last_ref[0] != 0)
    strips = jnp.where(crossing, MASKED, strips) * LOG2E
    for g in range(tiles):
        strips_s[g] = strips[:, g * 128:(g + 1) * 128]

    def head(h, carry):
        strip = jnp.concatenate([strips_s[g, pl.ds(h, cell, stride=slots), :] for g in range(tiles)], axis=1)
        for p in range(lon_width):
            off = (lon_width - 1 - p) * cell
            rolled = pltpu.roll(strip, lanes - off, 1) if off else strip
            bias_s[p * cell:(p + 1) * cell, :] = rolled[:, :tokens]
        bias = bias_s[...].T
        out_ref[h] = jnp.concatenate([bias] * windows, axis=1)
        return carry

    lax.fori_loop(0, heads, head, 0)


def make_bias(last, table, order, levels, lat_rows, rels, slots, windows):
    heads = table.shape[0]
    cell = levels * lat_rows
    tokens = (rels + 1) // 2 * cell
    tiles = order.shape[1] // 128
    vmem = pl.BlockSpec(memory_space=pltpu.VMEM)
    return pl.pallas_call(
        functools.partial(bias_kernel, levels=levels, lat_rows=lat_rows, rels=rels, windows=windows),
        out_shape=jax.ShapeDtypeStruct((heads, tokens, windows * tokens), F32),
        in_specs=[pl.BlockSpec(memory_space=pltpu.SMEM), vmem, vmem],
        out_specs=vmem,
        scratch_shapes=[
            pltpu.VMEM((cell, slots, order.shape[0]), F32),
            pltpu.VMEM((tiles, cell * slots, 128), F32),
            pltpu.VMEM((tokens, tokens), F32),
        ],
        compiler_params=pltpu.CompilerParams(vmem_limit_bytes=32 * 1024 * 1024),
        name="make_bias",
    )(last, table, order)


def turn_kernel(x_ref, out_ref):
    blocks, rows, lanes = x_ref.shape
    turned = x_ref[...].astype(F32).reshape(blocks * rows, lanes).T.astype(BF16)
    for i in range(out_ref.shape[0]):
        out_ref[i] = turned


def turn(x, copies):
    blocks, rows, lanes = x.shape
    vmem = pl.BlockSpec(memory_space=pltpu.VMEM)
    return pl.pallas_call(
        turn_kernel,
        out_shape=jax.ShapeDtypeStruct((copies, lanes, blocks * rows), BF16),
        in_specs=[vmem],
        out_specs=vmem,
        name="turn_weights",
    )(x)


def load_weights(w_s, w_same_ref, w_other_ref, parity):
    pairs, packed, _ = w_same_ref.shape
    part = packed // 4
    for ref, side in ((w_same_ref, parity), (w_other_ref, 1 - parity)):
        for i in range(pairs):
            block = ref[i].astype(F32)
            start = pl.multiple_of((2 * i + side) * part, part)
            for k in range(w_s.shape[0]):
                w_s[k, pl.ds(start, part), :] = block[k * part:(k + 1) * part]


def normalise(x_ref):
    xf = x_ref[...].astype(F32)
    mean = jnp.mean(xf, axis=1, keepdims=True)
    centred = xf - mean
    var = jnp.mean(centred * centred, axis=1, keepdims=True)
    inv = 1.0 / jnp.sqrt(var + EPSILON)
    return centred * inv, inv


def block_kernel(
    me_ref, x_ref, c_ref, gain_ref, w_same_ref, w_other_ref, bias_ref, order_ref, pick_ref,
    same_ref, other_ref, dq_s, dk_s, dv_s,
    w_s, gw_s, normed_s, q_s, d_s, k_s, v_s, ctx_s, dsum_s, fold_s,
    *, heads, windows, levels, lat_rows, rels,
):
    feat = x_ref.shape[1]
    dim = feat // heads
    lon_width = (rels + 1) // 2
    cell = levels * lat_rows
    tokens = lon_width * cell
    scale = 1.0 / math.sqrt(dim)
    tiles = fold_s.shape[0]
    lanes = tiles * 128
    slots = fold_s.shape[1] // cell
    pairs, packed, _ = w_same_ref.shape
    part = packed // 4
    parity = me_ref[0] % 2

    load_weights(w_s, w_same_ref, w_other_ref, parity)
    std, _ = normalise(x_ref)
    normed_s[...] = (std * gain_ref[...]).astype(BF16)
    window = lax.broadcasted_iota(jnp.int32, (dim, windows * tokens), 1) // tokens

    def apart(x):
        x = x.astype(BF16).reshape(heads, dim, windows * tokens)
        return [jnp.where((window == w)[None], x, jnp.zeros_like(x)) for w in range(windows)]

    w_qry = w_s[0].astype(BF16)
    w_key = w_s[1].astype(BF16)
    w_val = w_s[2].astype(BF16)
    w_out = w_s[3].T.astype(BF16)
    for dst, x in ((q_s, mm(w_qry, normed_s[...], NT)), (d_s, mm(w_out, c_ref[...], NT))):
        for w, block in enumerate(apart(x)):
            dst[:, w * dim:(w + 1) * dim, :] = block
    for w in range(windows):
        nw = normed_s[w * tokens:(w + 1) * tokens]
        k_s[:, w * dim:(w + 1) * dim, :] = mm(w_key, nw, NT).astype(BF16).reshape(heads, dim, tokens)
        v_s[:, w * dim:(w + 1) * dim, :] = mm(w_val, nw, NT).astype(BF16).reshape(heads, dim, tokens)
    dsum_s[...] = jnp.zeros_like(dsum_s)
    fold_s[...] = jnp.zeros_like(fold_s)

    def own(x):
        out = x[:dim]
        for w in range(1, windows):
            out = jnp.where(window == w, x[w * dim:(w + 1) * dim], out)
        return out

    def head(h, carry):
        qh, dh, kh, vh = q_s[h], d_s[h], k_s[h], v_s[h]
        score = mm(kh, qh, TN) * (scale * LOG2E) + bias_ref[h]
        d_prob = mm(vh, dh, TN)
        expo = jnp.exp2(score - jnp.max(score, axis=0, keepdims=True))
        prob = expo * (1.0 / jnp.sum(expo, axis=0, keepdims=True))
        low = prob.astype(BF16)
        ctx = own(mm(vh, low, NN))
        ctx_s[h] = ctx.astype(BF16)
        dv_s[h] = mm(dh, low, NT).astype(BF16)
        d_ctx = dh[:dim].astype(F32)
        for w in range(1, windows):
            d_ctx = d_ctx + dh[w * dim:(w + 1) * dim].astype(F32)
        inner = jnp.sum(ctx * d_ctx, axis=0, keepdims=True)
        d_low = (prob * (d_prob - inner)).astype(BF16)
        dq_s[h] = (own(mm(kh, d_low, NN)) * scale).astype(BF16)
        both = mm(jnp.concatenate([qh, pick_ref[...]], axis=0), d_low, NT)
        dk_s[h] = (both[:windows * dim] * scale).astype(BF16)
        dsum_s[:, :tokens] = both[windows * dim:]
        folded = jnp.zeros((cell, lanes), F32)
        for p in range(lon_width):
            off = (lon_width - 1 - p) * cell
            piece = dsum_s[p * cell:(p + 1) * cell, :]
            folded = folded + (pltpu.roll(piece, off, 1) if off else piece)
        for g in range(tiles):
            fold_s[g, pl.ds(h, cell, stride=slots), :] = folded[:, g * 128:(g + 1) * 128]
        return carry

    if UNROLL:
        lax.fori_loop(0, heads, head, 0, unroll=UNROLL)

    def by_window(ref, w):
        return ref[:, w * dim:(w + 1) * dim, :].reshape(feat, tokens)

    gw_s[0] = mm(dq_s[...].reshape(feat, windows * tokens), normed_s[...], NN)
    gw_s[3] = mm(ctx_s[...].reshape(feat, windows * tokens), c_ref[...], NN).T
    for i, ref in ((1, dk_s), (2, dv_s)):
        total = jnp.zeros((feat, feat), F32)
        for w in range(windows):
            total = total + mm(by_window(ref, w), normed_s[w * tokens:(w + 1) * tokens], NN)
        gw_s[i] = total
    g_gain = jnp.zeros((1, feat), F32)
    for i in range(3):
        g_gain = g_gain + jnp.sum(gw_s[i] * w_s[i], axis=0, keepdims=True)
    g_gain = g_gain / gain_ref[...]

    fold = jnp.concatenate([fold_s[g] for g in range(tiles)], axis=1).astype(BF16)
    back = mm(fold, order_ref[...], NT)
    width = lat_rows * rels
    half = back.shape[1] // levels
    per = 2 * pairs // (levels * levels)
    run = lat_rows // per
    wide = -(-run * width // 128) * 128
    back = back.reshape(levels * per, run, slots, levels * half)
    full = []
    for w in range(levels):
        line = jnp.zeros((levels * per * slots, wide), F32)
        for k in range(run):
            piece = back[:, k, :, w * half:(w + 1) * half].reshape(levels * per * slots, half)
            piece = jnp.concatenate([piece, jnp.zeros((levels * per * slots, wide - half), F32)], axis=1)
            line = line + (pltpu.roll(piece, k * width, 1) if k else piece)
        full.append(line)

    lane = lax.broadcasted_iota(jnp.int32, (8, feat), 1) % 128
    row = lax.broadcasted_iota(jnp.int32, (8, feat), 0)
    gains = jnp.zeros((8, feat), F32)
    for i in range(4):
        turned = jnp.concatenate(
            [pltpu.roll(g_gain[:, g * 128:(g + 1) * 128], (160 - 32 * i) % 128, 1) for g in range(feat // 128)], axis=1
        )
        gains = jnp.where((row == 4 + i) & (lane >= 32) & (lane < 64), turned, gains)

    for ref, side in ((same_ref, parity), (other_ref, 1 - parity)):
        for i in range(pairs):
            start = pl.multiple_of((2 * i + side) * part, part)
            block = jnp.concatenate([gw_s[k, pl.ds(start, part), :] for k in range(4)], axis=0)
            ref[i, 0:packed, :] = block.astype(BF16)
    for j in range(2 * pairs):
        z, w, a = j // (levels * per), j // per % levels, j % per
        at = (z * per + a) * slots
        line = full[w][at:at + slots]
        tail = line[:, feat:]
        moved = jnp.concatenate([pltpu.roll(tail[:8], 4, 0), tail[:8], pltpu.roll(tail[8:], 4, 0)], axis=1)
        moved = jnp.where(lane < 32, moved, gains)
        lines = jnp.concatenate([line[:8, :feat], jnp.where(row >= 4, moved, line[8:, :feat])], axis=0).astype(BF16)

        @pl.when(parity == j % 2)
        def _():
            same_ref[j // 2, packed:, :] = lines

        @pl.when(parity != j % 2)
        def _():
            other_ref[j // 2, packed:, :] = lines


def run_block(me, x, c, gain, w_same, w_other, bias, order, pick, heads, windows, levels, lat_rows, rels):
    rows, feat = x.shape
    tokens = rows // windows
    dim = feat // heads
    cell = levels * lat_rows
    tiles = order.shape[1] // 128
    slots = heads + -heads % 16
    pairs, packed, _ = w_same.shape
    vmem = pl.BlockSpec(memory_space=pltpu.VMEM)
    sent = jax.ShapeDtypeStruct((pairs, packed + slots, feat), BF16)
    aligned = jax.ShapeDtypeStruct((heads, windows * dim, tokens), BF16)
    return pl.pallas_call(
        functools.partial(block_kernel, heads=heads, windows=windows, levels=levels, lat_rows=lat_rows, rels=rels),
        out_shape=(sent, sent, jax.ShapeDtypeStruct((heads, dim, rows), BF16), aligned, aligned),
        in_specs=[pl.BlockSpec(memory_space=pltpu.SMEM)] + [vmem] * 8,
        out_specs=[vmem] * 5,
        scratch_shapes=[
            pltpu.VMEM((4, feat, feat), F32),
            pltpu.VMEM((4, feat, feat), F32),
            pltpu.VMEM((rows, feat), BF16),
            pltpu.VMEM((heads, windows * dim, rows), BF16),
            pltpu.VMEM((heads, windows * dim, rows), BF16),
            pltpu.VMEM((heads, windows * dim, tokens), BF16),
            pltpu.VMEM((heads, windows * dim, tokens), BF16),
            pltpu.VMEM((heads, dim, rows), BF16),
            pltpu.VMEM((tokens, tiles * 128), F32),
            pltpu.VMEM((tiles, cell * slots, 128), F32),
        ],
        compiler_params=pltpu.CompilerParams(vmem_limit_bytes=48 * 1024 * 1024),
        name="window_block",
    )(me, x, c, gain, w_same, w_other, bias, order, pick)


def input_kernel(me_ref, x_ref, gain_ref, w_same_ref, w_other_ref, dq_ref, dk_ref, dv_ref, din_ref, w_s):
    heads, stacked, tokens = dk_ref.shape
    rows, feat = x_ref.shape
    windows = rows // tokens
    dim = stacked // windows
    load_weights(w_s, w_same_ref, w_other_ref, me_ref[0] % 2)
    std, inv = normalise(x_ref)
    gain = gain_ref[...]
    w_qry, w_key, w_val = (w_s[i].astype(BF16) for i in range(3))
    from_q = mm(dq_ref[...].reshape(feat, rows), w_qry, TN)
    for w in range(windows):
        at = slice(w * tokens, (w + 1) * tokens)
        d_normed = from_q[at]
        for ref, weight in ((dk_ref, w_key), (dv_ref, w_val)):
            d_normed = d_normed + mm(ref[:, w * dim:(w + 1) * dim, :].reshape(feat, tokens), weight, TN)
        g = d_normed * gain
        d_in = inv[at] * (
            g - jnp.mean(g, axis=1, keepdims=True) - std[at] * jnp.mean(g * std[at], axis=1, keepdims=True)
        )
        din_ref[at] = d_in.astype(BF16)


def input_gradient(me, x, gain, w_same, w_other, dq, dk, dv):
    feat = x.shape[1]
    vmem = pl.BlockSpec(memory_space=pltpu.VMEM)
    return pl.pallas_call(
        input_kernel,
        out_shape=jax.ShapeDtypeStruct(x.shape, BF16),
        in_specs=[pl.BlockSpec(memory_space=pltpu.SMEM)] + [vmem] * 7,
        out_specs=vmem,
        scratch_shapes=[pltpu.VMEM((3, feat, feat), F32)],
        compiler_params=pltpu.CompilerParams(vmem_limit_bytes=32 * 1024 * 1024),
        name="input_gradient",
    )(me, x, gain, w_same, w_other, dq, dk, dv)


def sum_kernel(x_ref, out_ref, table_ref, *, packed):
    pieces, rows, feat = x_ref.shape
    total = x_ref[0].astype(F32)
    for i in range(1, pieces):
        total = total + x_ref[i].astype(F32)
    turned = total[:packed].T
    blocks = out_ref.shape[0]
    part = feat // blocks
    lane = lax.broadcasted_iota(jnp.int32, (1, feat), 1) % 128
    gain = jnp.zeros((1, feat), F32)
    for i in range(4):
        line = total[rows - 4 + i:rows - 3 + i]
        moved = jnp.concatenate(
            [pltpu.roll(line[:, g * 128:(g + 1) * 128], (32 * i - 32) % 128, 1) for g in range(feat // 128)], axis=1
        )
        gain = jnp.where((lane >= 32 * i) & (lane < 32 * i + 32), moved, gain)
    high = gain.astype(BF16).astype(F32)
    gains = jnp.concatenate(
        [src[:, k * packed:(k + 1) * packed] for src in (high, gain - high) for k in range(feat // packed)], axis=0
    )
    for i in range(blocks):
        out_ref[i] = jnp.concatenate([turned[i * part:(i + 1) * part], gains], axis=0).astype(BF16)
    table_ref[...] = total[packed:]


def sum_and_turn(x, blocks, packed):
    pieces, rows, feat = x.shape
    vmem = pl.BlockSpec(memory_space=pltpu.VMEM)
    return pl.pallas_call(
        functools.partial(sum_kernel, packed=packed),
        out_shape=(
            jax.ShapeDtypeStruct((blocks, feat // blocks + 2 * (feat // packed), packed), BF16),
            jax.ShapeDtypeStruct((rows - packed, feat), F32),
        ),
        in_specs=[vmem],
        out_specs=[vmem, vmem],
        name="sum_and_turn",
    )(x)


def last_kernel(x_ref, query_ref, key_ref, value_ref, out_ref, gain_ref):
    total = x_ref[0].astype(F32)
    for i in range(1, x_ref.shape[0]):
        total = total + x_ref[i].astype(F32)
    part = query_ref.shape[0]
    for i, ref in enumerate((query_ref, key_ref, value_ref, out_ref)):
        ref[...] = total[:part, i * part:(i + 1) * part]
    count = (total.shape[0] - part) // 2
    gain = total[part:part + count] + total[part + count:]
    gain_ref[...] = jnp.concatenate([gain[k:k + 1] for k in range(count)], axis=1)


def last_sum(x, part, feat):
    vmem = pl.BlockSpec(memory_space=pltpu.VMEM)
    block = jax.ShapeDtypeStruct((part, part), F32)
    return pl.pallas_call(
        last_kernel,
        out_shape=(block, block, block, block, jax.ShapeDtypeStruct((1, feat), F32)),
        in_specs=[vmem],
        out_specs=[vmem] * 5,
        name="last_sum",
    )(x)


def swap(x, axis, bit):
    n = lax.axis_size(axis)
    return lax.ppermute(x, axis, [(i, i ^ bit) for i in range(n)])


def shift(x, lat_by, lon_by):
    lats, lons = lax.axis_size("lat"), lax.axis_size("lon")
    if lon_by == 0:
        return lax.ppermute(x, "lat", [(i, (i + lat_by) % lats) for i in range(lats)])
    if lat_by == 0:
        return lax.ppermute(x, "lon", [(i, (i + lon_by) % lons) for i in range(lons)])
    pairs = [
        (a * lons + b, (a + lat_by) % lats * lons + (b + lon_by) % lons)
        for a in range(lats)
        for b in range(lons)
    ]
    return lax.ppermute(x, ("lat", "lon"), pairs)


def spread_over_lat(x):
    return lax.all_to_all(x, "lat", 0, 0)


def spread_over_lon(x):
    n = lax.axis_size("lon")
    groups = [list(range(c, n, 2)) for c in range(2)]
    return lax.all_to_all(x, "lon", 0, 0, axis_index_groups=groups)


def local(fields, cotangent, norm_gain, w_query, w_key, w_value, w_out, rel_table):
    levels, lat_rows, lon_cols, feat = fields.shape
    heads = rel_table.shape[1]
    rels = rel_table.shape[2] // (levels * levels * lat_rows * lat_rows)
    lon_width = (rels + 1) // 2
    half_rows = lat_rows // 2
    half_cols = lon_width // 2
    windows = lon_cols // lon_width
    lats = lax.axis_size("lat")
    lons = lax.axis_size("lon")
    me_lat = lax.axis_index("lat")
    me_lon = lax.axis_index("lon")
    part = w_query.shape[0]

    both = jnp.stack([fields, cotangent]).transpose(3, 0, 1, 2, 4)

    mine = jnp.concatenate([w_query, w_key, w_value, w_out], axis=1)
    rows_all = spread_over_lat(jnp.broadcast_to(mine[None], (lats,) + mine.shape))
    own = both[half_cols:, :, :, half_rows:]
    south = shift(both[half_cols:, :, :, :half_rows], -1, 0)
    east = shift(both[:half_cols, :, :, half_rows:], 0, -1)
    corner = shift(both[:half_cols, :, :, :half_rows], -1, -1)
    rows_all, own, south, east, corner = lax.optimization_barrier((rows_all, own, south, east, corner))
    turned = turn(rows_all, lons // 2)
    turned, own, south, east, corner, table = lax.optimization_barrier(
        (turned, own, south, east, corner, rel_table[0])
    )
    w_same = spread_over_lon(turned)
    moved = jnp.concatenate(
        [jnp.concatenate([own, south], axis=3), jnp.concatenate([east, corner], axis=3)], axis=0
    )
    shifted = moved[:, 0].reshape(-1, feat)
    cot_shift = moved[:, 1].reshape(-1, feat)

    order = jnp.asarray(offset_order(rels, levels, lat_rows, 256), BF16)
    last = (me_lat == lats - 1).astype(jnp.int32).reshape(1)
    slots = heads + -heads % 16
    bias = make_bias(last, table, order, levels, lat_rows, rels, slots, windows)
    w_same, bias = lax.optimization_barrier((w_same, bias))
    w_other = swap(w_same, "lon", 1)
    tokens = lon_width * levels * lat_rows
    pick = jnp.asarray(np.tile(np.eye(tokens, dtype=np.float32), (1, windows)), BF16)

    me = me_lon.reshape(1)
    gain = norm_gain[None]
    g_same, g_other, dq, dk, dv = run_block(
        me, shifted, cot_shift, gain, w_same, w_other, bias, order, pick, heads, windows, levels, lat_rows, rels
    )

    paired = (g_same.astype(F32) + swap(g_other, "lon", 1).astype(F32)).astype(BF16)
    paired, dq, dk, dv = lax.optimization_barrier((paired, dq, dk, dv))
    arrived = spread_over_lon(paired)
    message, lines = sum_and_turn(arrived, lats, 4 * part)
    grad_query, grad_key, grad_value, grad_out, grad_gain = last_sum(spread_over_lat(message), part, feat)
    d_input = input_gradient(me, shifted, gain, w_same, w_other, dq, dk, dv)

    d_in = d_input.reshape(lon_cols, levels, lat_rows, feat)
    stay = lon_cols - half_cols
    west = shift(d_in[stay:, :, :half_rows], 0, 1)
    north = shift(d_in[:stay, :, half_rows:], 1, 0)
    corner = shift(d_in[stay:, :, half_rows:], 1, 1)
    west, north, corner, d_in, lines, _ = lax.optimization_barrier((west, north, corner, d_in, lines, message))
    over = rel_table.shape[2] // lons - feat
    groups = feat // 128
    tail = lines[heads:].reshape(slots - heads, groups, 128)[:, :, :over].transpose(1, 0, 2)
    grad_table = jnp.concatenate([lines[:heads], tail.reshape(heads, over)], axis=1)[None]
    back = jnp.concatenate(
        [jnp.concatenate([corner, west], axis=2), jnp.concatenate([north, d_in[:stay, :, :half_rows]], axis=2)],
        axis=0,
    ).transpose(1, 2, 0, 3)
    grad_fields = (cotangent.astype(F32) + back.astype(F32)).astype(BF16)
    return (grad_fields, grad_query, grad_key, grad_value, grad_out, grad_table, grad_gain.reshape(feat))


def solution(mesh):
    return jax.shard_map(
        local,
        mesh=mesh,
        in_specs=(
            P(None, "lat", "lon", None),
            P(None, "lat", "lon", None),
            P(),
            P("lat", "lon"),
            P("lat", "lon"),
            P("lat", "lon"),
            P("lat", "lon"),
            P("lat", None, None),
        ),
        out_specs=(
            P(None, "lat", "lon", None),
            P("lat", "lon"),
            P("lat", "lon"),
            P("lat", "lon"),
            P("lat", "lon"),
            P("lat", None, "lon"),
            P(),
        ),
        check_vma=False,
    )
```

```python
import functools
import math

import jax
import jax.numpy as jnp
import numpy as np
from jax import lax
from jax.experimental import pallas as pl
from jax.experimental.pallas import tpu as pltpu
from jax.sharding import PartitionSpec as P

EPSILON = 1e-05
MASKED = -1000000000.0
LOG2E = math.log2(math.e)
UNROLL = 6
BLOCK_MB = 28
SMALL_MB = 16
F32 = jnp.float32
BF16 = jnp.bfloat16
NN = (((1,), (0,)), ((), ()))
NT = (((1,), (1,)), ((), ()))
TN = (((0,), (0,)), ((), ()))


def mm(a, b, dims):
    return lax.dot_general(a, b, dims, preferred_element_type=F32)


def offset_order(rels, levels, lat_rows, group):
    lanes = rels * levels * lat_rows
    order = np.zeros((levels * group, lanes + -lanes % 128), np.float32)
    for level in range(levels):
        for lat in range(lat_rows):
            for rel in range(rels):
                order[level * group + lat * rels + rel, ((rels - 1 - rel) * levels + level) * lat_rows + lat] = 1.0
    return order


def bias_kernel(last_ref, table_ref, order_ref, out_ref, table_s, strips_s, bias_s, *, levels, lat_rows, rels, windows):
    heads = table_ref.shape[0]
    slots = table_s.shape[1]
    cell = levels * lat_rows
    width = lat_rows * rels
    group = table_s.shape[2] // levels
    tiles = strips_s.shape[0]
    lanes = tiles * 128
    lon_width = (rels + 1) // 2
    tokens = lon_width * cell
    table_s[...] = jnp.zeros_like(table_s)
    table = table_ref[...]
    for z in range(levels):
        for w in range(levels):
            for a in range(lat_rows):
                at = ((z * levels + w) * lat_rows + a) * width
                table_s[z * lat_rows + a, 0:heads, w * group:w * group + width] = table[:, at:at + width]
    full = table_s[...].reshape(cell * slots, levels * group)
    order = order_ref[...]
    high = full.astype(BF16)
    rest = full - high.astype(F32)
    mid = rest.astype(BF16)
    low = (rest - mid.astype(F32)).astype(BF16)
    strips = mm(high, order, NN) + mm(mid, order, NN) + mm(low, order, NN)
    row = lax.broadcasted_iota(jnp.int32, (cell * slots, 1), 0) // slots
    lane = lax.broadcasted_iota(jnp.int32, (1, lanes), 1)
    row_north = (row % lat_rows < lat_rows // 2).astype(F32)
    lane_north = (lane % lat_rows < lat_rows // 2).astype(F32)
    crossing = (row_north != lane_north) & (last_ref[0] != 0)
    strips = jnp.where(crossing, MASKED, strips) * LOG2E
    for g in range(tiles):
        strips_s[g] = strips[:, g * 128:(g + 1) * 128]

    def head(h, carry):
        strip = jnp.concatenate([strips_s[g, pl.ds(h, cell, stride=slots), :] for g in range(tiles)], axis=1)
        for p in range(lon_width):
            off = (lon_width - 1 - p) * cell
            rolled = pltpu.roll(strip, lanes - off, 1) if off else strip
            bias_s[p * cell:(p + 1) * cell, :] = rolled[:, :tokens]
        bias = bias_s[...].T
        out_ref[h] = jnp.concatenate([bias] * windows, axis=1)
        return carry

    lax.fori_loop(0, heads, head, 0)


def make_bias(last, table, order, levels, lat_rows, rels, slots, windows):
    heads = table.shape[0]
    cell = levels * lat_rows
    tokens = (rels + 1) // 2 * cell
    tiles = order.shape[1] // 128
    vmem = pl.BlockSpec(memory_space=pltpu.VMEM)
    return pl.pallas_call(
        functools.partial(bias_kernel, levels=levels, lat_rows=lat_rows, rels=rels, windows=windows),
        out_shape=jax.ShapeDtypeStruct((heads, tokens, windows * tokens), F32),
        in_specs=[pl.BlockSpec(memory_space=pltpu.SMEM), vmem, vmem],
        out_specs=vmem,
        scratch_shapes=[
            pltpu.VMEM((cell, slots, order.shape[0]), F32),
            pltpu.VMEM((tiles, cell * slots, 128), F32),
            pltpu.VMEM((tokens, tokens), F32),
        ],
        compiler_params=pltpu.CompilerParams(vmem_limit_bytes=SMALL_MB * 2**20),
        name="make_bias",
    )(last, table, order)


def turn_kernel(x_ref, out_ref):
    blocks, rows, lanes = x_ref.shape
    turned = x_ref[...].astype(F32).reshape(blocks * rows, lanes).T.astype(BF16)
    for i in range(out_ref.shape[0]):
        out_ref[i] = turned


def turn(x, copies):
    blocks, rows, lanes = x.shape
    vmem = pl.BlockSpec(memory_space=pltpu.VMEM)
    return pl.pallas_call(
        turn_kernel,
        out_shape=jax.ShapeDtypeStruct((copies, lanes, blocks * rows), BF16),
        in_specs=[vmem],
        out_specs=vmem,
        compiler_params=pltpu.CompilerParams(vmem_limit_bytes=SMALL_MB * 2**20),
        name="turn_weights",
    )(x)


def load_weights(w_s, w_same_ref, w_other_ref, parity):
    pairs, packed, _ = w_same_ref.shape
    part = packed // 4
    for ref, side in ((w_same_ref, parity), (w_other_ref, 1 - parity)):
        for i in range(pairs):
            block = ref[i].astype(F32)
            start = pl.multiple_of((2 * i + side) * part, part)
            for k in range(w_s.shape[0]):
                w_s[k, pl.ds(start, part), :] = block[k * part:(k + 1) * part]


def normalise(x_ref):
    xf = x_ref[...].astype(F32)
    mean = jnp.mean(xf, axis=1, keepdims=True)
    centred = xf - mean
    var = jnp.mean(centred * centred, axis=1, keepdims=True)
    inv = 1.0 / jnp.sqrt(var + EPSILON)
    return centred * inv, inv


def block_kernel(
    me_ref, x_ref, c_ref, gain_ref, w_same_ref, w_other_ref, bias_ref, order_ref,
    same_ref, other_ref, dq_s, dk_s, dv_s,
    w_s, gw_s, normed_s, q_s, d_s, k_s, v_s, ctx_s, dsum_s, fold_s, pick_s,
    *, heads, windows, levels, lat_rows, rels,
):
    feat = x_ref.shape[1]
    dim = feat // heads
    lon_width = (rels + 1) // 2
    cell = levels * lat_rows
    tokens = lon_width * cell
    scale = 1.0 / math.sqrt(dim)
    tiles = fold_s.shape[0]
    lanes = tiles * 128
    slots = fold_s.shape[1] // cell
    pairs, packed, _ = w_same_ref.shape
    part = packed // 4
    parity = me_ref[0] % 2

    load_weights(w_s, w_same_ref, w_other_ref, parity)
    std, _ = normalise(x_ref)
    normed_s[...] = (std * gain_ref[...]).astype(BF16)
    window = lax.broadcasted_iota(jnp.int32, (dim, windows * tokens), 1) // tokens

    def apart(x):
        x = x.astype(BF16).reshape(heads, dim, windows * tokens)
        return [jnp.where((window == w)[None], x, jnp.zeros_like(x)) for w in range(windows)]

    w_qry = w_s[0].astype(BF16)
    w_key = w_s[1].astype(BF16)
    w_val = w_s[2].astype(BF16)
    w_out = w_s[3].T.astype(BF16)
    for dst, x in ((q_s, mm(w_qry, normed_s[...], NT)), (d_s, mm(w_out, c_ref[...], NT))):
        for w, block in enumerate(apart(x)):
            dst[:, w * dim:(w + 1) * dim, :] = block
    for w in range(windows):
        nw = normed_s[w * tokens:(w + 1) * tokens]
        k_s[:, w * dim:(w + 1) * dim, :] = mm(w_key, nw, NT).astype(BF16).reshape(heads, dim, tokens)
        v_s[:, w * dim:(w + 1) * dim, :] = mm(w_val, nw, NT).astype(BF16).reshape(heads, dim, tokens)
    query = lax.broadcasted_iota(jnp.int32, (tokens, tokens * windows), 1) % tokens
    pick_s[...] = (query == lax.broadcasted_iota(jnp.int32, query.shape, 0)).astype(F32).astype(BF16)
    dsum_s[...] = jnp.zeros_like(dsum_s)
    fold_s[...] = jnp.zeros_like(fold_s)

    def own(x):
        out = x[:dim]
        for w in range(1, windows):
            out = jnp.where(window == w, x[w * dim:(w + 1) * dim], out)
        return out

    def head(h, carry):
        qh, dh, kh, vh = q_s[h], d_s[h], k_s[h], v_s[h]
        score = mm(kh, qh, TN) * (scale * LOG2E) + bias_ref[h]
        d_prob = mm(vh, dh, TN)
        expo = jnp.exp2(score - jnp.max(score, axis=0, keepdims=True))
        prob = expo * (1.0 / jnp.sum(expo, axis=0, keepdims=True))
        low = prob.astype(BF16)
        ctx = own(mm(vh, low, NN))
        ctx_s[h] = ctx.astype(BF16)
        dv_s[h] = mm(dh, low, NT).astype(BF16)
        d_ctx = dh[:dim].astype(F32)
        for w in range(1, windows):
            d_ctx = d_ctx + dh[w * dim:(w + 1) * dim].astype(F32)
        inner = jnp.sum(ctx * d_ctx, axis=0, keepdims=True)
        d_low = (prob * (d_prob - inner)).astype(BF16)
        dq_s[h] = (own(mm(kh, d_low, NN)) * scale).astype(BF16)
        both = mm(jnp.concatenate([qh, pick_s[...]], axis=0), d_low, NT)
        dk_s[h] = (both[:windows * dim] * scale).astype(BF16)
        dsum_s[:, :tokens] = both[windows * dim:]
        folded = jnp.zeros((cell, lanes), F32)
        for p in range(lon_width):
            off = (lon_width - 1 - p) * cell
            piece = dsum_s[p * cell:(p + 1) * cell, :]
            folded = folded + (pltpu.roll(piece, off, 1) if off else piece)
        for g in range(tiles):
            fold_s[g, pl.ds(h, cell, stride=slots), :] = folded[:, g * 128:(g + 1) * 128]
        return carry

    if UNROLL:
        lax.fori_loop(0, heads, head, 0, unroll=UNROLL)

    def by_window(ref, w):
        return ref[:, w * dim:(w + 1) * dim, :].reshape(feat, tokens)

    gw_s[0] = mm(dq_s[...].reshape(feat, windows * tokens), normed_s[...], NN)
    gw_s[3] = mm(ctx_s[...].reshape(feat, windows * tokens), c_ref[...], NN).T
    for i, ref in ((1, dk_s), (2, dv_s)):
        total = jnp.zeros((feat, feat), F32)
        for w in range(windows):
            total = total + mm(by_window(ref, w), normed_s[w * tokens:(w + 1) * tokens], NN)
        gw_s[i] = total
    g_gain = jnp.zeros((1, feat), F32)
    for i in range(3):
        g_gain = g_gain + jnp.sum(gw_s[i] * w_s[i], axis=0, keepdims=True)
    g_gain = g_gain / gain_ref[...]

    fold = jnp.concatenate([fold_s[g] for g in range(tiles)], axis=1).astype(BF16)
    back = mm(fold, order_ref[...], NT)
    width = lat_rows * rels
    half = back.shape[1] // levels
    per = 2 * pairs // (levels * levels)
    run = lat_rows // per
    wide = -(-run * width // 128) * 128
    back = back.reshape(levels * per, run, slots, levels * half)
    full = []
    for w in range(levels):
        line = jnp.zeros((levels * per * slots, wide), F32)
        for k in range(run):
            piece = back[:, k, :, w * half:(w + 1) * half].reshape(levels * per * slots, half)
            piece = jnp.concatenate([piece, jnp.zeros((levels * per * slots, wide - half), F32)], axis=1)
            line = line + (pltpu.roll(piece, k * width, 1) if k else piece)
        full.append(line)

    lane = lax.broadcasted_iota(jnp.int32, (8, feat), 1) % 128
    row = lax.broadcasted_iota(jnp.int32, (8, feat), 0)
    gains = jnp.zeros((8, feat), F32)
    for i in range(4):
        turned = jnp.concatenate(
            [pltpu.roll(g_gain[:, g * 128:(g + 1) * 128], (160 - 32 * i) % 128, 1) for g in range(feat // 128)], axis=1
        )
        gains = jnp.where((row == 4 + i) & (lane >= 32) & (lane < 64), turned, gains)

    for ref, side in ((same_ref, parity), (other_ref, 1 - parity)):
        for i in range(pairs):
            start = pl.multiple_of((2 * i + side) * part, part)
            block = jnp.concatenate([gw_s[k, pl.ds(start, part), :] for k in range(4)], axis=0)
            ref[i, 0:packed, :] = block.astype(BF16)
    for j in range(2 * pairs):
        z, w, a = j // (levels * per), j // per % levels, j % per
        at = (z * per + a) * slots
        line = full[w][at:at + slots]
        tail = line[:, feat:]
        moved = jnp.concatenate([pltpu.roll(tail[:8], 4, 0), tail[:8], pltpu.roll(tail[8:], 4, 0)], axis=1)
        moved = jnp.where(lane < 32, moved, gains)
        lines = jnp.concatenate([line[:8, :feat], jnp.where(row >= 4, moved, line[8:, :feat])], axis=0).astype(BF16)

        @pl.when(parity == j % 2)
        def _():
            same_ref[j // 2, packed:, :] = lines

        @pl.when(parity != j % 2)
        def _():
            other_ref[j // 2, packed:, :] = lines


def run_block(me, x, c, gain, w_same, w_other, bias, order, heads, windows, levels, lat_rows, rels):
    rows, feat = x.shape
    tokens = rows // windows
    dim = feat // heads
    cell = levels * lat_rows
    tiles = order.shape[1] // 128
    slots = heads + -heads % 16
    pairs, packed, _ = w_same.shape
    vmem = pl.BlockSpec(memory_space=pltpu.VMEM)
    sent = jax.ShapeDtypeStruct((pairs, packed + slots, feat), BF16)
    aligned = jax.ShapeDtypeStruct((heads, windows * dim, tokens), BF16)
    return pl.pallas_call(
        functools.partial(block_kernel, heads=heads, windows=windows, levels=levels, lat_rows=lat_rows, rels=rels),
        out_shape=(sent, sent, jax.ShapeDtypeStruct((heads, dim, rows), BF16), aligned, aligned),
        in_specs=[pl.BlockSpec(memory_space=pltpu.SMEM)] + [vmem] * 7,
        out_specs=[vmem] * 5,
        scratch_shapes=[
            pltpu.VMEM((4, feat, feat), F32),
            pltpu.VMEM((4, feat, feat), F32),
            pltpu.VMEM((rows, feat), BF16),
            pltpu.VMEM((heads, windows * dim, rows), BF16),
            pltpu.VMEM((heads, windows * dim, rows), BF16),
            pltpu.VMEM((heads, windows * dim, tokens), BF16),
            pltpu.VMEM((heads, windows * dim, tokens), BF16),
            pltpu.VMEM((heads, dim, rows), BF16),
            pltpu.VMEM((tokens, tiles * 128), F32),
            pltpu.VMEM((tiles, cell * slots, 128), F32),
            pltpu.VMEM((tokens, rows), BF16),
        ],
        compiler_params=pltpu.CompilerParams(vmem_limit_bytes=BLOCK_MB * 2**20),
        name="window_block",
    )(me, x, c, gain, w_same, w_other, bias, order)


def input_kernel(me_ref, x_ref, gain_ref, w_same_ref, w_other_ref, dq_ref, dk_ref, dv_ref, din_ref, w_s):
    heads, stacked, tokens = dk_ref.shape
    rows, feat = x_ref.shape
    windows = rows // tokens
    dim = stacked // windows
    load_weights(w_s, w_same_ref, w_other_ref, me_ref[0] % 2)
    std, inv = normalise(x_ref)
    gain = gain_ref[...]
    w_qry, w_key, w_val = (w_s[i].astype(BF16) for i in range(3))
    from_q = mm(dq_ref[...].reshape(feat, rows), w_qry, TN)
    for w in range(windows):
        at = slice(w * tokens, (w + 1) * tokens)
        d_normed = from_q[at]
        for ref, weight in ((dk_ref, w_key), (dv_ref, w_val)):
            d_normed = d_normed + mm(ref[:, w * dim:(w + 1) * dim, :].reshape(feat, tokens), weight, TN)
        g = d_normed * gain
        d_in = inv[at] * (
            g - jnp.mean(g, axis=1, keepdims=True) - std[at] * jnp.mean(g * std[at], axis=1, keepdims=True)
        )
        din_ref[at] = d_in.astype(BF16)


def input_gradient(me, x, gain, w_same, w_other, dq, dk, dv):
    feat = x.shape[1]
    vmem = pl.BlockSpec(memory_space=pltpu.VMEM)
    return pl.pallas_call(
        input_kernel,
        out_shape=jax.ShapeDtypeStruct(x.shape, BF16),
        in_specs=[pl.BlockSpec(memory_space=pltpu.SMEM)] + [vmem] * 7,
        out_specs=vmem,
        scratch_shapes=[pltpu.VMEM((3, feat, feat), F32)],
        compiler_params=pltpu.CompilerParams(vmem_limit_bytes=SMALL_MB * 2**20),
        name="input_gradient",
    )(me, x, gain, w_same, w_other, dq, dk, dv)


def sum_kernel(x_ref, out_ref, table_ref, *, packed):
    pieces, rows, feat = x_ref.shape
    total = x_ref[0].astype(F32)
    for i in range(1, pieces):
        total = total + x_ref[i].astype(F32)
    turned = total[:packed].T
    blocks = out_ref.shape[0]
    part = feat // blocks
    lane = lax.broadcasted_iota(jnp.int32, (1, feat), 1) % 128
    gain = jnp.zeros((1, feat), F32)
    for i in range(4):
        line = total[rows - 4 + i:rows - 3 + i]
        moved = jnp.concatenate(
            [pltpu.roll(line[:, g * 128:(g + 1) * 128], (32 * i - 32) % 128, 1) for g in range(feat // 128)], axis=1
        )
        gain = jnp.where((lane >= 32 * i) & (lane < 32 * i + 32), moved, gain)
    high = gain.astype(BF16).astype(F32)
    gains = jnp.concatenate(
        [src[:, k * packed:(k + 1) * packed] for src in (high, gain - high) for k in range(feat // packed)], axis=0
    )
    for i in range(blocks):
        out_ref[i] = jnp.concatenate([turned[i * part:(i + 1) * part], gains], axis=0).astype(BF16)
    table_ref[...] = total[packed:]


def sum_and_turn(x, blocks, packed):
    pieces, rows, feat = x.shape
    vmem = pl.BlockSpec(memory_space=pltpu.VMEM)
    return pl.pallas_call(
        functools.partial(sum_kernel, packed=packed),
        out_shape=(
            jax.ShapeDtypeStruct((blocks, feat // blocks + 2 * (feat // packed), packed), BF16),
            jax.ShapeDtypeStruct((rows - packed, feat), F32),
        ),
        in_specs=[vmem],
        out_specs=[vmem, vmem],
        compiler_params=pltpu.CompilerParams(vmem_limit_bytes=SMALL_MB * 2**20),
        name="sum_and_turn",
    )(x)


def last_kernel(x_ref, query_ref, key_ref, value_ref, out_ref, gain_ref):
    total = x_ref[0].astype(F32)
    for i in range(1, x_ref.shape[0]):
        total = total + x_ref[i].astype(F32)
    part = query_ref.shape[0]
    for i, ref in enumerate((query_ref, key_ref, value_ref, out_ref)):
        ref[...] = total[:part, i * part:(i + 1) * part]
    count = (total.shape[0] - part) // 2
    gain = total[part:part + count] + total[part + count:]
    gain_ref[...] = jnp.concatenate([gain[k:k + 1] for k in range(count)], axis=1).reshape(gain_ref.shape)


def last_sum(x, part, feat):
    vmem = pl.BlockSpec(memory_space=pltpu.VMEM)
    block = jax.ShapeDtypeStruct((part, part), F32)
    return pl.pallas_call(
        last_kernel,
        out_shape=(block, block, block, block, jax.ShapeDtypeStruct((feat,), F32)),
        in_specs=[vmem],
        out_specs=[vmem] * 5,
        compiler_params=pltpu.CompilerParams(vmem_limit_bytes=SMALL_MB * 2**20),
        name="last_sum",
    )(x)


def swap(x, axis, bit):
    n = lax.axis_size(axis)
    return lax.ppermute(x, axis, [(i, i ^ bit) for i in range(n)])


def shift(x, lat_by, lon_by):
    lats, lons = lax.axis_size("lat"), lax.axis_size("lon")
    if lon_by == 0:
        return lax.ppermute(x, "lat", [(i, (i + lat_by) % lats) for i in range(lats)])
    if lat_by == 0:
        return lax.ppermute(x, "lon", [(i, (i + lon_by) % lons) for i in range(lons)])
    pairs = [
        (a * lons + b, (a + lat_by) % lats * lons + (b + lon_by) % lons)
        for a in range(lats)
        for b in range(lons)
    ]
    return lax.ppermute(x, ("lat", "lon"), pairs)


def spread_over_lat(x):
    return lax.all_to_all(x, "lat", 0, 0)


def spread_over_lon(x):
    n = lax.axis_size("lon")
    groups = [list(range(c, n, 2)) for c in range(2)]
    return lax.all_to_all(x, "lon", 0, 0, axis_index_groups=groups)


def local(fields, cotangent, norm_gain, w_query, w_key, w_value, w_out, rel_table):
    levels, lat_rows, lon_cols, feat = fields.shape
    heads = rel_table.shape[1]
    rels = rel_table.shape[2] // (levels * levels * lat_rows * lat_rows)
    lon_width = (rels + 1) // 2
    half_rows = lat_rows // 2
    half_cols = lon_width // 2
    windows = lon_cols // lon_width
    lats = lax.axis_size("lat")
    lons = lax.axis_size("lon")
    me_lat = lax.axis_index("lat")
    me_lon = lax.axis_index("lon")
    part = w_query.shape[0]

    both = jnp.stack([fields, cotangent]).transpose(3, 0, 1, 2, 4)

    mine = jnp.concatenate([w_query, w_key, w_value, w_out], axis=1)
    rows_all = spread_over_lat(jnp.broadcast_to(mine[None], (lats,) + mine.shape))
    turned = turn(rows_all, lons // 2)
    pieces = (
        both[half_cols:, :, :, half_rows:],
        both[half_cols:, :, :, :half_rows],
        both[:half_cols, :, :, half_rows:],
        both[:half_cols, :, :, :half_rows],
    )
    turned, pieces = lax.optimization_barrier((turned, pieces))
    w_same = spread_over_lon(turned)
    own = pieces[0]
    south = shift(pieces[1], -1, 0)
    east = shift(pieces[2], 0, -1)
    corner = shift(pieces[3], -1, -1)
    own, south, east, corner, table = lax.optimization_barrier((own, south, east, corner, rel_table[0]))
    moved = jnp.concatenate(
        [jnp.concatenate([own, south], axis=3), jnp.concatenate([east, corner], axis=3)], axis=0
    )
    shifted = moved[:, 0].reshape(-1, feat)
    cot_shift = moved[:, 1].reshape(-1, feat)

    order = jnp.asarray(offset_order(rels, levels, lat_rows, 256), BF16)
    last = (me_lat == lats - 1).astype(jnp.int32).reshape(1)
    slots = heads + -heads % 16
    bias = make_bias(last, table, order, levels, lat_rows, rels, slots, windows)
    w_same, bias = lax.optimization_barrier((w_same, bias))
    w_other = swap(w_same, "lon", 1)

    me = me_lon.reshape(1)
    gain = norm_gain[None]
    g_same, g_other, dq, dk, dv = run_block(
        me, shifted, cot_shift, gain, w_same, w_other, bias, order, heads, windows, levels, lat_rows, rels
    )

    paired = (g_same.astype(F32) + swap(g_other, "lon", 1).astype(F32)).astype(BF16)
    paired, dq, dk, dv = lax.optimization_barrier((paired, dq, dk, dv))
    arrived = spread_over_lon(paired)
    message, lines = sum_and_turn(arrived, lats, 4 * part)
    grad_query, grad_key, grad_value, grad_out, grad_gain = last_sum(spread_over_lat(message), part, feat)
    d_input = input_gradient(me, shifted, gain, w_same, w_other, dq, dk, dv)

    d_in = d_input.reshape(lon_cols, levels, lat_rows, feat)
    stay = lon_cols - half_cols
    west = shift(d_in[stay:, :, :half_rows], 0, 1)
    north = shift(d_in[:stay, :, half_rows:], 1, 0)
    corner = shift(d_in[stay:, :, half_rows:], 1, 1)
    west, north, corner, d_in, lines, _ = lax.optimization_barrier((west, north, corner, d_in, lines, message))
    over = rel_table.shape[2] // lons - feat
    groups = feat // 128
    tail = lines[heads:].reshape(slots - heads, groups, 128)[:, :, :over].transpose(1, 0, 2)
    grad_table = jnp.concatenate([lines[:heads], tail.reshape(heads, over)], axis=1)[None]
    back = jnp.concatenate(
        [jnp.concatenate([corner, west], axis=2), jnp.concatenate([north, d_in[:stay, :, :half_rows]], axis=2)],
        axis=0,
    ).transpose(1, 2, 0, 3)
    grad_fields = (cotangent.astype(F32) + back.astype(F32)).astype(BF16)
    return (grad_fields, grad_query, grad_key, grad_value, grad_out, grad_table, grad_gain)


def solution(mesh):
    return jax.shard_map(
        local,
        mesh=mesh,
        in_specs=(
            P(None, "lat", "lon", None),
            P(None, "lat", "lon", None),
            P(),
            P("lat", "lon"),
            P("lat", "lon"),
            P("lat", "lon"),
            P("lat", "lon"),
            P("lat", None, None),
        ),
        out_specs=(
            P(None, "lat", "lon", None),
            P("lat", "lon"),
            P("lat", "lon"),
            P("lat", "lon"),
            P("lat", "lon"),
            P("lat", None, "lon"),
            P(),
        ),
        check_vma=False,
    )
```

```python
import functools
import math

import jax
import jax.numpy as jnp
import numpy as np
from jax import lax
from jax.experimental import pallas as pl
from jax.experimental.pallas import tpu as pltpu
from jax.sharding import PartitionSpec as P

EPSILON = 1e-05
MASKED = -1000000000.0
LOG2E = math.log2(math.e)
UNROLL = 6
BLOCK_MB = 48
SMALL_MB = 16
F32 = jnp.float32
BF16 = jnp.bfloat16
NN = (((1,), (0,)), ((), ()))
NT = (((1,), (1,)), ((), ()))
TN = (((0,), (0,)), ((), ()))


def mm(a, b, dims):
    return lax.dot_general(a, b, dims, preferred_element_type=F32)


def offset_order(rels, levels, lat_rows, group):
    lanes = rels * levels * lat_rows
    order = np.zeros((levels * group, lanes + -lanes % 128), np.float32)
    for level in range(levels):
        for lat in range(lat_rows):
            for rel in range(rels):
                order[level * group + lat * rels + rel, ((rels - 1 - rel) * levels + level) * lat_rows + lat] = 1.0
    return order


def bias_kernel(last_ref, table_ref, order_ref, out_ref, table_s, strips_s, bias_s, *, levels, lat_rows, rels, windows):
    heads = table_ref.shape[0]
    slots = table_s.shape[1]
    cell = levels * lat_rows
    width = lat_rows * rels
    group = table_s.shape[2] // levels
    tiles = strips_s.shape[0]
    lanes = tiles * 128
    lon_width = (rels + 1) // 2
    tokens = lon_width * cell
    table_s[...] = jnp.zeros_like(table_s)
    table = table_ref[...]
    for z in range(levels):
        for w in range(levels):
            for a in range(lat_rows):
                at = ((z * levels + w) * lat_rows + a) * width
                table_s[z * lat_rows + a, 0:heads, w * group:w * group + width] = table[:, at:at + width]
    full = table_s[...].reshape(cell * slots, levels * group)
    order = order_ref[...]
    high = full.astype(BF16)
    rest = full - high.astype(F32)
    mid = rest.astype(BF16)
    low = (rest - mid.astype(F32)).astype(BF16)
    strips = mm(high, order, NN) + mm(mid, order, NN) + mm(low, order, NN)
    row = lax.broadcasted_iota(jnp.int32, (cell * slots, 1), 0) // slots
    lane = lax.broadcasted_iota(jnp.int32, (1, lanes), 1)
    row_north = (row % lat_rows < lat_rows // 2).astype(F32)
    lane_north = (lane % lat_rows < lat_rows // 2).astype(F32)
    crossing = (row_north != lane_north) & (last_ref[0] != 0)
    strips = jnp.where(crossing, MASKED, strips) * LOG2E
    for g in range(tiles):
        strips_s[g] = strips[:, g * 128:(g + 1) * 128]

    def head(h, carry):
        strip = jnp.concatenate([strips_s[g, pl.ds(h, cell, stride=slots), :] for g in range(tiles)], axis=1)
        for p in range(lon_width):
            off = (lon_width - 1 - p) * cell
            rolled = pltpu.roll(strip, lanes - off, 1) if off else strip
            bias_s[p * cell:(p + 1) * cell, :] = rolled[:, :tokens]
        bias = bias_s[...].T
        out_ref[h] = jnp.concatenate([bias] * windows, axis=1)
        return carry

    lax.fori_loop(0, heads, head, 0)


def make_bias(last, table, order, levels, lat_rows, rels, slots, windows):
    heads = table.shape[0]
    cell = levels * lat_rows
    tokens = (rels + 1) // 2 * cell
    tiles = order.shape[1] // 128
    vmem = pl.BlockSpec(memory_space=pltpu.VMEM)
    return pl.pallas_call(
        functools.partial(bias_kernel, levels=levels, lat_rows=lat_rows, rels=rels, windows=windows),
        out_shape=jax.ShapeDtypeStruct((heads, tokens, windows * tokens), F32),
        in_specs=[pl.BlockSpec(memory_space=pltpu.SMEM), vmem, vmem],
        out_specs=vmem,
        scratch_shapes=[
            pltpu.VMEM((cell, slots, order.shape[0]), F32),
            pltpu.VMEM((tiles, cell * slots, 128), F32),
            pltpu.VMEM((tokens, tokens), F32),
        ],
        compiler_params=pltpu.CompilerParams(vmem_limit_bytes=SMALL_MB * 2**20),
        name="make_bias",
    )(last, table, order)


def turn_kernel(x_ref, out_ref):
    blocks, rows, lanes = x_ref.shape
    turned = x_ref[...].astype(F32).reshape(blocks * rows, lanes).T.astype(BF16)
    for i in range(out_ref.shape[0]):
        out_ref[i] = turned


def turn(x, copies):
    blocks, rows, lanes = x.shape
    vmem = pl.BlockSpec(memory_space=pltpu.VMEM)
    return pl.pallas_call(
        turn_kernel,
        out_shape=jax.ShapeDtypeStruct((copies, lanes, blocks * rows), BF16),
        in_specs=[vmem],
        out_specs=vmem,
        compiler_params=pltpu.CompilerParams(vmem_limit_bytes=SMALL_MB * 2**20),
        name="turn_weights",
    )(x)


def load_weights(w_s, w_same_ref, w_other_ref, parity):
    pairs, packed, _ = w_same_ref.shape
    part = packed // 4
    for ref, side in ((w_same_ref, parity), (w_other_ref, 1 - parity)):
        for i in range(pairs):
            block = ref[i].astype(F32)
            start = pl.multiple_of((2 * i + side) * part, part)
            for k in range(w_s.shape[0]):
                w_s[k, pl.ds(start, part), :] = block[k * part:(k + 1) * part]


def normalise(x_ref):
    xf = x_ref[...].astype(F32)
    mean = jnp.mean(xf, axis=1, keepdims=True)
    centred = xf - mean
    var = jnp.mean(centred * centred, axis=1, keepdims=True)
    inv = 1.0 / jnp.sqrt(var + EPSILON)
    return centred * inv, inv


def block_kernel(
    me_ref, x_ref, c_ref, gain_ref, w_same_ref, w_other_ref, bias_ref, order_ref,
    same_ref, other_ref, dq_s, dk_s, dv_s,
    w_s, gw_s, normed_s, q_s, d_s, k_s, v_s, ctx_s, dsum_s, fold_s, pick_s,
    *, heads, windows, levels, lat_rows, rels,
):
    feat = x_ref.shape[1]
    dim = feat // heads
    lon_width = (rels + 1) // 2
    cell = levels * lat_rows
    tokens = lon_width * cell
    scale = 1.0 / math.sqrt(dim)
    tiles = fold_s.shape[0]
    lanes = tiles * 128
    slots = fold_s.shape[1] // cell
    pairs, packed, _ = w_same_ref.shape
    part = packed // 4
    parity = me_ref[0] % 2

    load_weights(w_s, w_same_ref, w_other_ref, parity)
    std, _ = normalise(x_ref)
    normed_s[...] = (std * gain_ref[...]).astype(BF16)
    window = lax.broadcasted_iota(jnp.int32, (dim, windows * tokens), 1) // tokens

    def apart(x):
        x = x.astype(BF16).reshape(heads, dim, windows * tokens)
        return [jnp.where((window == w)[None], x, jnp.zeros_like(x)) for w in range(windows)]

    w_qry = w_s[0].astype(BF16)
    w_key = w_s[1].astype(BF16)
    w_val = w_s[2].astype(BF16)
    w_out = w_s[3].T.astype(BF16)
    for dst, x in ((q_s, mm(w_qry, normed_s[...], NT)), (d_s, mm(w_out, c_ref[...], NT))):
        for w, block in enumerate(apart(x)):
            dst[:, w * dim:(w + 1) * dim, :] = block
    for w in range(windows):
        nw = normed_s[w * tokens:(w + 1) * tokens]
        k_s[:, w * dim:(w + 1) * dim, :] = mm(w_key, nw, NT).astype(BF16).reshape(heads, dim, tokens)
        v_s[:, w * dim:(w + 1) * dim, :] = mm(w_val, nw, NT).astype(BF16).reshape(heads, dim, tokens)
    query = lax.broadcasted_iota(jnp.int32, (tokens, tokens * windows), 1) % tokens
    pick_s[...] = (query == lax.broadcasted_iota(jnp.int32, query.shape, 0)).astype(F32).astype(BF16)
    dsum_s[...] = jnp.zeros_like(dsum_s)
    fold_s[...] = jnp.zeros_like(fold_s)

    def own(x):
        out = x[:dim]
        for w in range(1, windows):
            out = jnp.where(window == w, x[w * dim:(w + 1) * dim], out)
        return out

    def head(h, carry):
        qh, dh, kh, vh = q_s[h], d_s[h], k_s[h], v_s[h]
        score = mm(kh, qh, TN) * (scale * LOG2E) + bias_ref[h]
        d_prob = mm(vh, dh, TN)
        expo = jnp.exp2(score - jnp.max(score, axis=0, keepdims=True))
        prob = expo * (1.0 / jnp.sum(expo, axis=0, keepdims=True))
        low = prob.astype(BF16)
        ctx = own(mm(vh, low, NN))
        ctx_s[h] = ctx.astype(BF16)
        dv_s[h] = mm(dh, low, NT).astype(BF16)
        d_ctx = dh[:dim].astype(F32)
        for w in range(1, windows):
            d_ctx = d_ctx + dh[w * dim:(w + 1) * dim].astype(F32)
        inner = jnp.sum(ctx * d_ctx, axis=0, keepdims=True)
        d_low = (prob * (d_prob - inner)).astype(BF16)
        dq_s[h] = (own(mm(kh, d_low, NN)) * scale).astype(BF16)
        both = mm(jnp.concatenate([qh, pick_s[...]], axis=0), d_low, NT)
        dk_s[h] = (both[:windows * dim] * scale).astype(BF16)
        dsum_s[:, :tokens] = both[windows * dim:]
        folded = jnp.zeros((cell, lanes), F32)
        for p in range(lon_width):
            off = (lon_width - 1 - p) * cell
            piece = dsum_s[p * cell:(p + 1) * cell, :]
            folded = folded + (pltpu.roll(piece, off, 1) if off else piece)
        for g in range(tiles):
            fold_s[g, pl.ds(h, cell, stride=slots), :] = folded[:, g * 128:(g + 1) * 128]
        return carry

    if UNROLL:
        lax.fori_loop(0, heads, head, 0, unroll=UNROLL)

    def by_window(ref, w):
        return ref[:, w * dim:(w + 1) * dim, :].reshape(feat, tokens)

    gw_s[0] = mm(dq_s[...].reshape(feat, windows * tokens), normed_s[...], NN)
    gw_s[3] = mm(ctx_s[...].reshape(feat, windows * tokens), c_ref[...], NN).T
    for i, ref in ((1, dk_s), (2, dv_s)):
        total = jnp.zeros((feat, feat), F32)
        for w in range(windows):
            total = total + mm(by_window(ref, w), normed_s[w * tokens:(w + 1) * tokens], NN)
        gw_s[i] = total
    g_gain = jnp.zeros((1, feat), F32)
    for i in range(3):
        g_gain = g_gain + jnp.sum(gw_s[i] * w_s[i], axis=0, keepdims=True)
    g_gain = g_gain / gain_ref[...]

    fold = jnp.concatenate([fold_s[g] for g in range(tiles)], axis=1).astype(BF16)
    back = mm(fold, order_ref[...], NT)
    width = lat_rows * rels
    half = back.shape[1] // levels
    per = 2 * pairs // (levels * levels)
    run = lat_rows // per
    wide = -(-run * width // 128) * 128
    back = back.reshape(levels * per, run, slots, levels * half)
    full = []
    for w in range(levels):
        line = jnp.zeros((levels * per * slots, wide), F32)
        for k in range(run):
            piece = back[:, k, :, w * half:(w + 1) * half].reshape(levels * per * slots, half)
            piece = jnp.concatenate([piece, jnp.zeros((levels * per * slots, wide - half), F32)], axis=1)
            line = line + (pltpu.roll(piece, k * width, 1) if k else piece)
        full.append(line)

    lane = lax.broadcasted_iota(jnp.int32, (8, feat), 1) % 128
    row = lax.broadcasted_iota(jnp.int32, (8, feat), 0)
    gains = jnp.zeros((8, feat), F32)
    for i in range(4):
        turned = jnp.concatenate(
            [pltpu.roll(g_gain[:, g * 128:(g + 1) * 128], (160 - 32 * i) % 128, 1) for g in range(feat // 128)], axis=1
        )
        gains = jnp.where((row == 4 + i) & (lane >= 32) & (lane < 64), turned, gains)

    for ref, side in ((same_ref, parity), (other_ref, 1 - parity)):
        for i in range(pairs):
            start = pl.multiple_of((2 * i + side) * part, part)
            block = jnp.concatenate([gw_s[k, pl.ds(start, part), :] for k in range(4)], axis=0)
            ref[i, 0:packed, :] = block.astype(BF16)
    for j in range(2 * pairs):
        z, w, a = j // (levels * per), j // per % levels, j % per
        at = (z * per + a) * slots
        line = full[w][at:at + slots]
        tail = line[:, feat:]
        moved = jnp.concatenate([pltpu.roll(tail[:8], 4, 0), tail[:8], pltpu.roll(tail[8:], 4, 0)], axis=1)
        moved = jnp.where(lane < 32, moved, gains)
        lines = jnp.concatenate([line[:8, :feat], jnp.where(row >= 4, moved, line[8:, :feat])], axis=0).astype(BF16)

        @pl.when(parity == j % 2)
        def _():
            same_ref[j // 2, packed:, :] = lines

        @pl.when(parity != j % 2)
        def _():
            other_ref[j // 2, packed:, :] = lines


def run_block(me, x, c, gain, w_same, w_other, bias, order, heads, windows, levels, lat_rows, rels):
    rows, feat = x.shape
    tokens = rows // windows
    dim = feat // heads
    cell = levels * lat_rows
    tiles = order.shape[1] // 128
    slots = heads + -heads % 16
    pairs, packed, _ = w_same.shape
    vmem = pl.BlockSpec(memory_space=pltpu.VMEM)
    sent = jax.ShapeDtypeStruct((pairs, packed + slots, feat), BF16)
    aligned = jax.ShapeDtypeStruct((heads, windows * dim, tokens), BF16)
    return pl.pallas_call(
        functools.partial(block_kernel, heads=heads, windows=windows, levels=levels, lat_rows=lat_rows, rels=rels),
        out_shape=(sent, sent, jax.ShapeDtypeStruct((heads, dim, rows), BF16), aligned, aligned),
        in_specs=[pl.BlockSpec(memory_space=pltpu.SMEM)] + [vmem] * 7,
        out_specs=[vmem] * 5,
        scratch_shapes=[
            pltpu.VMEM((4, feat, feat), F32),
            pltpu.VMEM((4, feat, feat), F32),
            pltpu.VMEM((rows, feat), BF16),
            pltpu.VMEM((heads, windows * dim, rows), BF16),
            pltpu.VMEM((heads, windows * dim, rows), BF16),
            pltpu.VMEM((heads, windows * dim, tokens), BF16),
            pltpu.VMEM((heads, windows * dim, tokens), BF16),
            pltpu.VMEM((heads, dim, rows), BF16),
            pltpu.VMEM((tokens, tiles * 128), F32),
            pltpu.VMEM((tiles, cell * slots, 128), F32),
            pltpu.VMEM((tokens, rows), BF16),
        ],
        compiler_params=pltpu.CompilerParams(vmem_limit_bytes=BLOCK_MB * 2**20),
        name="window_block",
    )(me, x, c, gain, w_same, w_other, bias, order)


def input_kernel(me_ref, x_ref, gain_ref, w_same_ref, w_other_ref, dq_ref, dk_ref, dv_ref, din_ref, w_s):
    heads, stacked, tokens = dk_ref.shape
    rows, feat = x_ref.shape
    windows = rows // tokens
    dim = stacked // windows
    load_weights(w_s, w_same_ref, w_other_ref, me_ref[0] % 2)
    std, inv = normalise(x_ref)
    gain = gain_ref[...]
    w_qry, w_key, w_val = (w_s[i].astype(BF16) for i in range(3))
    from_q = mm(dq_ref[...].reshape(feat, rows), w_qry, TN)
    for w in range(windows):
        at = slice(w * tokens, (w + 1) * tokens)
        d_normed = from_q[at]
        for ref, weight in ((dk_ref, w_key), (dv_ref, w_val)):
            d_normed = d_normed + mm(ref[:, w * dim:(w + 1) * dim, :].reshape(feat, tokens), weight, TN)
        g = d_normed * gain
        d_in = inv[at] * (
            g - jnp.mean(g, axis=1, keepdims=True) - std[at] * jnp.mean(g * std[at], axis=1, keepdims=True)
        )
        din_ref[at] = d_in.astype(BF16)


def input_gradient(me, x, gain, w_same, w_other, dq, dk, dv):
    feat = x.shape[1]
    vmem = pl.BlockSpec(memory_space=pltpu.VMEM)
    return pl.pallas_call(
        input_kernel,
        out_shape=jax.ShapeDtypeStruct(x.shape, BF16),
        in_specs=[pl.BlockSpec(memory_space=pltpu.SMEM)] + [vmem] * 7,
        out_specs=vmem,
        scratch_shapes=[pltpu.VMEM((3, feat, feat), F32)],
        compiler_params=pltpu.CompilerParams(vmem_limit_bytes=SMALL_MB * 2**20),
        name="input_gradient",
    )(me, x, gain, w_same, w_other, dq, dk, dv)


def sum_kernel(x_ref, out_ref, table_ref, *, packed):
    pieces, rows, feat = x_ref.shape
    total = x_ref[0].astype(F32)
    for i in range(1, pieces):
        total = total + x_ref[i].astype(F32)
    turned = total[:packed].T
    blocks = out_ref.shape[0]
    part = feat // blocks
    lane = lax.broadcasted_iota(jnp.int32, (1, feat), 1) % 128
    gain = jnp.zeros((1, feat), F32)
    for i in range(4):
        line = total[rows - 4 + i:rows - 3 + i]
        moved = jnp.concatenate(
            [pltpu.roll(line[:, g * 128:(g + 1) * 128], (32 * i - 32) % 128, 1) for g in range(feat // 128)], axis=1
        )
        gain = jnp.where((lane >= 32 * i) & (lane < 32 * i + 32), moved, gain)
    high = gain.astype(BF16).astype(F32)
    gains = jnp.concatenate(
        [src[:, k * packed:(k + 1) * packed] for src in (high, gain - high) for k in range(feat // packed)], axis=0
    )
    for i in range(blocks):
        out_ref[i] = jnp.concatenate([turned[i * part:(i + 1) * part], gains], axis=0).astype(BF16)
    table_ref[...] = total[packed:]


def sum_and_turn(x, blocks, packed):
    pieces, rows, feat = x.shape
    vmem = pl.BlockSpec(memory_space=pltpu.VMEM)
    return pl.pallas_call(
        functools.partial(sum_kernel, packed=packed),
        out_shape=(
            jax.ShapeDtypeStruct((blocks, feat // blocks + 2 * (feat // packed), packed), BF16),
            jax.ShapeDtypeStruct((rows - packed, feat), F32),
        ),
        in_specs=[vmem],
        out_specs=[vmem, vmem],
        compiler_params=pltpu.CompilerParams(vmem_limit_bytes=SMALL_MB * 2**20),
        name="sum_and_turn",
    )(x)


def last_kernel(x_ref, query_ref, key_ref, value_ref, out_ref, gain_ref):
    total = x_ref[0].astype(F32)
    for i in range(1, x_ref.shape[0]):
        total = total + x_ref[i].astype(F32)
    part = query_ref.shape[0]
    for i, ref in enumerate((query_ref, key_ref, value_ref, out_ref)):
        ref[...] = total[:part, i * part:(i + 1) * part]
    count = (total.shape[0] - part) // 2
    gain = total[part:part + count] + total[part + count:]
    gain_ref[...] = jnp.concatenate([gain[k:k + 1] for k in range(count)], axis=1).reshape(gain_ref.shape)


def last_sum(x, part, feat):
    vmem = pl.BlockSpec(memory_space=pltpu.VMEM)
    block = jax.ShapeDtypeStruct((part, part), F32)
    return pl.pallas_call(
        last_kernel,
        out_shape=(block, block, block, block, jax.ShapeDtypeStruct((feat,), F32)),
        in_specs=[vmem],
        out_specs=[vmem] * 5,
        compiler_params=pltpu.CompilerParams(vmem_limit_bytes=SMALL_MB * 2**20),
        name="last_sum",
    )(x)


def swap(x, axis, bit):
    n = lax.axis_size(axis)
    return lax.ppermute(x, axis, [(i, i ^ bit) for i in range(n)])


def shift(x, lat_by, lon_by):
    lats, lons = lax.axis_size("lat"), lax.axis_size("lon")
    if lon_by == 0:
        return lax.ppermute(x, "lat", [(i, (i + lat_by) % lats) for i in range(lats)])
    if lat_by == 0:
        return lax.ppermute(x, "lon", [(i, (i + lon_by) % lons) for i in range(lons)])
    pairs = [
        (a * lons + b, (a + lat_by) % lats * lons + (b + lon_by) % lons)
        for a in range(lats)
        for b in range(lons)
    ]
    return lax.ppermute(x, ("lat", "lon"), pairs)


def spread_over_lat(x):
    return lax.all_to_all(x, "lat", 0, 0)


def spread_over_lon(x):
    n = lax.axis_size("lon")
    groups = [list(range(c, n, 2)) for c in range(2)]
    return lax.all_to_all(x, "lon", 0, 0, axis_index_groups=groups)


def local(fields, cotangent, norm_gain, w_query, w_key, w_value, w_out, rel_table):
    levels, lat_rows, lon_cols, feat = fields.shape
    heads = rel_table.shape[1]
    rels = rel_table.shape[2] // (levels * levels * lat_rows * lat_rows)
    lon_width = (rels + 1) // 2
    half_rows = lat_rows // 2
    half_cols = lon_width // 2
    windows = lon_cols // lon_width
    lats = lax.axis_size("lat")
    lons = lax.axis_size("lon")
    me_lat = lax.axis_index("lat")
    me_lon = lax.axis_index("lon")
    part = w_query.shape[0]

    both = jnp.stack([fields, cotangent]).transpose(3, 0, 1, 2, 4)

    mine = jnp.concatenate([w_query, w_key, w_value, w_out], axis=1)
    rows_all = spread_over_lat(jnp.broadcast_to(mine[None], (lats,) + mine.shape))
    turned = turn(rows_all, lons // 2)
    turned, table = lax.optimization_barrier((turned, rel_table[0]))
    w_same = spread_over_lon(turned)
    own = both[half_cols:, :, :, half_rows:]
    south = shift(both[half_cols:, :, :, :half_rows], -1, 0)
    east = shift(both[:half_cols, :, :, half_rows:], 0, -1)
    corner = shift(both[:half_cols, :, :, :half_rows], -1, -1)

    order = jnp.asarray(offset_order(rels, levels, lat_rows, 256), BF16)
    last = (me_lat == lats - 1).astype(jnp.int32).reshape(1)
    slots = heads + -heads % 16
    bias = make_bias(last, table, order, levels, lat_rows, rels, slots, windows)
    w_same, bias, own, south, east, corner = lax.optimization_barrier((w_same, bias, own, south, east, corner))
    w_other = swap(w_same, "lon", 1)
    moved = jnp.concatenate(
        [jnp.concatenate([own, south], axis=3), jnp.concatenate([east, corner], axis=3)], axis=0
    )
    shifted = moved[:, 0].reshape(-1, feat)
    cot_shift = moved[:, 1].reshape(-1, feat)

    me = me_lon.reshape(1)
    gain = norm_gain[None]
    g_same, g_other, dq, dk, dv = run_block(
        me, shifted, cot_shift, gain, w_same, w_other, bias, order, heads, windows, levels, lat_rows, rels
    )

    paired = (g_same.astype(F32) + swap(g_other, "lon", 1).astype(F32)).astype(BF16)
    paired, dq, dk, dv = lax.optimization_barrier((paired, dq, dk, dv))
    arrived = spread_over_lon(paired)
    message, lines = sum_and_turn(arrived, lats, 4 * part)
    grad_query, grad_key, grad_value, grad_out, grad_gain = last_sum(spread_over_lat(message), part, feat)
    d_input = input_gradient(me, shifted, gain, w_same, w_other, dq, dk, dv)

    d_in = d_input.reshape(lon_cols, levels, lat_rows, feat)
    stay = lon_cols - half_cols
    west = shift(d_in[stay:, :, :half_rows], 0, 1)
    north = shift(d_in[:stay, :, half_rows:], 1, 0)
    corner = shift(d_in[stay:, :, half_rows:], 1, 1)
    west, north, corner, d_in, lines, _ = lax.optimization_barrier((west, north, corner, d_in, lines, message))
    over = rel_table.shape[2] // lons - feat
    groups = feat // 128
    tail = lines[heads:].reshape(slots - heads, groups, 128)[:, :, :over].transpose(1, 0, 2)
    grad_table = jnp.concatenate([lines[:heads], tail.reshape(heads, over)], axis=1)[None]
    back = jnp.concatenate(
        [jnp.concatenate([corner, west], axis=2), jnp.concatenate([north, d_in[:stay, :, :half_rows]], axis=2)],
        axis=0,
    ).transpose(1, 2, 0, 3)
    grad_fields = (cotangent.astype(F32) + back.astype(F32)).astype(BF16)
    return (grad_fields, grad_query, grad_key, grad_value, grad_out, grad_table, grad_gain)


def solution(mesh):
    return jax.shard_map(
        local,
        mesh=mesh,
        in_specs=(
            P(None, "lat", "lon", None),
            P(None, "lat", "lon", None),
            P(),
            P("lat", "lon"),
            P("lat", "lon"),
            P("lat", "lon"),
            P("lat", "lon"),
            P("lat", None, None),
        ),
        out_specs=(
            P(None, "lat", "lon", None),
            P("lat", "lon"),
            P("lat", "lon"),
            P("lat", "lon"),
            P("lat", "lon"),
            P("lat", None, "lon"),
            P(),
        ),
        check_vma=False,
    )
```

```python
import functools
import math

import jax
import jax.numpy as jnp
import numpy as np
from jax import lax
from jax.experimental import pallas as pl
from jax.experimental.pallas import tpu as pltpu
from jax.sharding import PartitionSpec as P

EPSILON = 1e-05
MASKED = -1000000000.0
LOG2E = math.log2(math.e)
UNROLL = 12
BLOCK_MB = 48
SMALL_MB = 16
F32 = jnp.float32
BF16 = jnp.bfloat16
NN = (((1,), (0,)), ((), ()))
NT = (((1,), (1,)), ((), ()))
TN = (((0,), (0,)), ((), ()))


def mm(a, b, dims):
    return lax.dot_general(a, b, dims, preferred_element_type=F32)


def offset_order(rels, levels, lat_rows, group):
    lanes = rels * levels * lat_rows
    order = np.zeros((levels * group, lanes + -lanes % 128), np.float32)
    for level in range(levels):
        for lat in range(lat_rows):
            for rel in range(rels):
                order[level * group + lat * rels + rel, ((rels - 1 - rel) * levels + level) * lat_rows + lat] = 1.0
    return order


def bias_kernel(last_ref, table_ref, order_ref, out_ref, table_s, strips_s, bias_s, *, levels, lat_rows, rels, windows):
    heads = table_ref.shape[0]
    slots = table_s.shape[1]
    cell = levels * lat_rows
    width = lat_rows * rels
    group = table_s.shape[2] // levels
    tiles = strips_s.shape[0]
    lanes = tiles * 128
    lon_width = (rels + 1) // 2
    tokens = lon_width * cell
    table_s[...] = jnp.zeros_like(table_s)
    table = table_ref[...]
    for z in range(levels):
        for w in range(levels):
            for a in range(lat_rows):
                at = ((z * levels + w) * lat_rows + a) * width
                table_s[z * lat_rows + a, 0:heads, w * group:w * group + width] = table[:, at:at + width]
    full = table_s[...].reshape(cell * slots, levels * group)
    order = order_ref[...]
    high = full.astype(BF16)
    rest = full - high.astype(F32)
    mid = rest.astype(BF16)
    low = (rest - mid.astype(F32)).astype(BF16)
    strips = mm(high, order, NN) + mm(mid, order, NN) + mm(low, order, NN)
    row = lax.broadcasted_iota(jnp.int32, (cell * slots, 1), 0) // slots
    lane = lax.broadcasted_iota(jnp.int32, (1, lanes), 1)
    row_north = (row % lat_rows < lat_rows // 2).astype(F32)
    lane_north = (lane % lat_rows < lat_rows // 2).astype(F32)
    crossing = (row_north != lane_north) & (last_ref[0] != 0)
    strips = jnp.where(crossing, MASKED, strips) * LOG2E
    for g in range(tiles):
        strips_s[g] = strips[:, g * 128:(g + 1) * 128]

    def head(h, carry):
        strip = jnp.concatenate([strips_s[g, pl.ds(h, cell, stride=slots), :] for g in range(tiles)], axis=1)
        for p in range(lon_width):
            off = (lon_width - 1 - p) * cell
            rolled = pltpu.roll(strip, lanes - off, 1) if off else strip
            bias_s[p * cell:(p + 1) * cell, :] = rolled[:, :tokens]
        out_ref[h] = bias_s[...].T
        return carry

    lax.fori_loop(0, heads, head, 0)


def make_bias(last, table, order, levels, lat_rows, rels, slots, windows):
    heads = table.shape[0]
    cell = levels * lat_rows
    tokens = (rels + 1) // 2 * cell
    tiles = order.shape[1] // 128
    vmem = pl.BlockSpec(memory_space=pltpu.VMEM)
    return pl.pallas_call(
        functools.partial(bias_kernel, levels=levels, lat_rows=lat_rows, rels=rels, windows=windows),
        out_shape=jax.ShapeDtypeStruct((heads, tokens, tokens), F32),
        in_specs=[pl.BlockSpec(memory_space=pltpu.SMEM), vmem, vmem],
        out_specs=vmem,
        scratch_shapes=[
            pltpu.VMEM((cell, slots, order.shape[0]), F32),
            pltpu.VMEM((tiles, cell * slots, 128), F32),
            pltpu.VMEM((tokens, tokens), F32),
        ],
        compiler_params=pltpu.CompilerParams(vmem_limit_bytes=SMALL_MB * 2**20),
        name="make_bias",
    )(last, table, order)


def turn_kernel(x_ref, out_ref):
    blocks, rows, lanes = x_ref.shape
    turned = x_ref[...].astype(F32).reshape(blocks * rows, lanes).T.astype(BF16)
    for i in range(out_ref.shape[0]):
        out_ref[i] = turned


def turn(x, copies):
    blocks, rows, lanes = x.shape
    vmem = pl.BlockSpec(memory_space=pltpu.VMEM)
    return pl.pallas_call(
        turn_kernel,
        out_shape=jax.ShapeDtypeStruct((copies, lanes, blocks * rows), BF16),
        in_specs=[vmem],
        out_specs=vmem,
        compiler_params=pltpu.CompilerParams(vmem_limit_bytes=SMALL_MB * 2**20),
        name="turn_weights",
    )(x)


def load_weights(w_s, w_same_ref, w_other_ref, parity):
    pairs, packed, _ = w_same_ref.shape
    part = packed // 4
    for ref, side in ((w_same_ref, parity), (w_other_ref, 1 - parity)):
        for i in range(pairs):
            block = ref[i].astype(F32)
            start = pl.multiple_of((2 * i + side) * part, part)
            for k in range(w_s.shape[0]):
                w_s[k, pl.ds(start, part), :] = block[k * part:(k + 1) * part]


def normalise(x_ref):
    xf = x_ref[...].astype(F32)
    mean = jnp.mean(xf, axis=1, keepdims=True)
    centred = xf - mean
    var = jnp.mean(centred * centred, axis=1, keepdims=True)
    inv = 1.0 / jnp.sqrt(var + EPSILON)
    return centred * inv, inv


def block_kernel(
    me_ref, x_ref, c_ref, gain_ref, w_same_ref, w_other_ref, bias_ref, order_ref,
    same_ref, other_ref, dq_s, dk_s, dv_s,
    w_s, gw_s, normed_s, q_s, d_s, k_s, v_s, ctx_s, dsum_s, fold_s, pick_s, lines_s,
    *, heads, windows, levels, lat_rows, rels,
):
    feat = x_ref.shape[1]
    dim = feat // heads
    lon_width = (rels + 1) // 2
    cell = levels * lat_rows
    tokens = lon_width * cell
    scale = 1.0 / math.sqrt(dim)
    tiles = fold_s.shape[0]
    lanes = tiles * 128
    slots = fold_s.shape[1] // cell
    pairs, packed, _ = w_same_ref.shape
    part = packed // 4
    parity = me_ref[0] % 2

    load_weights(w_s, w_same_ref, w_other_ref, parity)
    std, _ = normalise(x_ref)
    normed_s[...] = (std * gain_ref[...]).astype(BF16)
    window = lax.broadcasted_iota(jnp.int32, (dim, windows * tokens), 1) // tokens

    def apart(x):
        x = x.astype(BF16).reshape(heads, dim, windows * tokens)
        return [jnp.where((window == w)[None], x, jnp.zeros_like(x)) for w in range(windows)]

    w_qry = w_s[0].astype(BF16)
    w_key = w_s[1].astype(BF16)
    w_val = w_s[2].astype(BF16)
    w_out = w_s[3].T.astype(BF16)
    for dst, x in ((q_s, mm(w_qry, normed_s[...], NT)), (d_s, mm(w_out, c_ref[...], NT))):
        for w, block in enumerate(apart(x)):
            dst[:, w * dim:(w + 1) * dim, :] = block
    for w in range(windows):
        nw = normed_s[w * tokens:(w + 1) * tokens]
        k_s[:, w * dim:(w + 1) * dim, :] = mm(w_key, nw, NT).astype(BF16).reshape(heads, dim, tokens)
        v_s[:, w * dim:(w + 1) * dim, :] = mm(w_val, nw, NT).astype(BF16).reshape(heads, dim, tokens)
    query = lax.broadcasted_iota(jnp.int32, (tokens, tokens * windows), 1) % tokens
    pick_s[...] = (query == lax.broadcasted_iota(jnp.int32, query.shape, 0)).astype(F32).astype(BF16)
    dsum_s[...] = jnp.zeros_like(dsum_s)
    fold_s[...] = jnp.zeros_like(fold_s)

    def own(x):
        out = x[:dim]
        for w in range(1, windows):
            out = jnp.where(window == w, x[w * dim:(w + 1) * dim], out)
        return out

    def head(h, carry):
        qh, dh, kh, vh = q_s[h], d_s[h], k_s[h], v_s[h]
        score = mm(kh, qh, TN) * (scale * LOG2E) + jnp.concatenate([bias_ref[h]] * windows, axis=1)
        d_prob = mm(vh, dh, TN)
        expo = jnp.exp2(score - jnp.max(score, axis=0, keepdims=True))
        prob = expo * (1.0 / jnp.sum(expo, axis=0, keepdims=True))
        low = prob.astype(BF16)
        ctx = own(mm(vh, low, NN))
        ctx_s[h] = ctx.astype(BF16)
        dv_s[h] = mm(dh, low, NT).astype(BF16)
        d_ctx = dh[:dim].astype(F32)
        for w in range(1, windows):
            d_ctx = d_ctx + dh[w * dim:(w + 1) * dim].astype(F32)
        inner = jnp.sum(ctx * d_ctx, axis=0, keepdims=True)
        d_low = (prob * (d_prob - inner)).astype(BF16)
        dq_s[h] = (own(mm(kh, d_low, NN)) * scale).astype(BF16)
        both = mm(jnp.concatenate([qh, pick_s[...]], axis=0), d_low, NT)
        dk_s[h] = (both[:windows * dim] * scale).astype(BF16)
        dsum_s[:, :tokens] = both[windows * dim:]
        folded = jnp.zeros((cell, lanes), F32)
        for p in range(lon_width):
            off = (lon_width - 1 - p) * cell
            piece = dsum_s[p * cell:(p + 1) * cell, :]
            folded = folded + (pltpu.roll(piece, off, 1) if off else piece)
        for g in range(tiles):
            fold_s[g, pl.ds(h, cell, stride=slots), :] = folded[:, g * 128:(g + 1) * 128]
        return carry

    if UNROLL:
        lax.fori_loop(0, heads, head, 0, unroll=UNROLL)

    def by_window(ref, w):
        return ref[:, w * dim:(w + 1) * dim, :].reshape(feat, tokens)

    gw_s[0] = mm(dq_s[...].reshape(feat, windows * tokens), normed_s[...], NN)
    gw_s[3] = mm(ctx_s[...].reshape(feat, windows * tokens), c_ref[...], NN).T
    for i, ref in ((1, dk_s), (2, dv_s)):
        total = jnp.zeros((feat, feat), F32)
        for w in range(windows):
            total = total + mm(by_window(ref, w), normed_s[w * tokens:(w + 1) * tokens], NN)
        gw_s[i] = total
    g_gain = jnp.zeros((1, feat), F32)
    for i in range(3):
        g_gain = g_gain + jnp.sum(gw_s[i] * w_s[i], axis=0, keepdims=True)
    g_gain = g_gain / gain_ref[...]

    fold = jnp.concatenate([fold_s[g] for g in range(tiles)], axis=1).astype(BF16)
    back = mm(fold, order_ref[...], NT)
    width = lat_rows * rels
    half = back.shape[1] // levels
    per = 2 * pairs // (levels * levels)
    run = lat_rows // per
    wide = -(-run * width // 128) * 128
    back = back.reshape(levels * per, run, slots, levels * half)
    full = []
    for w in range(levels):
        line = jnp.zeros((levels * per * slots, wide), F32)
        for k in range(run):
            piece = back[:, k, :, w * half:(w + 1) * half].reshape(levels * per * slots, half)
            piece = jnp.concatenate([piece, jnp.zeros((levels * per * slots, wide - half), F32)], axis=1)
            line = line + (pltpu.roll(piece, k * width, 1) if k else piece)
        full.append(line)

    lane = lax.broadcasted_iota(jnp.int32, (8, feat), 1) % 128
    row = lax.broadcasted_iota(jnp.int32, (8, feat), 0)
    gains = jnp.zeros((8, feat), F32)
    for i in range(4):
        turned = jnp.concatenate(
            [pltpu.roll(g_gain[:, g * 128:(g + 1) * 128], (160 - 32 * i) % 128, 1) for g in range(feat // 128)], axis=1
        )
        gains = jnp.where((row == 4 + i) & (lane >= 32) & (lane < 64), turned, gains)

    for j in range(2 * pairs):
        z, w, a = j // (levels * per), j // per % levels, j % per
        at = (z * per + a) * slots
        line = full[w][at:at + slots]
        tail = line[:, feat:]
        moved = jnp.concatenate([pltpu.roll(tail[:8], 4, 0), tail[:8], pltpu.roll(tail[8:], 4, 0)], axis=1)
        moved = jnp.where(lane < 32, moved, gains)
        lines_s[j] = jnp.concatenate([line[:8, :feat], jnp.where(row >= 4, moved, line[8:, :feat])], axis=0).astype(BF16)
    for ref, side in ((same_ref, parity), (other_ref, 1 - parity)):
        for i in range(pairs):
            start = pl.multiple_of((2 * i + side) * part, part)
            block = jnp.concatenate([gw_s[k, pl.ds(start, part), :] for k in range(4)], axis=0)
            ref[i, 0:packed, :] = block.astype(BF16)
            ref[i, packed:, :] = lines_s[2 * i + side]


def run_block(me, x, c, gain, w_same, w_other, bias, order, heads, windows, levels, lat_rows, rels):
    rows, feat = x.shape
    tokens = rows // windows
    dim = feat // heads
    cell = levels * lat_rows
    tiles = order.shape[1] // 128
    slots = heads + -heads % 16
    pairs, packed, _ = w_same.shape
    vmem = pl.BlockSpec(memory_space=pltpu.VMEM)
    sent = jax.ShapeDtypeStruct((pairs, packed + slots, feat), BF16)
    aligned = jax.ShapeDtypeStruct((heads, windows * dim, tokens), BF16)
    return pl.pallas_call(
        functools.partial(block_kernel, heads=heads, windows=windows, levels=levels, lat_rows=lat_rows, rels=rels),
        out_shape=(sent, sent, jax.ShapeDtypeStruct((heads, dim, rows), BF16), aligned, aligned),
        in_specs=[pl.BlockSpec(memory_space=pltpu.SMEM)] + [vmem] * 7,
        out_specs=[vmem] * 5,
        scratch_shapes=[
            pltpu.VMEM((4, feat, feat), F32),
            pltpu.VMEM((4, feat, feat), F32),
            pltpu.VMEM((rows, feat), BF16),
            pltpu.VMEM((heads, windows * dim, rows), BF16),
            pltpu.VMEM((heads, windows * dim, rows), BF16),
            pltpu.VMEM((heads, windows * dim, tokens), BF16),
            pltpu.VMEM((heads, windows * dim, tokens), BF16),
            pltpu.VMEM((heads, dim, rows), BF16),
            pltpu.VMEM((tokens, tiles * 128), F32),
            pltpu.VMEM((tiles, cell * slots, 128), F32),
            pltpu.VMEM((tokens, rows), BF16),
            pltpu.VMEM((2 * pairs, slots, feat), BF16),
        ],
        compiler_params=pltpu.CompilerParams(vmem_limit_bytes=BLOCK_MB * 2**20),
        name="window_block",
    )(me, x, c, gain, w_same, w_other, bias, order)


def input_kernel(me_ref, x_ref, gain_ref, w_same_ref, w_other_ref, dq_ref, dk_ref, dv_ref, din_ref, w_s):
    heads, stacked, tokens = dk_ref.shape
    rows, feat = x_ref.shape
    windows = rows // tokens
    dim = stacked // windows
    load_weights(w_s, w_same_ref, w_other_ref, me_ref[0] % 2)
    std, inv = normalise(x_ref)
    gain = gain_ref[...]
    w_qry, w_key, w_val = (w_s[i].astype(BF16) for i in range(3))
    from_q = mm(dq_ref[...].reshape(feat, rows), w_qry, TN)
    for w in range(windows):
        at = slice(w * tokens, (w + 1) * tokens)
        d_normed = from_q[at]
        for ref, weight in ((dk_ref, w_key), (dv_ref, w_val)):
            d_normed = d_normed + mm(ref[:, w * dim:(w + 1) * dim, :].reshape(feat, tokens), weight, TN)
        g = d_normed * gain
        d_in = inv[at] * (
            g - jnp.mean(g, axis=1, keepdims=True) - std[at] * jnp.mean(g * std[at], axis=1, keepdims=True)
        )
        din_ref[at] = d_in.astype(BF16)


def input_gradient(me, x, gain, w_same, w_other, dq, dk, dv):
    feat = x.shape[1]
    vmem = pl.BlockSpec(memory_space=pltpu.VMEM)
    return pl.pallas_call(
        input_kernel,
        out_shape=jax.ShapeDtypeStruct(x.shape, BF16),
        in_specs=[pl.BlockSpec(memory_space=pltpu.SMEM)] + [vmem] * 7,
        out_specs=vmem,
        scratch_shapes=[pltpu.VMEM((3, feat, feat), F32)],
        compiler_params=pltpu.CompilerParams(vmem_limit_bytes=SMALL_MB * 2**20),
        name="input_gradient",
    )(me, x, gain, w_same, w_other, dq, dk, dv)


def sum_kernel(x_ref, out_ref, table_ref, *, packed):
    pieces, rows, feat = x_ref.shape
    total = x_ref[0].astype(F32)
    for i in range(1, pieces):
        total = total + x_ref[i].astype(F32)
    turned = total[:packed].T
    blocks = out_ref.shape[0]
    part = feat // blocks
    lane = lax.broadcasted_iota(jnp.int32, (1, feat), 1) % 128
    gain = jnp.zeros((1, feat), F32)
    for i in range(4):
        line = total[rows - 4 + i:rows - 3 + i]
        moved = jnp.concatenate(
            [pltpu.roll(line[:, g * 128:(g + 1) * 128], (32 * i - 32) % 128, 1) for g in range(feat // 128)], axis=1
        )
        gain = jnp.where((lane >= 32 * i) & (lane < 32 * i + 32), moved, gain)
    high = gain.astype(BF16).astype(F32)
    gains = jnp.concatenate(
        [src[:, k * packed:(k + 1) * packed] for src in (high, gain - high) for k in range(feat // packed)], axis=0
    )
    for i in range(blocks):
        out_ref[i] = jnp.concatenate([turned[i * part:(i + 1) * part], gains], axis=0).astype(BF16)
    table_ref[...] = total[packed:]


def sum_and_turn(x, blocks, packed):
    pieces, rows, feat = x.shape
    vmem = pl.BlockSpec(memory_space=pltpu.VMEM)
    return pl.pallas_call(
        functools.partial(sum_kernel, packed=packed),
        out_shape=(
            jax.ShapeDtypeStruct((blocks, feat // blocks + 2 * (feat // packed), packed), BF16),
            jax.ShapeDtypeStruct((rows - packed, feat), F32),
        ),
        in_specs=[vmem],
        out_specs=[vmem, vmem],
        compiler_params=pltpu.CompilerParams(vmem_limit_bytes=SMALL_MB * 2**20),
        name="sum_and_turn",
    )(x)


def last_kernel(x_ref, query_ref, key_ref, value_ref, out_ref, gain_ref):
    total = x_ref[0].astype(F32)
    for i in range(1, x_ref.shape[0]):
        total = total + x_ref[i].astype(F32)
    part = query_ref.shape[0]
    for i, ref in enumerate((query_ref, key_ref, value_ref, out_ref)):
        ref[...] = total[:part, i * part:(i + 1) * part]
    count = (total.shape[0] - part) // 2
    gain = total[part:part + count] + total[part + count:]
    gain_ref[...] = jnp.concatenate([gain[k:k + 1] for k in range(count)], axis=1).reshape(gain_ref.shape)


def last_sum(x, part, feat):
    vmem = pl.BlockSpec(memory_space=pltpu.VMEM)
    block = jax.ShapeDtypeStruct((part, part), F32)
    return pl.pallas_call(
        last_kernel,
        out_shape=(block, block, block, block, jax.ShapeDtypeStruct((feat,), F32)),
        in_specs=[vmem],
        out_specs=[vmem] * 5,
        compiler_params=pltpu.CompilerParams(vmem_limit_bytes=SMALL_MB * 2**20),
        name="last_sum",
    )(x)


def swap(x, axis, bit):
    n = lax.axis_size(axis)
    return lax.ppermute(x, axis, [(i, i ^ bit) for i in range(n)])


def shift(x, lat_by, lon_by):
    lats, lons = lax.axis_size("lat"), lax.axis_size("lon")
    if lon_by == 0:
        return lax.ppermute(x, "lat", [(i, (i + lat_by) % lats) for i in range(lats)])
    if lat_by == 0:
        return lax.ppermute(x, "lon", [(i, (i + lon_by) % lons) for i in range(lons)])
    pairs = [
        (a * lons + b, (a + lat_by) % lats * lons + (b + lon_by) % lons)
        for a in range(lats)
        for b in range(lons)
    ]
    return lax.ppermute(x, ("lat", "lon"), pairs)


def spread_over_lat(x):
    return lax.all_to_all(x, "lat", 0, 0)


def spread_over_lon(x):
    n = lax.axis_size("lon")
    groups = [list(range(c, n, 2)) for c in range(2)]
    return lax.all_to_all(x, "lon", 0, 0, axis_index_groups=groups)


def local(fields, cotangent, norm_gain, w_query, w_key, w_value, w_out, rel_table):
    levels, lat_rows, lon_cols, feat = fields.shape
    heads = rel_table.shape[1]
    rels = rel_table.shape[2] // (levels * levels * lat_rows * lat_rows)
    lon_width = (rels + 1) // 2
    half_rows = lat_rows // 2
    half_cols = lon_width // 2
    windows = lon_cols // lon_width
    lats = lax.axis_size("lat")
    lons = lax.axis_size("lon")
    me_lat = lax.axis_index("lat")
    me_lon = lax.axis_index("lon")
    part = w_query.shape[0]

    both = jnp.stack([fields, cotangent]).transpose(3, 0, 1, 2, 4)

    mine = jnp.concatenate([w_query, w_key, w_value, w_out], axis=1)
    rows_all = spread_over_lat(jnp.broadcast_to(mine[None], (lats,) + mine.shape))
    turned = turn(rows_all, lons // 2)
    turned, table = lax.optimization_barrier((turned, rel_table[0]))
    w_same = spread_over_lon(turned)
    own = both[half_cols:, :, :, half_rows:]
    south = shift(both[half_cols:, :, :, :half_rows], -1, 0)
    east = shift(both[:half_cols, :, :, half_rows:], 0, -1)
    corner = shift(both[:half_cols, :, :, :half_rows], -1, -1)

    order = jnp.asarray(offset_order(rels, levels, lat_rows, 256), BF16)
    last = (me_lat == lats - 1).astype(jnp.int32).reshape(1)
    slots = heads + -heads % 16
    bias = make_bias(last, table, order, levels, lat_rows, rels, slots, windows)
    w_same, bias, own, south, east, corner = lax.optimization_barrier((w_same, bias, own, south, east, corner))
    w_other = swap(w_same, "lon", 1)
    moved = jnp.concatenate(
        [jnp.concatenate([own, south], axis=3), jnp.concatenate([east, corner], axis=3)], axis=0
    )
    shifted = moved[:, 0].reshape(-1, feat)
    cot_shift = moved[:, 1].reshape(-1, feat)

    me = me_lon.reshape(1)
    gain = norm_gain[None]
    g_same, g_other, dq, dk, dv = run_block(
        me, shifted, cot_shift, gain, w_same, w_other, bias, order, heads, windows, levels, lat_rows, rels
    )

    paired = (g_same.astype(F32) + swap(g_other, "lon", 1).astype(F32)).astype(BF16)
    paired, dq, dk, dv = lax.optimization_barrier((paired, dq, dk, dv))
    arrived = spread_over_lon(paired)
    message, lines = sum_and_turn(arrived, lats, 4 * part)
    grad_query, grad_key, grad_value, grad_out, grad_gain = last_sum(spread_over_lat(message), part, feat)
    d_input = input_gradient(me, shifted, gain, w_same, w_other, dq, dk, dv)

    d_in = d_input.reshape(lon_cols, levels, lat_rows, feat)
    stay = lon_cols - half_cols
    west = shift(d_in[stay:, :, :half_rows], 0, 1)
    north = shift(d_in[:stay, :, half_rows:], 1, 0)
    corner = shift(d_in[stay:, :, half_rows:], 1, 1)
    west, north, corner, d_in, lines, _ = lax.optimization_barrier((west, north, corner, d_in, lines, message))
    over = rel_table.shape[2] // lons - feat
    groups = feat // 128
    tail = lines[heads:].reshape(slots - heads, groups, 128)[:, :, :over].transpose(1, 0, 2)
    grad_table = jnp.concatenate([lines[:heads], tail.reshape(heads, over)], axis=1)[None]
    back = jnp.concatenate(
        [jnp.concatenate([corner, west], axis=2), jnp.concatenate([north, d_in[:stay, :, :half_rows]], axis=2)],
        axis=0,
    ).transpose(1, 2, 0, 3)
    grad_fields = (cotangent.astype(F32) + back.astype(F32)).astype(BF16)
    return (grad_fields, grad_query, grad_key, grad_value, grad_out, grad_table, grad_gain)


def solution(mesh):
    return jax.shard_map(
        local,
        mesh=mesh,
        in_specs=(
            P(None, "lat", "lon", None),
            P(None, "lat", "lon", None),
            P(),
            P("lat", "lon"),
            P("lat", "lon"),
            P("lat", "lon"),
            P("lat", "lon"),
            P("lat", None, None),
        ),
        out_specs=(
            P(None, "lat", "lon", None),
            P("lat", "lon"),
            P("lat", "lon"),
            P("lat", "lon"),
            P("lat", "lon"),
            P("lat", None, "lon"),
            P(),
        ),
        check_vma=False,
    )
```

```python
import functools
import math

import jax
import jax.numpy as jnp
import numpy as np
from jax import lax
from jax.experimental import pallas as pl
from jax.experimental.pallas import tpu as pltpu
from jax.sharding import PartitionSpec as P

EPSILON = 1e-05
MASKED = -1000000000.0
LOG2E = math.log2(math.e)
BLOCK_MB = 48
SMALL_MB = 16
F32 = jnp.float32
BF16 = jnp.bfloat16
NN = (((1,), (0,)), ((), ()))
NT = (((1,), (1,)), ((), ()))
TN = (((0,), (0,)), ((), ()))


def mm(a, b, dims):
    return lax.dot_general(a, b, dims, preferred_element_type=F32)


def offset_order(rels, levels, lat_rows, group):
    lanes = rels * levels * lat_rows
    order = np.zeros((levels * group, lanes + -lanes % 128), np.float32)
    for level in range(levels):
        for lat in range(lat_rows):
            for rel in range(rels):
                order[level * group + lat * rels + rel, ((rels - 1 - rel) * levels + level) * lat_rows + lat] = 1.0
    return order


def bias_kernel(last_ref, table_ref, order_ref, out_ref, table_s, strips_s, bias_s, *, levels, lat_rows, rels, windows):
    heads = table_ref.shape[0]
    slots = table_s.shape[1]
    cell = levels * lat_rows
    width = lat_rows * rels
    group = table_s.shape[2] // levels
    tiles = strips_s.shape[0]
    lanes = tiles * 128
    lon_width = (rels + 1) // 2
    tokens = lon_width * cell
    table_s[...] = jnp.zeros_like(table_s)
    table = table_ref[...]
    for z in range(levels):
        for w in range(levels):
            for a in range(lat_rows):
                at = ((z * levels + w) * lat_rows + a) * width
                table_s[z * lat_rows + a, 0:heads, w * group:w * group + width] = table[:, at:at + width]
    full = table_s[...].reshape(cell * slots, levels * group)
    order = order_ref[...]
    high = full.astype(BF16)
    rest = full - high.astype(F32)
    mid = rest.astype(BF16)
    low = (rest - mid.astype(F32)).astype(BF16)
    strips = mm(high, order, NN) + mm(mid, order, NN) + mm(low, order, NN)
    row = lax.broadcasted_iota(jnp.int32, (cell * slots, 1), 0) // slots
    lane = lax.broadcasted_iota(jnp.int32, (1, lanes), 1)
    row_north = (row % lat_rows < lat_rows // 2).astype(F32)
    lane_north = (lane % lat_rows < lat_rows // 2).astype(F32)
    crossing = (row_north != lane_north) & (last_ref[0] != 0)
    strips = jnp.where(crossing, MASKED, strips) * LOG2E
    for g in range(tiles):
        strips_s[g, 0:cell * slots, :] = strips[:, g * 128:(g + 1) * 128]

    def head(h, carry):
        strip = jnp.concatenate([strips_s[g, pl.ds(h, cell, stride=slots), :] for g in range(tiles)], axis=1)
        for p in range(lon_width):
            off = (lon_width - 1 - p) * cell
            rolled = pltpu.roll(strip, lanes - off, 1) if off else strip
            bias_s[p * cell:(p + 1) * cell, :] = rolled[:, :tokens]
        out_ref[h] = bias_s[...].T
        return carry

    lax.fori_loop(0, heads, head, 0)


def make_bias(last, table, order, levels, lat_rows, rels, slots, windows):
    heads = table.shape[0]
    cell = levels * lat_rows
    tokens = (rels + 1) // 2 * cell
    tiles = order.shape[1] // 128
    vmem = pl.BlockSpec(memory_space=pltpu.VMEM)
    return pl.pallas_call(
        functools.partial(bias_kernel, levels=levels, lat_rows=lat_rows, rels=rels, windows=windows),
        out_shape=jax.ShapeDtypeStruct((heads, tokens, tokens), F32),
        in_specs=[pl.BlockSpec(memory_space=pltpu.SMEM), vmem, vmem],
        out_specs=vmem,
        scratch_shapes=[
            pltpu.VMEM((cell, slots, order.shape[0]), F32),
            pltpu.VMEM((tiles, (cell + 1) * slots, 128), F32),
            pltpu.VMEM((tokens, tokens), F32),
        ],
        compiler_params=pltpu.CompilerParams(vmem_limit_bytes=SMALL_MB * 2**20),
        name="make_bias",
    )(last, table, order)


def turn_kernel(x_ref, out_ref):
    blocks, rows, lanes = x_ref.shape
    turned = x_ref[...].astype(F32).reshape(blocks * rows, lanes).T.astype(BF16)
    for i in range(out_ref.shape[0]):
        out_ref[i] = turned


def turn(x, copies):
    blocks, rows, lanes = x.shape
    vmem = pl.BlockSpec(memory_space=pltpu.VMEM)
    return pl.pallas_call(
        turn_kernel,
        out_shape=jax.ShapeDtypeStruct((copies, lanes, blocks * rows), BF16),
        in_specs=[vmem],
        out_specs=vmem,
        compiler_params=pltpu.CompilerParams(vmem_limit_bytes=SMALL_MB * 2**20),
        name="turn_weights",
    )(x)


def load_weights(w_s, w_same_ref, w_other_ref, parity):
    pairs, packed, _ = w_same_ref.shape
    part = packed // 4
    for ref, side in ((w_same_ref, parity), (w_other_ref, 1 - parity)):
        for i in range(pairs):
            block = ref[i].astype(F32)
            start = pl.multiple_of((2 * i + side) * part, part)
            for k in range(w_s.shape[0]):
                w_s[k, pl.ds(start, part), :] = block[k * part:(k + 1) * part]


def normalise(x_ref):
    xf = x_ref[...].astype(F32)
    mean = jnp.mean(xf, axis=1, keepdims=True)
    centred = xf - mean
    var = jnp.mean(centred * centred, axis=1, keepdims=True)
    inv = 1.0 / jnp.sqrt(var + EPSILON)
    return centred * inv, inv


def block_kernel(
    me_ref, x_ref, c_ref, gain_ref, w_same_ref, w_other_ref, bias_ref, order_ref,
    same_ref, other_ref, dq_s, dk_s, dv_s,
    w_s, gw_s, normed_s, q_s, d_s, k_s, v_s, ctx_s, dsum_s, fold_s, pick_s, lines_s,
    *, heads, windows, levels, lat_rows, rels,
):
    feat = x_ref.shape[1]
    dim = feat // heads
    lon_width = (rels + 1) // 2
    cell = levels * lat_rows
    tokens = lon_width * cell
    scale = 1.0 / math.sqrt(dim)
    tiles = fold_s.shape[0]
    lanes = tiles * 128
    slots = fold_s.shape[1] // (cell + 1)
    pairs, packed, _ = w_same_ref.shape
    part = packed // 4
    parity = me_ref[0] % 2

    load_weights(w_s, w_same_ref, w_other_ref, parity)
    std, _ = normalise(x_ref)
    normed_s[...] = (std * gain_ref[...]).astype(BF16)
    window = lax.broadcasted_iota(jnp.int32, (dim, windows * tokens), 1) // tokens

    def apart(x):
        x = x.astype(BF16).reshape(heads, dim, windows * tokens)
        return [jnp.where((window == w)[None], x, jnp.zeros_like(x)) for w in range(windows)]

    w_qry = w_s[0].astype(BF16)
    w_key = w_s[1].astype(BF16)
    w_val = w_s[2].astype(BF16)
    w_out = w_s[3].T.astype(BF16)
    for dst, x in ((q_s, mm(w_qry, normed_s[...], NT)), (d_s, mm(w_out, c_ref[...], NT))):
        for w, block in enumerate(apart(x)):
            dst[:, w * dim:(w + 1) * dim, :] = block
    for w in range(windows):
        nw = normed_s[w * tokens:(w + 1) * tokens]
        k_s[:, w * dim:(w + 1) * dim, :] = mm(w_key, nw, NT).astype(BF16).reshape(heads, dim, tokens)
        v_s[:, w * dim:(w + 1) * dim, :] = mm(w_val, nw, NT).astype(BF16).reshape(heads, dim, tokens)
    query = lax.broadcasted_iota(jnp.int32, (tokens, tokens * windows), 1) % tokens
    pick_s[...] = (query == lax.broadcasted_iota(jnp.int32, query.shape, 0)).astype(F32).astype(BF16)
    dsum_s[...] = jnp.zeros_like(dsum_s)
    fold_s[...] = jnp.zeros_like(fold_s)

    def own(x):
        out = x[:dim]
        for w in range(1, windows):
            out = jnp.where(window == w, x[w * dim:(w + 1) * dim], out)
        return out

    def head(h, carry):
        qh, dh, kh, vh = q_s[h], d_s[h], k_s[h], v_s[h]
        score = mm(kh, qh, TN) * (scale * LOG2E) + jnp.concatenate([bias_ref[h]] * windows, axis=1)
        d_prob = mm(vh, dh, TN)
        expo = jnp.exp2(score - jnp.max(score, axis=0, keepdims=True))
        prob = expo * (1.0 / jnp.sum(expo, axis=0, keepdims=True))
        low = prob.astype(BF16)
        ctx = own(mm(vh, low, NN))
        ctx_s[h] = ctx.astype(BF16)
        dv_s[h] = mm(dh, low, NT).astype(BF16)
        d_ctx = dh[:dim].astype(F32)
        for w in range(1, windows):
            d_ctx = d_ctx + dh[w * dim:(w + 1) * dim].astype(F32)
        inner = jnp.sum(ctx * d_ctx, axis=0, keepdims=True)
        d_low = (prob * (d_prob - inner)).astype(BF16)
        dq_s[h] = (own(mm(kh, d_low, NN)) * scale).astype(BF16)
        both = mm(jnp.concatenate([qh, pick_s[...]], axis=0), d_low, NT)
        dk_s[h] = (both[:windows * dim] * scale).astype(BF16)
        dsum_s[:, :tokens] = both[windows * dim:]
        folded = jnp.zeros((cell, lanes), F32)
        for p in range(lon_width):
            off = (lon_width - 1 - p) * cell
            piece = dsum_s[p * cell:(p + 1) * cell, :]
            folded = folded + (pltpu.roll(piece, off, 1) if off else piece)
        for g in range(tiles):
            fold_s[g, pl.ds(h, cell, stride=slots), :] = folded[:, g * 128:(g + 1) * 128]
        return carry

    lax.fori_loop(0, heads, head, 0, unroll=True)

    def by_window(ref, w):
        return ref[:, w * dim:(w + 1) * dim, :].reshape(feat, tokens)

    gw_s[0] = mm(dq_s[...].reshape(feat, windows * tokens), normed_s[...], NN)
    gw_s[3] = mm(ctx_s[...].reshape(feat, windows * tokens), c_ref[...], NN).T
    for i, ref in ((1, dk_s), (2, dv_s)):
        total = jnp.zeros((feat, feat), F32)
        for w in range(windows):
            total = total + mm(by_window(ref, w), normed_s[w * tokens:(w + 1) * tokens], NN)
        gw_s[i] = total
    g_gain = jnp.zeros((1, feat), F32)
    for i in range(3):
        g_gain = g_gain + jnp.sum(gw_s[i] * w_s[i], axis=0, keepdims=True)
    g_gain = g_gain / gain_ref[...]

    fold = jnp.concatenate([fold_s[g, 0:cell * slots, :] for g in range(tiles)], axis=1).astype(BF16)
    back = mm(fold, order_ref[...], NT)
    width = lat_rows * rels
    half = back.shape[1] // levels
    per = 2 * pairs // (levels * levels)
    run = lat_rows // per
    wide = -(-run * width // 128) * 128
    back = back.reshape(levels * per, run, slots, levels * half)
    full = []
    for w in range(levels):
        line = jnp.zeros((levels * per * slots, wide), F32)
        for k in range(run):
            piece = back[:, k, :, w * half:(w + 1) * half].reshape(levels * per * slots, half)
            piece = jnp.concatenate([piece, jnp.zeros((levels * per * slots, wide - half), F32)], axis=1)
            line = line + (pltpu.roll(piece, k * width, 1) if k else piece)
        full.append(line)

    lane = lax.broadcasted_iota(jnp.int32, (8, feat), 1) % 128
    row = lax.broadcasted_iota(jnp.int32, (8, feat), 0)
    gains = jnp.zeros((8, feat), F32)
    for i in range(4):
        turned = jnp.concatenate(
            [pltpu.roll(g_gain[:, g * 128:(g + 1) * 128], (160 - 32 * i) % 128, 1) for g in range(feat // 128)], axis=1
        )
        gains = jnp.where((row == 4 + i) & (lane >= 32) & (lane < 64), turned, gains)

    for j in range(2 * pairs):
        z, w, a = j // (levels * per), j // per % levels, j % per
        at = (z * per + a) * slots
        line = full[w][at:at + slots]
        tail = line[:, feat:]
        moved = jnp.concatenate([pltpu.roll(tail[:8], 4, 0), tail[:8], pltpu.roll(tail[8:], 4, 0)], axis=1)
        moved = jnp.where(lane < 32, moved, gains)
        lines_s[j] = jnp.concatenate([line[:8, :feat], jnp.where(row >= 4, moved, line[8:, :feat])], axis=0).astype(BF16)
    for ref, side in ((same_ref, parity), (other_ref, 1 - parity)):
        for i in range(pairs):
            start = pl.multiple_of((2 * i + side) * part, part)
            block = jnp.concatenate([gw_s[k, pl.ds(start, part), :] for k in range(4)], axis=0)
            ref[i, 0:packed, :] = block.astype(BF16)
            ref[i, packed:, :] = lines_s[2 * i + side]


def run_block(me, x, c, gain, w_same, w_other, bias, order, heads, windows, levels, lat_rows, rels):
    rows, feat = x.shape
    tokens = rows // windows
    dim = feat // heads
    cell = levels * lat_rows
    tiles = order.shape[1] // 128
    slots = heads + -heads % 16
    pairs, packed, _ = w_same.shape
    vmem = pl.BlockSpec(memory_space=pltpu.VMEM)
    sent = jax.ShapeDtypeStruct((pairs, packed + slots, feat), BF16)
    aligned = jax.ShapeDtypeStruct((heads, windows * dim, tokens), BF16)
    return pl.pallas_call(
        functools.partial(block_kernel, heads=heads, windows=windows, levels=levels, lat_rows=lat_rows, rels=rels),
        out_shape=(sent, sent, jax.ShapeDtypeStruct((heads, dim, rows), BF16), aligned, aligned),
        in_specs=[pl.BlockSpec(memory_space=pltpu.SMEM)] + [vmem] * 7,
        out_specs=[vmem] * 5,
        scratch_shapes=[
            pltpu.VMEM((4, feat, feat), F32),
            pltpu.VMEM((4, feat, feat), F32),
            pltpu.VMEM((rows, feat), BF16),
            pltpu.VMEM((heads, windows * dim, rows), BF16),
            pltpu.VMEM((heads, windows * dim, rows), BF16),
            pltpu.VMEM((heads, windows * dim, tokens), BF16),
            pltpu.VMEM((heads, windows * dim, tokens), BF16),
            pltpu.VMEM((heads, dim, rows), BF16),
            pltpu.VMEM((tokens, tiles * 128), F32),
            pltpu.VMEM((tiles, (cell + 1) * slots, 128), F32),
            pltpu.VMEM((tokens, rows), BF16),
            pltpu.VMEM((2 * pairs, slots, feat), BF16),
        ],
        compiler_params=pltpu.CompilerParams(vmem_limit_bytes=BLOCK_MB * 2**20),
        name="window_block",
    )(me, x, c, gain, w_same, w_other, bias, order)


def input_kernel(me_ref, x_ref, gain_ref, w_same_ref, w_other_ref, dq_ref, dk_ref, dv_ref, din_ref, w_s):
    heads, stacked, tokens = dk_ref.shape
    rows, feat = x_ref.shape
    windows = rows // tokens
    dim = stacked // windows
    load_weights(w_s, w_same_ref, w_other_ref, me_ref[0] % 2)
    std, inv = normalise(x_ref)
    gain = gain_ref[...]
    w_qry, w_key, w_val = (w_s[i].astype(BF16) for i in range(3))
    from_q = mm(dq_ref[...].reshape(feat, rows), w_qry, TN)
    for w in range(windows):
        at = slice(w * tokens, (w + 1) * tokens)
        d_normed = from_q[at]
        for ref, weight in ((dk_ref, w_key), (dv_ref, w_val)):
            d_normed = d_normed + mm(ref[:, w * dim:(w + 1) * dim, :].reshape(feat, tokens), weight, TN)
        g = d_normed * gain
        d_in = inv[at] * (
            g - jnp.mean(g, axis=1, keepdims=True) - std[at] * jnp.mean(g * std[at], axis=1, keepdims=True)
        )
        din_ref[at] = d_in.astype(BF16)


def input_gradient(me, x, gain, w_same, w_other, dq, dk, dv):
    feat = x.shape[1]
    vmem = pl.BlockSpec(memory_space=pltpu.VMEM)
    return pl.pallas_call(
        input_kernel,
        out_shape=jax.ShapeDtypeStruct(x.shape, BF16),
        in_specs=[pl.BlockSpec(memory_space=pltpu.SMEM)] + [vmem] * 7,
        out_specs=vmem,
        scratch_shapes=[pltpu.VMEM((3, feat, feat), F32)],
        compiler_params=pltpu.CompilerParams(vmem_limit_bytes=SMALL_MB * 2**20),
        name="input_gradient",
    )(me, x, gain, w_same, w_other, dq, dk, dv)


def sum_kernel(x_ref, out_ref, table_ref, *, packed):
    pieces, rows, feat = x_ref.shape
    total = x_ref[0].astype(F32)
    for i in range(1, pieces):
        total = total + x_ref[i].astype(F32)
    turned = total[:packed].T
    blocks = out_ref.shape[0]
    part = feat // blocks
    lane = lax.broadcasted_iota(jnp.int32, (1, feat), 1) % 128
    gain = jnp.zeros((1, feat), F32)
    for i in range(4):
        line = total[rows - 4 + i:rows - 3 + i]
        moved = jnp.concatenate(
            [pltpu.roll(line[:, g * 128:(g + 1) * 128], (32 * i - 32) % 128, 1) for g in range(feat // 128)], axis=1
        )
        gain = jnp.where((lane >= 32 * i) & (lane < 32 * i + 32), moved, gain)
    high = gain.astype(BF16).astype(F32)
    gains = jnp.concatenate(
        [src[:, k * packed:(k + 1) * packed] for src in (high, gain - high) for k in range(feat // packed)], axis=0
    )
    for i in range(blocks):
        out_ref[i] = jnp.concatenate([turned[i * part:(i + 1) * part], gains], axis=0).astype(BF16)
    table_ref[...] = total[packed:]


def sum_and_turn(x, blocks, packed):
    pieces, rows, feat = x.shape
    vmem = pl.BlockSpec(memory_space=pltpu.VMEM)
    return pl.pallas_call(
        functools.partial(sum_kernel, packed=packed),
        out_shape=(
            jax.ShapeDtypeStruct((blocks, feat // blocks + 2 * (feat // packed), packed), BF16),
            jax.ShapeDtypeStruct((rows - packed, feat), F32),
        ),
        in_specs=[vmem],
        out_specs=[vmem, vmem],
        compiler_params=pltpu.CompilerParams(vmem_limit_bytes=SMALL_MB * 2**20),
        name="sum_and_turn",
    )(x)


def last_kernel(x_ref, query_ref, key_ref, value_ref, out_ref, gain_ref):
    total = x_ref[0].astype(F32)
    for i in range(1, x_ref.shape[0]):
        total = total + x_ref[i].astype(F32)
    part = query_ref.shape[0]
    for i, ref in enumerate((query_ref, key_ref, value_ref, out_ref)):
        ref[...] = total[:part, i * part:(i + 1) * part]
    count = (total.shape[0] - part) // 2
    gain = total[part:part + count] + total[part + count:]
    gain_ref[...] = jnp.concatenate([gain[k:k + 1] for k in range(count)], axis=1).reshape(gain_ref.shape)


def last_sum(x, part, feat):
    vmem = pl.BlockSpec(memory_space=pltpu.VMEM)
    block = jax.ShapeDtypeStruct((part, part), F32)
    return pl.pallas_call(
        last_kernel,
        out_shape=(block, block, block, block, jax.ShapeDtypeStruct((feat,), F32)),
        in_specs=[vmem],
        out_specs=[vmem] * 5,
        compiler_params=pltpu.CompilerParams(vmem_limit_bytes=SMALL_MB * 2**20),
        name="last_sum",
    )(x)


def swap(x, axis, bit):
    n = lax.axis_size(axis)
    return lax.ppermute(x, axis, [(i, i ^ bit) for i in range(n)])


def shift(x, lat_by, lon_by):
    lats, lons = lax.axis_size("lat"), lax.axis_size("lon")
    if lon_by == 0:
        return lax.ppermute(x, "lat", [(i, (i + lat_by) % lats) for i in range(lats)])
    if lat_by == 0:
        return lax.ppermute(x, "lon", [(i, (i + lon_by) % lons) for i in range(lons)])
    pairs = [
        (a * lons + b, (a + lat_by) % lats * lons + (b + lon_by) % lons)
        for a in range(lats)
        for b in range(lons)
    ]
    return lax.ppermute(x, ("lat", "lon"), pairs)


def spread_over_lat(x):
    return lax.all_to_all(x, "lat", 0, 0)


def spread_over_lon(x):
    n = lax.axis_size("lon")
    groups = [list(range(c, n, 2)) for c in range(2)]
    return lax.all_to_all(x, "lon", 0, 0, axis_index_groups=groups)


def local(fields, cotangent, norm_gain, w_query, w_key, w_value, w_out, rel_table):
    levels, lat_rows, lon_cols, feat = fields.shape
    heads = rel_table.shape[1]
    rels = rel_table.shape[2] // (levels * levels * lat_rows * lat_rows)
    lon_width = (rels + 1) // 2
    half_rows = lat_rows // 2
    half_cols = lon_width // 2
    windows = lon_cols // lon_width
    lats = lax.axis_size("lat")
    lons = lax.axis_size("lon")
    me_lat = lax.axis_index("lat")
    me_lon = lax.axis_index("lon")
    part = w_query.shape[0]

    both = jnp.stack([fields, cotangent]).transpose(3, 0, 1, 2, 4)

    mine = jnp.concatenate([w_query, w_key, w_value, w_out], axis=1)
    rows_all = spread_over_lat(jnp.broadcast_to(mine[None], (lats,) + mine.shape))
    turned = turn(rows_all, lons // 2)
    turned, table = lax.optimization_barrier((turned, rel_table[0]))
    w_same = spread_over_lon(turned)
    own = both[half_cols:, :, :, half_rows:]
    south = shift(both[half_cols:, :, :, :half_rows], -1, 0)
    east = shift(both[:half_cols, :, :, half_rows:], 0, -1)
    corner = shift(both[:half_cols, :, :, :half_rows], -1, -1)

    order = jnp.asarray(offset_order(rels, levels, lat_rows, 256), BF16)
    last = (me_lat == lats - 1).astype(jnp.int32).reshape(1)
    slots = heads + -heads % 16
    bias = make_bias(last, table, order, levels, lat_rows, rels, slots, windows)
    w_same, bias, own, south, east, corner = lax.optimization_barrier((w_same, bias, own, south, east, corner))
    w_other = swap(w_same, "lon", 1)
    moved = jnp.concatenate(
        [jnp.concatenate([own, south], axis=3), jnp.concatenate([east, corner], axis=3)], axis=0
    )
    shifted = moved[:, 0].reshape(-1, feat)
    cot_shift = moved[:, 1].reshape(-1, feat)

    me = me_lon.reshape(1)
    gain = norm_gain[None]
    g_same, g_other, dq, dk, dv = run_block(
        me, shifted, cot_shift, gain, w_same, w_other, bias, order, heads, windows, levels, lat_rows, rels
    )

    paired = (g_same.astype(F32) + swap(g_other, "lon", 1).astype(F32)).astype(BF16)
    paired, dq, dk, dv = lax.optimization_barrier((paired, dq, dk, dv))
    arrived = spread_over_lon(paired)
    message, lines = sum_and_turn(arrived, lats, 4 * part)
    grad_query, grad_key, grad_value, grad_out, grad_gain = last_sum(spread_over_lat(message), part, feat)
    d_input = input_gradient(me, shifted, gain, w_same, w_other, dq, dk, dv)

    d_in = d_input.reshape(lon_cols, levels, lat_rows, feat)
    stay = lon_cols - half_cols
    west = shift(d_in[stay:, :, :half_rows], 0, 1)
    north = shift(d_in[:stay, :, half_rows:], 1, 0)
    corner = shift(d_in[stay:, :, half_rows:], 1, 1)
    west, north, corner, d_in, lines, _ = lax.optimization_barrier((west, north, corner, d_in, lines, message))
    over = rel_table.shape[2] // lons - feat
    groups = feat // 128
    tail = lines[heads:].reshape(slots - heads, groups, 128)[:, :, :over].transpose(1, 0, 2)
    grad_table = jnp.concatenate([lines[:heads], tail.reshape(heads, over)], axis=1)[None]
    back = jnp.concatenate(
        [jnp.concatenate([corner, west], axis=2), jnp.concatenate([north, d_in[:stay, :, :half_rows]], axis=2)],
        axis=0,
    ).transpose(1, 2, 0, 3)
    grad_fields = (cotangent.astype(F32) + back.astype(F32)).astype(BF16)
    return (grad_fields, grad_query, grad_key, grad_value, grad_out, grad_table, grad_gain)


def solution(mesh):
    return jax.shard_map(
        local,
        mesh=mesh,
        in_specs=(
            P(None, "lat", "lon", None),
            P(None, "lat", "lon", None),
            P(),
            P("lat", "lon"),
            P("lat", "lon"),
            P("lat", "lon"),
            P("lat", "lon"),
            P("lat", None, None),
        ),
        out_specs=(
            P(None, "lat", "lon", None),
            P("lat", "lon"),
            P("lat", "lon"),
            P("lat", "lon"),
            P("lat", "lon"),
            P("lat", None, "lon"),
            P(),
        ),
        check_vma=False,
    )
```

```python
import functools
import math

import jax
import jax.numpy as jnp
import numpy as np
from jax import lax
from jax.experimental import pallas as pl
from jax.experimental.pallas import tpu as pltpu
from jax.sharding import PartitionSpec as P

EPSILON = 1e-05
MASKED = -1000000000.0
LOG2E = math.log2(math.e)
BLOCK_MB = 48
SMALL_MB = 16
F32 = jnp.float32
BF16 = jnp.bfloat16
NN = (((1,), (0,)), ((), ()))
NT = (((1,), (1,)), ((), ()))
TN = (((0,), (0,)), ((), ()))


def mm(a, b, dims):
    return lax.dot_general(a, b, dims, preferred_element_type=F32)


def offset_order(rels, levels, lat_rows, group):
    lanes = rels * levels * lat_rows
    order = np.zeros((levels * group, lanes + -lanes % 128), np.float32)
    for level in range(levels):
        for lat in range(lat_rows):
            for rel in range(rels):
                order[level * group + lat * rels + rel, ((rels - 1 - rel) * levels + level) * lat_rows + lat] = 1.0
    return order


def bias_kernel(last_ref, table_ref, order_ref, out_ref, table_s, strips_s, bias_s, *, levels, lat_rows, rels, windows):
    heads = table_ref.shape[0]
    slots = table_s.shape[1]
    cell = levels * lat_rows
    width = lat_rows * rels
    group = table_s.shape[2] // levels
    tiles = strips_s.shape[0]
    lanes = tiles * 128
    lon_width = (rels + 1) // 2
    tokens = lon_width * cell
    table_s[...] = jnp.zeros_like(table_s)
    table = table_ref[...]
    for z in range(levels):
        for w in range(levels):
            for a in range(lat_rows):
                at = ((z * levels + w) * lat_rows + a) * width
                table_s[z * lat_rows + a, 0:heads, w * group:w * group + width] = table[:, at:at + width]
    full = table_s[...].reshape(cell * slots, levels * group)
    order = order_ref[...]
    high = full.astype(BF16)
    rest = full - high.astype(F32)
    mid = rest.astype(BF16)
    low = (rest - mid.astype(F32)).astype(BF16)
    strips = mm(high, order, NN) + mm(mid, order, NN) + mm(low, order, NN)
    row = lax.broadcasted_iota(jnp.int32, (cell * slots, 1), 0) // slots
    lane = lax.broadcasted_iota(jnp.int32, (1, lanes), 1)
    row_north = (row % lat_rows < lat_rows // 2).astype(F32)
    lane_north = (lane % lat_rows < lat_rows // 2).astype(F32)
    crossing = (row_north != lane_north) & (last_ref[0] != 0)
    strips = jnp.where(crossing, MASKED, strips) * LOG2E
    for g in range(tiles):
        strips_s[g, 0:cell * slots, :] = strips[:, g * 128:(g + 1) * 128]

    def head(h, carry):
        strip = jnp.concatenate([strips_s[g, pl.ds(h, cell, stride=slots), :] for g in range(tiles)], axis=1)
        for p in range(lon_width):
            off = (lon_width - 1 - p) * cell
            rolled = pltpu.roll(strip, lanes - off, 1) if off else strip
            bias_s[p * cell:(p + 1) * cell, :] = rolled[:, :tokens]
        out_ref[h] = bias_s[...].T
        return carry

    lax.fori_loop(0, heads, head, 0)


def make_bias(last, table, order, levels, lat_rows, rels, slots, windows):
    heads = table.shape[0]
    cell = levels * lat_rows
    tokens = (rels + 1) // 2 * cell
    tiles = order.shape[1] // 128
    vmem = pl.BlockSpec(memory_space=pltpu.VMEM)
    return pl.pallas_call(
        functools.partial(bias_kernel, levels=levels, lat_rows=lat_rows, rels=rels, windows=windows),
        out_shape=jax.ShapeDtypeStruct((heads, tokens, tokens), F32),
        in_specs=[pl.BlockSpec(memory_space=pltpu.SMEM), vmem, vmem],
        out_specs=vmem,
        scratch_shapes=[
            pltpu.VMEM((cell, slots, order.shape[0]), F32),
            pltpu.VMEM((tiles, (cell + 1) * slots, 128), F32),
            pltpu.VMEM((tokens, tokens), F32),
        ],
        compiler_params=pltpu.CompilerParams(vmem_limit_bytes=SMALL_MB * 2**20),
        name="make_bias",
    )(last, table, order)


def turn_kernel(x_ref, out_ref):
    blocks, rows, lanes = x_ref.shape
    turned = x_ref[...].astype(F32).reshape(blocks * rows, lanes).T.astype(BF16)
    for i in range(out_ref.shape[0]):
        out_ref[i] = turned


def turn(x, copies):
    blocks, rows, lanes = x.shape
    vmem = pl.BlockSpec(memory_space=pltpu.VMEM)
    return pl.pallas_call(
        turn_kernel,
        out_shape=jax.ShapeDtypeStruct((copies, lanes, blocks * rows), BF16),
        in_specs=[vmem],
        out_specs=vmem,
        compiler_params=pltpu.CompilerParams(vmem_limit_bytes=SMALL_MB * 2**20),
        name="turn_weights",
    )(x)


def load_weights(w_s, w_same_ref, w_other_ref, parity):
    pairs, packed, _ = w_same_ref.shape
    part = packed // 4
    for ref, side in ((w_same_ref, parity), (w_other_ref, 1 - parity)):
        for i in range(pairs):
            block = ref[i].astype(F32)
            start = pl.multiple_of((2 * i + side) * part, part)
            for k in range(w_s.shape[0]):
                w_s[k, pl.ds(start, part), :] = block[k * part:(k + 1) * part]


def normalise(x_ref):
    xf = x_ref[...].astype(F32)
    mean = jnp.mean(xf, axis=1, keepdims=True)
    centred = xf - mean
    var = jnp.mean(centred * centred, axis=1, keepdims=True)
    inv = 1.0 / jnp.sqrt(var + EPSILON)
    return centred * inv, inv


def block_kernel(
    me_ref, x_ref, c_ref, gain_ref, w_same_ref, w_other_ref, bias_ref, order_ref,
    same_ref, other_ref, dq_s, dk_s, dv_s,
    w_s, gw_s, normed_s, q_s, d_s, k_s, v_s, ctx_s, dsum_s, fold_s, pick_s, lines_s, bias_s, bias_sem,
    *, heads, windows, levels, lat_rows, rels,
):
    feat = x_ref.shape[1]
    dim = feat // heads
    lon_width = (rels + 1) // 2
    cell = levels * lat_rows
    tokens = lon_width * cell
    scale = 1.0 / math.sqrt(dim)
    tiles = fold_s.shape[0]
    lanes = tiles * 128
    slots = fold_s.shape[1] // (cell + 1)
    pairs, packed, _ = w_same_ref.shape
    part = packed // 4
    parity = me_ref[0] % 2

    bias_copy = pltpu.make_async_copy(bias_ref, bias_s, bias_sem)
    bias_copy.start()
    load_weights(w_s, w_same_ref, w_other_ref, parity)
    std, _ = normalise(x_ref)
    normed_s[...] = (std * gain_ref[...]).astype(BF16)
    window = lax.broadcasted_iota(jnp.int32, (dim, windows * tokens), 1) // tokens

    def apart(x):
        x = x.astype(BF16).reshape(heads, dim, windows * tokens)
        return [jnp.where((window == w)[None], x, jnp.zeros_like(x)) for w in range(windows)]

    w_qry = w_s[0].astype(BF16)
    w_key = w_s[1].astype(BF16)
    w_val = w_s[2].astype(BF16)
    w_out = w_s[3].T.astype(BF16)
    for dst, x in ((q_s, mm(w_qry, normed_s[...], NT)), (d_s, mm(w_out, c_ref[...], NT))):
        for w, block in enumerate(apart(x)):
            dst[:, w * dim:(w + 1) * dim, :] = block
    for w in range(windows):
        nw = normed_s[w * tokens:(w + 1) * tokens]
        k_s[:, w * dim:(w + 1) * dim, :] = mm(w_key, nw, NT).astype(BF16).reshape(heads, dim, tokens)
        v_s[:, w * dim:(w + 1) * dim, :] = mm(w_val, nw, NT).astype(BF16).reshape(heads, dim, tokens)
    query = lax.broadcasted_iota(jnp.int32, (tokens, tokens * windows), 1) % tokens
    pick_s[...] = (query == lax.broadcasted_iota(jnp.int32, query.shape, 0)).astype(F32).astype(BF16)
    dsum_s[...] = jnp.zeros_like(dsum_s)
    fold_s[...] = jnp.zeros_like(fold_s)

    def own(x):
        out = x[:dim]
        for w in range(1, windows):
            out = jnp.where(window == w, x[w * dim:(w + 1) * dim], out)
        return out

    def head(h, carry):
        qh, dh, kh, vh = q_s[h], d_s[h], k_s[h], v_s[h]
        score = mm(kh, qh, TN) * (scale * LOG2E) + jnp.concatenate([bias_s[h]] * windows, axis=1)
        d_prob = mm(vh, dh, TN)
        expo = jnp.exp2(score - jnp.max(score, axis=0, keepdims=True))
        prob = expo * (1.0 / jnp.sum(expo, axis=0, keepdims=True))
        low = prob.astype(BF16)
        ctx = own(mm(vh, low, NN))
        ctx_s[h] = ctx.astype(BF16)
        dv_s[h] = mm(dh, low, NT).astype(BF16)
        d_ctx = dh[:dim].astype(F32)
        for w in range(1, windows):
            d_ctx = d_ctx + dh[w * dim:(w + 1) * dim].astype(F32)
        inner = jnp.sum(ctx * d_ctx, axis=0, keepdims=True)
        d_low = (prob * (d_prob - inner)).astype(BF16)
        dq_s[h] = (own(mm(kh, d_low, NN)) * scale).astype(BF16)
        both = mm(jnp.concatenate([qh, pick_s[...]], axis=0), d_low, NT)
        dk_s[h] = (both[:windows * dim] * scale).astype(BF16)
        dsum_s[:, :tokens] = both[windows * dim:]
        folded = jnp.zeros((cell, lanes), F32)
        for p in range(lon_width):
            off = (lon_width - 1 - p) * cell
            piece = dsum_s[p * cell:(p + 1) * cell, :]
            folded = folded + (pltpu.roll(piece, off, 1) if off else piece)
        for g in range(tiles):
            fold_s[g, pl.ds(h, cell, stride=slots), :] = folded[:, g * 128:(g + 1) * 128]
        return carry

    bias_copy.wait()
    lax.fori_loop(0, heads, head, 0, unroll=True)

    def by_window(ref, w):
        return ref[:, w * dim:(w + 1) * dim, :].reshape(feat, tokens)

    gw_s[0] = mm(dq_s[...].reshape(feat, windows * tokens), normed_s[...], NN)
    gw_s[3] = mm(ctx_s[...].reshape(feat, windows * tokens), c_ref[...], NN).T
    for i, ref in ((1, dk_s), (2, dv_s)):
        total = jnp.zeros((feat, feat), F32)
        for w in range(windows):
            total = total + mm(by_window(ref, w), normed_s[w * tokens:(w + 1) * tokens], NN)
        gw_s[i] = total
    g_gain = jnp.zeros((1, feat), F32)
    for i in range(3):
        g_gain = g_gain + jnp.sum(gw_s[i] * w_s[i], axis=0, keepdims=True)
    g_gain = g_gain / gain_ref[...]

    fold = jnp.concatenate([fold_s[g, 0:cell * slots, :] for g in range(tiles)], axis=1).astype(BF16)
    back = mm(fold, order_ref[...], NT)
    width = lat_rows * rels
    half = back.shape[1] // levels
    per = 2 * pairs // (levels * levels)
    run = lat_rows // per
    wide = -(-run * width // 128) * 128
    back = back.reshape(levels * per, run, slots, levels * half)
    full = []
    for w in range(levels):
        line = jnp.zeros((levels * per * slots, wide), F32)
        for k in range(run):
            piece = back[:, k, :, w * half:(w + 1) * half].reshape(levels * per * slots, half)
            piece = jnp.concatenate([piece, jnp.zeros((levels * per * slots, wide - half), F32)], axis=1)
            line = line + (pltpu.roll(piece, k * width, 1) if k else piece)
        full.append(line)

    lane = lax.broadcasted_iota(jnp.int32, (8, feat), 1) % 128
    row = lax.broadcasted_iota(jnp.int32, (8, feat), 0)
    gains = jnp.zeros((8, feat), F32)
    for i in range(4):
        turned = jnp.concatenate(
            [pltpu.roll(g_gain[:, g * 128:(g + 1) * 128], (160 - 32 * i) % 128, 1) for g in range(feat // 128)], axis=1
        )
        gains = jnp.where((row == 4 + i) & (lane >= 32) & (lane < 64), turned, gains)

    for j in range(2 * pairs):
        z, w, a = j // (levels * per), j // per % levels, j % per
        at = (z * per + a) * slots
        line = full[w][at:at + slots]
        tail = line[:, feat:]
        moved = jnp.concatenate([pltpu.roll(tail[:8], 4, 0), tail[:8], pltpu.roll(tail[8:], 4, 0)], axis=1)
        moved = jnp.where(lane < 32, moved, gains)
        lines_s[j] = jnp.concatenate([line[:8, :feat], jnp.where(row >= 4, moved, line[8:, :feat])], axis=0).astype(BF16)
    for ref, side in ((same_ref, parity), (other_ref, 1 - parity)):
        for i in range(pairs):
            start = pl.multiple_of((2 * i + side) * part, part)
            block = jnp.concatenate([gw_s[k, pl.ds(start, part), :] for k in range(4)], axis=0)
            ref[i, 0:packed, :] = block.astype(BF16)
            ref[i, packed:, :] = lines_s[2 * i + side]


def run_block(me, x, c, gain, w_same, w_other, bias, order, heads, windows, levels, lat_rows, rels):
    rows, feat = x.shape
    tokens = rows // windows
    dim = feat // heads
    cell = levels * lat_rows
    tiles = order.shape[1] // 128
    slots = heads + -heads % 16
    pairs, packed, _ = w_same.shape
    vmem = pl.BlockSpec(memory_space=pltpu.VMEM)
    sent = jax.ShapeDtypeStruct((pairs, packed + slots, feat), BF16)
    aligned = jax.ShapeDtypeStruct((heads, windows * dim, tokens), BF16)
    return pl.pallas_call(
        functools.partial(block_kernel, heads=heads, windows=windows, levels=levels, lat_rows=lat_rows, rels=rels),
        out_shape=(sent, sent, jax.ShapeDtypeStruct((heads, dim, rows), BF16), aligned, aligned),
        in_specs=[pl.BlockSpec(memory_space=pltpu.SMEM)] + [vmem] * 5 + [pl.BlockSpec(memory_space=pl.ANY), vmem],
        out_specs=[vmem] * 5,
        scratch_shapes=[
            pltpu.VMEM((4, feat, feat), F32),
            pltpu.VMEM((4, feat, feat), F32),
            pltpu.VMEM((rows, feat), BF16),
            pltpu.VMEM((heads, windows * dim, rows), BF16),
            pltpu.VMEM((heads, windows * dim, rows), BF16),
            pltpu.VMEM((heads, windows * dim, tokens), BF16),
            pltpu.VMEM((heads, windows * dim, tokens), BF16),
            pltpu.VMEM((heads, dim, rows), BF16),
            pltpu.VMEM((tokens, tiles * 128), F32),
            pltpu.VMEM((tiles, (cell + 1) * slots, 128), F32),
            pltpu.VMEM((tokens, rows), BF16),
            pltpu.VMEM((2 * pairs, slots, feat), BF16),
            pltpu.VMEM((heads, tokens, tokens), F32),
            pltpu.SemaphoreType.DMA,
        ],
        compiler_params=pltpu.CompilerParams(vmem_limit_bytes=BLOCK_MB * 2**20),
        name="window_block",
    )(me, x, c, gain, w_same, w_other, bias, order)


def input_kernel(me_ref, x_ref, gain_ref, w_same_ref, w_other_ref, dq_ref, dk_ref, dv_ref, din_ref, w_s):
    heads, stacked, tokens = dk_ref.shape
    rows, feat = x_ref.shape
    windows = rows // tokens
    dim = stacked // windows
    load_weights(w_s, w_same_ref, w_other_ref, me_ref[0] % 2)
    std, inv = normalise(x_ref)
    gain = gain_ref[...]
    w_qry, w_key, w_val = (w_s[i].astype(BF16) for i in range(3))
    from_q = mm(dq_ref[...].reshape(feat, rows), w_qry, TN)
    for w in range(windows):
        at = slice(w * tokens, (w + 1) * tokens)
        d_normed = from_q[at]
        for ref, weight in ((dk_ref, w_key), (dv_ref, w_val)):
            d_normed = d_normed + mm(ref[:, w * dim:(w + 1) * dim, :].reshape(feat, tokens), weight, TN)
        g = d_normed * gain
        d_in = inv[at] * (
            g - jnp.mean(g, axis=1, keepdims=True) - std[at] * jnp.mean(g * std[at], axis=1, keepdims=True)
        )
        din_ref[at] = d_in.astype(BF16)


def input_gradient(me, x, gain, w_same, w_other, dq, dk, dv):
    feat = x.shape[1]
    vmem = pl.BlockSpec(memory_space=pltpu.VMEM)
    return pl.pallas_call(
        input_kernel,
        out_shape=jax.ShapeDtypeStruct(x.shape, BF16),
        in_specs=[pl.BlockSpec(memory_space=pltpu.SMEM)] + [vmem] * 7,
        out_specs=vmem,
        scratch_shapes=[pltpu.VMEM((3, feat, feat), F32)],
        compiler_params=pltpu.CompilerParams(vmem_limit_bytes=SMALL_MB * 2**20),
        name="input_gradient",
    )(me, x, gain, w_same, w_other, dq, dk, dv)


def sum_kernel(x_ref, out_ref, table_ref, *, packed):
    pieces, rows, feat = x_ref.shape
    total = x_ref[0].astype(F32)
    for i in range(1, pieces):
        total = total + x_ref[i].astype(F32)
    turned = total[:packed].T
    blocks = out_ref.shape[0]
    part = feat // blocks
    lane = lax.broadcasted_iota(jnp.int32, (1, feat), 1) % 128
    gain = jnp.zeros((1, feat), F32)
    for i in range(4):
        line = total[rows - 4 + i:rows - 3 + i]
        moved = jnp.concatenate(
            [pltpu.roll(line[:, g * 128:(g + 1) * 128], (32 * i - 32) % 128, 1) for g in range(feat // 128)], axis=1
        )
        gain = jnp.where((lane >= 32 * i) & (lane < 32 * i + 32), moved, gain)
    high = gain.astype(BF16).astype(F32)
    gains = jnp.concatenate(
        [src[:, k * packed:(k + 1) * packed] for src in (high, gain - high) for k in range(feat // packed)], axis=0
    )
    for i in range(blocks):
        out_ref[i] = jnp.concatenate([turned[i * part:(i + 1) * part], gains], axis=0).astype(BF16)
    table_ref[...] = total[packed:]


def sum_and_turn(x, blocks, packed):
    pieces, rows, feat = x.shape
    vmem = pl.BlockSpec(memory_space=pltpu.VMEM)
    return pl.pallas_call(
        functools.partial(sum_kernel, packed=packed),
        out_shape=(
            jax.ShapeDtypeStruct((blocks, feat // blocks + 2 * (feat // packed), packed), BF16),
            jax.ShapeDtypeStruct((rows - packed, feat), F32),
        ),
        in_specs=[vmem],
        out_specs=[vmem, vmem],
        compiler_params=pltpu.CompilerParams(vmem_limit_bytes=SMALL_MB * 2**20),
        name="sum_and_turn",
    )(x)


def last_kernel(x_ref, query_ref, key_ref, value_ref, out_ref, gain_ref):
    total = x_ref[0].astype(F32)
    for i in range(1, x_ref.shape[0]):
        total = total + x_ref[i].astype(F32)
    part = query_ref.shape[0]
    for i, ref in enumerate((query_ref, key_ref, value_ref, out_ref)):
        ref[...] = total[:part, i * part:(i + 1) * part]
    count = (total.shape[0] - part) // 2
    gain = total[part:part + count] + total[part + count:]
    gain_ref[...] = jnp.concatenate([gain[k:k + 1] for k in range(count)], axis=1).reshape(gain_ref.shape)


def last_sum(x, part, feat):
    vmem = pl.BlockSpec(memory_space=pltpu.VMEM)
    block = jax.ShapeDtypeStruct((part, part), F32)
    return pl.pallas_call(
        last_kernel,
        out_shape=(block, block, block, block, jax.ShapeDtypeStruct((feat,), F32)),
        in_specs=[vmem],
        out_specs=[vmem] * 5,
        compiler_params=pltpu.CompilerParams(vmem_limit_bytes=SMALL_MB * 2**20),
        name="last_sum",
    )(x)


def swap(x, axis, bit):
    n = lax.axis_size(axis)
    return lax.ppermute(x, axis, [(i, i ^ bit) for i in range(n)])


def shift(x, lat_by, lon_by):
    lats, lons = lax.axis_size("lat"), lax.axis_size("lon")
    if lon_by == 0:
        return lax.ppermute(x, "lat", [(i, (i + lat_by) % lats) for i in range(lats)])
    if lat_by == 0:
        return lax.ppermute(x, "lon", [(i, (i + lon_by) % lons) for i in range(lons)])
    pairs = [
        (a * lons + b, (a + lat_by) % lats * lons + (b + lon_by) % lons)
        for a in range(lats)
        for b in range(lons)
    ]
    return lax.ppermute(x, ("lat", "lon"), pairs)


def spread_over_lat(x):
    return lax.all_to_all(x, "lat", 0, 0)


def spread_over_lon(x):
    n = lax.axis_size("lon")
    groups = [list(range(c, n, 2)) for c in range(2)]
    return lax.all_to_all(x, "lon", 0, 0, axis_index_groups=groups)


def local(fields, cotangent, norm_gain, w_query, w_key, w_value, w_out, rel_table):
    levels, lat_rows, lon_cols, feat = fields.shape
    heads = rel_table.shape[1]
    rels = rel_table.shape[2] // (levels * levels * lat_rows * lat_rows)
    lon_width = (rels + 1) // 2
    half_rows = lat_rows // 2
    half_cols = lon_width // 2
    windows = lon_cols // lon_width
    lats = lax.axis_size("lat")
    lons = lax.axis_size("lon")
    me_lat = lax.axis_index("lat")
    me_lon = lax.axis_index("lon")
    part = w_query.shape[0]

    both = jnp.stack([fields, cotangent]).transpose(3, 0, 1, 2, 4)

    mine = jnp.concatenate([w_query, w_key, w_value, w_out], axis=1)
    rows_all = spread_over_lat(jnp.broadcast_to(mine[None], (lats,) + mine.shape))
    turned = turn(rows_all, lons // 2)
    turned, table = lax.optimization_barrier((turned, rel_table[0]))
    w_same = spread_over_lon(turned)
    own = both[half_cols:, :, :, half_rows:]
    south = shift(both[half_cols:, :, :, :half_rows], -1, 0)
    east = shift(both[:half_cols, :, :, half_rows:], 0, -1)
    corner = shift(both[:half_cols, :, :, :half_rows], -1, -1)

    order = jnp.asarray(offset_order(rels, levels, lat_rows, 256), BF16)
    last = (me_lat == lats - 1).astype(jnp.int32).reshape(1)
    slots = heads + -heads % 16
    bias = make_bias(last, table, order, levels, lat_rows, rels, slots, windows)
    w_same, bias, own, south, east, corner = lax.optimization_barrier((w_same, bias, own, south, east, corner))
    w_other = swap(w_same, "lon", 1)
    moved = jnp.concatenate(
        [jnp.concatenate([own, south], axis=3), jnp.concatenate([east, corner], axis=3)], axis=0
    )
    shifted = moved[:, 0].reshape(-1, feat)
    cot_shift = moved[:, 1].reshape(-1, feat)

    me = me_lon.reshape(1)
    gain = norm_gain[None]
    g_same, g_other, dq, dk, dv = run_block(
        me, shifted, cot_shift, gain, w_same, w_other, bias, order, heads, windows, levels, lat_rows, rels
    )

    paired = (g_same.astype(F32) + swap(g_other, "lon", 1).astype(F32)).astype(BF16)
    d_input = input_gradient(me, shifted, gain, w_same, w_other, dq, dk, dv)
    paired, d_input = lax.optimization_barrier((paired, d_input))
    arrived = spread_over_lon(paired)
    message, lines = sum_and_turn(arrived, lats, 4 * part)
    grad_query, grad_key, grad_value, grad_out, grad_gain = last_sum(spread_over_lat(message), part, feat)

    d_in = d_input.reshape(lon_cols, levels, lat_rows, feat)
    stay = lon_cols - half_cols
    west = shift(d_in[stay:, :, :half_rows], 0, 1)
    north = shift(d_in[:stay, :, half_rows:], 1, 0)
    corner = shift(d_in[stay:, :, half_rows:], 1, 1)
    west, north, corner, d_in, lines, _ = lax.optimization_barrier((west, north, corner, d_in, lines, message))
    over = rel_table.shape[2] // lons - feat
    groups = feat // 128
    tail = lines[heads:].reshape(slots - heads, groups, 128)[:, :, :over].transpose(1, 0, 2)
    grad_table = jnp.concatenate([lines[:heads], tail.reshape(heads, over)], axis=1)[None]
    back = jnp.concatenate(
        [jnp.concatenate([corner, west], axis=2), jnp.concatenate([north, d_in[:stay, :, :half_rows]], axis=2)],
        axis=0,
    ).transpose(1, 2, 0, 3)
    grad_fields = (cotangent.astype(F32) + back.astype(F32)).astype(BF16)
    return (grad_fields, grad_query, grad_key, grad_value, grad_out, grad_table, grad_gain)


def solution(mesh):
    return jax.shard_map(
        local,
        mesh=mesh,
        in_specs=(
            P(None, "lat", "lon", None),
            P(None, "lat", "lon", None),
            P(),
            P("lat", "lon"),
            P("lat", "lon"),
            P("lat", "lon"),
            P("lat", "lon"),
            P("lat", None, None),
        ),
        out_specs=(
            P(None, "lat", "lon", None),
            P("lat", "lon"),
            P("lat", "lon"),
            P("lat", "lon"),
            P("lat", "lon"),
            P("lat", None, "lon"),
            P(),
        ),
        check_vma=False,
    )
```

```python
import functools
import math

import jax
import jax.numpy as jnp
import numpy as np
from jax import lax
from jax.experimental import pallas as pl
from jax.experimental.pallas import tpu as pltpu
from jax.sharding import PartitionSpec as P

EPSILON = 1e-05
MASKED = -1000000000.0
LOG2E = math.log2(math.e)
BLOCK_MB = 48
SMALL_MB = 16
F32 = jnp.float32
BF16 = jnp.bfloat16
NN = (((1,), (0,)), ((), ()))
NT = (((1,), (1,)), ((), ()))
TN = (((0,), (0,)), ((), ()))


def mm(a, b, dims):
    return lax.dot_general(a, b, dims, preferred_element_type=F32)


def offset_order(rels, levels, lat_rows, group):
    lanes = rels * levels * lat_rows
    order = np.zeros((levels * group, lanes + -lanes % 128), np.float32)
    for level in range(levels):
        for lat in range(lat_rows):
            for rel in range(rels):
                order[level * group + lat * rels + rel, ((rels - 1 - rel) * levels + level) * lat_rows + lat] = 1.0
    return order


def bias_kernel(last_ref, table_ref, order_ref, out_ref, table_s, strips_s, bias_s, out_s, sems, *, levels, lat_rows, rels, windows):
    heads = table_ref.shape[0]
    slots = table_s.shape[1]
    cell = levels * lat_rows
    width = lat_rows * rels
    group = table_s.shape[2] // levels
    tiles = strips_s.shape[0]
    lanes = tiles * 128
    lon_width = (rels + 1) // 2
    tokens = lon_width * cell
    table_s[...] = jnp.zeros_like(table_s)
    table = table_ref[...]
    for z in range(levels):
        for w in range(levels):
            for a in range(lat_rows):
                at = ((z * levels + w) * lat_rows + a) * width
                table_s[z * lat_rows + a, 0:heads, w * group:w * group + width] = table[:, at:at + width]
    full = table_s[...].reshape(cell * slots, levels * group)
    order = order_ref[...]
    high = full.astype(BF16)
    rest = full - high.astype(F32)
    mid = rest.astype(BF16)
    low = (rest - mid.astype(F32)).astype(BF16)
    strips = mm(high, order, NN) + mm(mid, order, NN) + mm(low, order, NN)
    row = lax.broadcasted_iota(jnp.int32, (cell * slots, 1), 0) // slots
    lane = lax.broadcasted_iota(jnp.int32, (1, lanes), 1)
    row_north = (row % lat_rows < lat_rows // 2).astype(F32)
    lane_north = (lane % lat_rows < lat_rows // 2).astype(F32)
    crossing = (row_north != lane_north) & (last_ref[0] != 0)
    strips = jnp.where(crossing, MASKED, strips) * LOG2E
    for g in range(tiles):
        strips_s[g, 0:cell * slots, :] = strips[:, g * 128:(g + 1) * 128]

    def head(h, carry):
        strip = jnp.concatenate([strips_s[g, pl.ds(h, cell, stride=slots), :] for g in range(tiles)], axis=1)
        for p in range(lon_width):
            off = (lon_width - 1 - p) * cell
            rolled = pltpu.roll(strip, lanes - off, 1) if off else strip
            bias_s[p * cell:(p + 1) * cell, :] = rolled[:, :tokens]
        out_s[h] = bias_s[...].T
        pltpu.make_async_copy(out_s.at[h], out_ref.at[h], sems.at[h]).start()
        return carry

    lax.fori_loop(0, heads, head, 0)
    for h in range(heads):
        pltpu.make_async_copy(out_s.at[h], out_ref.at[h], sems.at[h]).wait()


def make_bias(last, table, order, levels, lat_rows, rels, slots, windows):
    heads = table.shape[0]
    cell = levels * lat_rows
    tokens = (rels + 1) // 2 * cell
    tiles = order.shape[1] // 128
    vmem = pl.BlockSpec(memory_space=pltpu.VMEM)
    return pl.pallas_call(
        functools.partial(bias_kernel, levels=levels, lat_rows=lat_rows, rels=rels, windows=windows),
        out_shape=jax.ShapeDtypeStruct((heads, tokens, tokens), F32),
        in_specs=[pl.BlockSpec(memory_space=pltpu.SMEM), vmem, vmem],
        out_specs=pl.BlockSpec(memory_space=pl.ANY),
        scratch_shapes=[
            pltpu.VMEM((cell, slots, order.shape[0]), F32),
            pltpu.VMEM((tiles, (cell + 1) * slots, 128), F32),
            pltpu.VMEM((tokens, tokens), F32),
            pltpu.VMEM((heads, tokens, tokens), F32),
            pltpu.SemaphoreType.DMA((heads,)),
        ],
        compiler_params=pltpu.CompilerParams(vmem_limit_bytes=SMALL_MB * 2**20),
        name="make_bias",
    )(last, table, order)


def turn_kernel(x_ref, out_ref):
    blocks, rows, lanes = x_ref.shape
    turned = x_ref[...].astype(F32).reshape(blocks * rows, lanes).T.astype(BF16)
    for i in range(out_ref.shape[0]):
        out_ref[i] = turned


def turn(x, copies):
    blocks, rows, lanes = x.shape
    vmem = pl.BlockSpec(memory_space=pltpu.VMEM)
    return pl.pallas_call(
        turn_kernel,
        out_shape=jax.ShapeDtypeStruct((copies, lanes, blocks * rows), BF16),
        in_specs=[vmem],
        out_specs=vmem,
        compiler_params=pltpu.CompilerParams(vmem_limit_bytes=SMALL_MB * 2**20),
        name="turn_weights",
    )(x)


def load_weights(w_s, w_same_ref, w_other_ref, parity):
    pairs, packed, _ = w_same_ref.shape
    part = packed // 4
    for ref, side in ((w_same_ref, parity), (w_other_ref, 1 - parity)):
        for i in range(pairs):
            block = ref[i].astype(F32)
            start = pl.multiple_of((2 * i + side) * part, part)
            for k in range(w_s.shape[0]):
                w_s[k, pl.ds(start, part), :] = block[k * part:(k + 1) * part]


def normalise(x_ref):
    xf = x_ref[...].astype(F32)
    mean = jnp.mean(xf, axis=1, keepdims=True)
    centred = xf - mean
    var = jnp.mean(centred * centred, axis=1, keepdims=True)
    inv = 1.0 / jnp.sqrt(var + EPSILON)
    return centred * inv, inv


def block_kernel(
    me_ref, x_ref, c_ref, gain_ref, w_same_ref, w_other_ref, bias_ref, order_ref,
    same_ref, other_ref, dq_s, dk_s, dv_s,
    w_s, gw_s, normed_s, q_s, d_s, k_s, v_s, ctx_s, dsum_s, fold_s, pick_s, lines_s, bias_s, bias_sem,
    *, heads, windows, levels, lat_rows, rels,
):
    feat = x_ref.shape[1]
    dim = feat // heads
    lon_width = (rels + 1) // 2
    cell = levels * lat_rows
    tokens = lon_width * cell
    scale = 1.0 / math.sqrt(dim)
    tiles = fold_s.shape[0]
    lanes = tiles * 128
    slots = fold_s.shape[1] // (cell + 1)
    pairs, packed, _ = w_same_ref.shape
    part = packed // 4
    parity = me_ref[0] % 2

    bias_copy = pltpu.make_async_copy(bias_ref, bias_s, bias_sem)
    bias_copy.start()
    load_weights(w_s, w_same_ref, w_other_ref, parity)
    std, _ = normalise(x_ref)
    normed_s[...] = (std * gain_ref[...]).astype(BF16)
    window = lax.broadcasted_iota(jnp.int32, (dim, windows * tokens), 1) // tokens

    def apart(x):
        x = x.astype(BF16).reshape(heads, dim, windows * tokens)
        return [jnp.where((window == w)[None], x, jnp.zeros_like(x)) for w in range(windows)]

    w_qry = w_s[0].astype(BF16)
    w_key = w_s[1].astype(BF16)
    w_val = w_s[2].astype(BF16)
    w_out = w_s[3].T.astype(BF16)
    for dst, x in ((q_s, mm(w_qry, normed_s[...], NT)), (d_s, mm(w_out, c_ref[...], NT))):
        for w, block in enumerate(apart(x)):
            dst[:, w * dim:(w + 1) * dim, :] = block
    for w in range(windows):
        nw = normed_s[w * tokens:(w + 1) * tokens]
        k_s[:, w * dim:(w + 1) * dim, :] = mm(w_key, nw, NT).astype(BF16).reshape(heads, dim, tokens)
        v_s[:, w * dim:(w + 1) * dim, :] = mm(w_val, nw, NT).astype(BF16).reshape(heads, dim, tokens)
    query = lax.broadcasted_iota(jnp.int32, (tokens, tokens * windows), 1) % tokens
    pick_s[...] = (query == lax.broadcasted_iota(jnp.int32, query.shape, 0)).astype(F32).astype(BF16)
    dsum_s[...] = jnp.zeros_like(dsum_s)
    fold_s[...] = jnp.zeros_like(fold_s)

    def own(x):
        out = x[:dim]
        for w in range(1, windows):
            out = jnp.where(window == w, x[w * dim:(w + 1) * dim], out)
        return out

    def head(h, carry):
        qh, dh, kh, vh = q_s[h], d_s[h], k_s[h], v_s[h]
        score = mm(kh, qh, TN) * (scale * LOG2E) + jnp.concatenate([bias_s[h]] * windows, axis=1)
        d_prob = mm(vh, dh, TN)
        expo = jnp.exp2(score - jnp.max(score, axis=0, keepdims=True))
        prob = expo * (1.0 / jnp.sum(expo, axis=0, keepdims=True))
        low = prob.astype(BF16)
        ctx = own(mm(vh, low, NN))
        ctx_s[h] = ctx.astype(BF16)
        dv_s[h] = mm(dh, low, NT).astype(BF16)
        d_ctx = dh[:dim].astype(F32)
        for w in range(1, windows):
            d_ctx = d_ctx + dh[w * dim:(w + 1) * dim].astype(F32)
        inner = jnp.sum(ctx * d_ctx, axis=0, keepdims=True)
        d_low = (prob * (d_prob - inner)).astype(BF16)
        dq_s[h] = (own(mm(kh, d_low, NN)) * scale).astype(BF16)
        both = mm(jnp.concatenate([qh, pick_s[...]], axis=0), d_low, NT)
        dk_s[h] = (both[:windows * dim] * scale).astype(BF16)
        dsum_s[:, :tokens] = both[windows * dim:]
        folded = jnp.zeros((cell, lanes), F32)
        for p in range(lon_width):
            off = (lon_width - 1 - p) * cell
            piece = dsum_s[p * cell:(p + 1) * cell, :]
            folded = folded + (pltpu.roll(piece, off, 1) if off else piece)
        for g in range(tiles):
            fold_s[g, pl.ds(h, cell, stride=slots), :] = folded[:, g * 128:(g + 1) * 128]
        return carry

    bias_copy.wait()
    lax.fori_loop(0, heads, head, 0, unroll=True)

    def by_window(ref, w):
        return ref[:, w * dim:(w + 1) * dim, :].reshape(feat, tokens)

    gw_s[0] = mm(dq_s[...].reshape(feat, windows * tokens), normed_s[...], NN)
    gw_s[3] = mm(ctx_s[...].reshape(feat, windows * tokens), c_ref[...], NN).T
    for i, ref in ((1, dk_s), (2, dv_s)):
        total = jnp.zeros((feat, feat), F32)
        for w in range(windows):
            total = total + mm(by_window(ref, w), normed_s[w * tokens:(w + 1) * tokens], NN)
        gw_s[i] = total
    g_gain = jnp.zeros((1, feat), F32)
    for i in range(3):
        g_gain = g_gain + jnp.sum(gw_s[i] * w_s[i], axis=0, keepdims=True)
    g_gain = g_gain / gain_ref[...]

    fold = jnp.concatenate([fold_s[g, 0:cell * slots, :] for g in range(tiles)], axis=1).astype(BF16)
    back = mm(fold, order_ref[...], NT)
    width = lat_rows * rels
    half = back.shape[1] // levels
    per = 2 * pairs // (levels * levels)
    run = lat_rows // per
    wide = -(-run * width // 128) * 128
    back = back.reshape(levels * per, run, slots, levels * half)
    full = []
    for w in range(levels):
        line = jnp.zeros((levels * per * slots, wide), F32)
        for k in range(run):
            piece = back[:, k, :, w * half:(w + 1) * half].reshape(levels * per * slots, half)
            piece = jnp.concatenate([piece, jnp.zeros((levels * per * slots, wide - half), F32)], axis=1)
            line = line + (pltpu.roll(piece, k * width, 1) if k else piece)
        full.append(line)

    lane = lax.broadcasted_iota(jnp.int32, (8, feat), 1) % 128
    row = lax.broadcasted_iota(jnp.int32, (8, feat), 0)
    gains = jnp.zeros((8, feat), F32)
    for i in range(4):
        turned = jnp.concatenate(
            [pltpu.roll(g_gain[:, g * 128:(g + 1) * 128], (160 - 32 * i) % 128, 1) for g in range(feat // 128)], axis=1
        )
        gains = jnp.where((row == 4 + i) & (lane >= 32) & (lane < 64), turned, gains)

    for j in range(2 * pairs):
        z, w, a = j // (levels * per), j // per % levels, j % per
        at = (z * per + a) * slots
        line = full[w][at:at + slots]
        tail = line[:, feat:]
        moved = jnp.concatenate([pltpu.roll(tail[:8], 4, 0), tail[:8], pltpu.roll(tail[8:], 4, 0)], axis=1)
        moved = jnp.where(lane < 32, moved, gains)
        lines_s[j] = jnp.concatenate([line[:8, :feat], jnp.where(row >= 4, moved, line[8:, :feat])], axis=0).astype(BF16)
    for ref, side in ((same_ref, parity), (other_ref, 1 - parity)):
        for i in range(pairs):
            start = pl.multiple_of((2 * i + side) * part, part)
            block = jnp.concatenate([gw_s[k, pl.ds(start, part), :] for k in range(4)], axis=0)
            ref[i, 0:packed, :] = block.astype(BF16)
            ref[i, packed:, :] = lines_s[2 * i + side]


def run_block(me, x, c, gain, w_same, w_other, bias, order, heads, windows, levels, lat_rows, rels):
    rows, feat = x.shape
    tokens = rows // windows
    dim = feat // heads
    cell = levels * lat_rows
    tiles = order.shape[1] // 128
    slots = heads + -heads % 16
    pairs, packed, _ = w_same.shape
    vmem = pl.BlockSpec(memory_space=pltpu.VMEM)
    sent = jax.ShapeDtypeStruct((pairs, packed + slots, feat), BF16)
    aligned = jax.ShapeDtypeStruct((heads, windows * dim, tokens), BF16)
    return pl.pallas_call(
        functools.partial(block_kernel, heads=heads, windows=windows, levels=levels, lat_rows=lat_rows, rels=rels),
        out_shape=(sent, sent, jax.ShapeDtypeStruct((heads, dim, rows), BF16), aligned, aligned),
        in_specs=[pl.BlockSpec(memory_space=pltpu.SMEM)] + [vmem] * 5 + [pl.BlockSpec(memory_space=pl.ANY), vmem],
        out_specs=[vmem] * 5,
        scratch_shapes=[
            pltpu.VMEM((4, feat, feat), F32),
            pltpu.VMEM((4, feat, feat), F32),
            pltpu.VMEM((rows, feat), BF16),
            pltpu.VMEM((heads, windows * dim, rows), BF16),
            pltpu.VMEM((heads, windows * dim, rows), BF16),
            pltpu.VMEM((heads, windows * dim, tokens), BF16),
            pltpu.VMEM((heads, windows * dim, tokens), BF16),
            pltpu.VMEM((heads, dim, rows), BF16),
            pltpu.VMEM((tokens, tiles * 128), F32),
            pltpu.VMEM((tiles, (cell + 1) * slots, 128), F32),
            pltpu.VMEM((tokens, rows), BF16),
            pltpu.VMEM((2 * pairs, slots, feat), BF16),
            pltpu.VMEM((heads, tokens, tokens), F32),
            pltpu.SemaphoreType.DMA,
        ],
        compiler_params=pltpu.CompilerParams(vmem_limit_bytes=BLOCK_MB * 2**20),
        name="window_block",
    )(me, x, c, gain, w_same, w_other, bias, order)


def input_kernel(me_ref, x_ref, gain_ref, w_same_ref, w_other_ref, dq_ref, dk_ref, dv_ref, din_ref, w_s):
    heads, stacked, tokens = dk_ref.shape
    rows, feat = x_ref.shape
    windows = rows // tokens
    dim = stacked // windows
    load_weights(w_s, w_same_ref, w_other_ref, me_ref[0] % 2)
    std, inv = normalise(x_ref)
    gain = gain_ref[...]
    w_qry, w_key, w_val = (w_s[i].astype(BF16) for i in range(3))
    from_q = mm(dq_ref[...].reshape(feat, rows), w_qry, TN)
    for w in range(windows):
        at = slice(w * tokens, (w + 1) * tokens)
        d_normed = from_q[at]
        for ref, weight in ((dk_ref, w_key), (dv_ref, w_val)):
            d_normed = d_normed + mm(ref[:, w * dim:(w + 1) * dim, :].reshape(feat, tokens), weight, TN)
        g = d_normed * gain
        d_in = inv[at] * (
            g - jnp.mean(g, axis=1, keepdims=True) - std[at] * jnp.mean(g * std[at], axis=1, keepdims=True)
        )
        din_ref[at] = d_in.astype(BF16)


def input_gradient(me, x, gain, w_same, w_other, dq, dk, dv):
    feat = x.shape[1]
    vmem = pl.BlockSpec(memory_space=pltpu.VMEM)
    return pl.pallas_call(
        input_kernel,
        out_shape=jax.ShapeDtypeStruct(x.shape, BF16),
        in_specs=[pl.BlockSpec(memory_space=pltpu.SMEM)] + [vmem] * 7,
        out_specs=vmem,
        scratch_shapes=[pltpu.VMEM((3, feat, feat), F32)],
        compiler_params=pltpu.CompilerParams(vmem_limit_bytes=SMALL_MB * 2**20),
        name="input_gradient",
    )(me, x, gain, w_same, w_other, dq, dk, dv)


def sum_kernel(x_ref, out_ref, table_ref, *, packed):
    pieces, rows, feat = x_ref.shape
    total = x_ref[0].astype(F32)
    for i in range(1, pieces):
        total = total + x_ref[i].astype(F32)
    turned = total[:packed].T
    blocks = out_ref.shape[0]
    part = feat // blocks
    lane = lax.broadcasted_iota(jnp.int32, (1, feat), 1) % 128
    gain = jnp.zeros((1, feat), F32)
    for i in range(4):
        line = total[rows - 4 + i:rows - 3 + i]
        moved = jnp.concatenate(
            [pltpu.roll(line[:, g * 128:(g + 1) * 128], (32 * i - 32) % 128, 1) for g in range(feat // 128)], axis=1
        )
        gain = jnp.where((lane >= 32 * i) & (lane < 32 * i + 32), moved, gain)
    high = gain.astype(BF16).astype(F32)
    gains = jnp.concatenate(
        [src[:, k * packed:(k + 1) * packed] for src in (high, gain - high) for k in range(feat // packed)], axis=0
    )
    for i in range(blocks):
        out_ref[i] = jnp.concatenate([turned[i * part:(i + 1) * part], gains], axis=0).astype(BF16)
    table_ref[...] = total[packed:]


def sum_and_turn(x, blocks, packed):
    pieces, rows, feat = x.shape
    vmem = pl.BlockSpec(memory_space=pltpu.VMEM)
    return pl.pallas_call(
        functools.partial(sum_kernel, packed=packed),
        out_shape=(
            jax.ShapeDtypeStruct((blocks, feat // blocks + 2 * (feat // packed), packed), BF16),
            jax.ShapeDtypeStruct((rows - packed, feat), F32),
        ),
        in_specs=[vmem],
        out_specs=[vmem, vmem],
        compiler_params=pltpu.CompilerParams(vmem_limit_bytes=SMALL_MB * 2**20),
        name="sum_and_turn",
    )(x)


def last_kernel(x_ref, query_ref, key_ref, value_ref, out_ref, gain_ref):
    total = x_ref[0].astype(F32)
    for i in range(1, x_ref.shape[0]):
        total = total + x_ref[i].astype(F32)
    part = query_ref.shape[0]
    for i, ref in enumerate((query_ref, key_ref, value_ref, out_ref)):
        ref[...] = total[:part, i * part:(i + 1) * part]
    count = (total.shape[0] - part) // 2
    gain = total[part:part + count] + total[part + count:]
    gain_ref[...] = jnp.concatenate([gain[k:k + 1] for k in range(count)], axis=1).reshape(gain_ref.shape)


def last_sum(x, part, feat):
    vmem = pl.BlockSpec(memory_space=pltpu.VMEM)
    block = jax.ShapeDtypeStruct((part, part), F32)
    return pl.pallas_call(
        last_kernel,
        out_shape=(block, block, block, block, jax.ShapeDtypeStruct((feat,), F32)),
        in_specs=[vmem],
        out_specs=[vmem] * 5,
        compiler_params=pltpu.CompilerParams(vmem_limit_bytes=SMALL_MB * 2**20),
        name="last_sum",
    )(x)


def swap(x, axis, bit):
    n = lax.axis_size(axis)
    return lax.ppermute(x, axis, [(i, i ^ bit) for i in range(n)])


def shift(x, lat_by, lon_by):
    lats, lons = lax.axis_size("lat"), lax.axis_size("lon")
    if lon_by == 0:
        return lax.ppermute(x, "lat", [(i, (i + lat_by) % lats) for i in range(lats)])
    if lat_by == 0:
        return lax.ppermute(x, "lon", [(i, (i + lon_by) % lons) for i in range(lons)])
    pairs = [
        (a * lons + b, (a + lat_by) % lats * lons + (b + lon_by) % lons)
        for a in range(lats)
        for b in range(lons)
    ]
    return lax.ppermute(x, ("lat", "lon"), pairs)


def spread_over_lat(x):
    return lax.all_to_all(x, "lat", 0, 0)


def spread_over_lon(x):
    n = lax.axis_size("lon")
    groups = [list(range(c, n, 2)) for c in range(2)]
    return lax.all_to_all(x, "lon", 0, 0, axis_index_groups=groups)


def local(fields, cotangent, norm_gain, w_query, w_key, w_value, w_out, rel_table):
    levels, lat_rows, lon_cols, feat = fields.shape
    heads = rel_table.shape[1]
    rels = rel_table.shape[2] // (levels * levels * lat_rows * lat_rows)
    lon_width = (rels + 1) // 2
    half_rows = lat_rows // 2
    half_cols = lon_width // 2
    windows = lon_cols // lon_width
    lats = lax.axis_size("lat")
    lons = lax.axis_size("lon")
    me_lat = lax.axis_index("lat")
    me_lon = lax.axis_index("lon")
    part = w_query.shape[0]

    both = jnp.stack([fields, cotangent]).transpose(3, 0, 1, 2, 4)

    mine = jnp.concatenate([w_query, w_key, w_value, w_out], axis=1)
    rows_all = spread_over_lat(jnp.broadcast_to(mine[None], (lats,) + mine.shape))
    turned = turn(rows_all, lons // 2)
    turned, table = lax.optimization_barrier((turned, rel_table[0]))
    w_same = spread_over_lon(turned)
    own = both[half_cols:, :, :, half_rows:]
    south = shift(both[half_cols:, :, :, :half_rows], -1, 0)
    east = shift(both[:half_cols, :, :, half_rows:], 0, -1)
    corner = shift(both[:half_cols, :, :, :half_rows], -1, -1)

    order = jnp.asarray(offset_order(rels, levels, lat_rows, 256), BF16)
    last = (me_lat == lats - 1).astype(jnp.int32).reshape(1)
    slots = heads + -heads % 16
    bias = make_bias(last, table, order, levels, lat_rows, rels, slots, windows)
    w_same, bias, own, south, east, corner = lax.optimization_barrier((w_same, bias, own, south, east, corner))
    w_other = swap(w_same, "lon", 1)
    moved = jnp.concatenate(
        [jnp.concatenate([own, south], axis=3), jnp.concatenate([east, corner], axis=3)], axis=0
    )
    shifted = moved[:, 0].reshape(-1, feat)
    cot_shift = moved[:, 1].reshape(-1, feat)

    me = me_lon.reshape(1)
    gain = norm_gain[None]
    g_same, g_other, dq, dk, dv = run_block(
        me, shifted, cot_shift, gain, w_same, w_other, bias, order, heads, windows, levels, lat_rows, rels
    )

    paired = (g_same.astype(F32) + swap(g_other, "lon", 1).astype(F32)).astype(BF16)
    d_input = input_gradient(me, shifted, gain, w_same, w_other, dq, dk, dv)
    paired, d_input = lax.optimization_barrier((paired, d_input))
    arrived = spread_over_lon(paired)
    message, lines = sum_and_turn(arrived, lats, 4 * part)
    grad_query, grad_key, grad_value, grad_out, grad_gain = last_sum(spread_over_lat(message), part, feat)

    d_in = d_input.reshape(lon_cols, levels, lat_rows, feat)
    stay = lon_cols - half_cols
    west = shift(d_in[stay:, :, :half_rows], 0, 1)
    north = shift(d_in[:stay, :, half_rows:], 1, 0)
    corner = shift(d_in[stay:, :, half_rows:], 1, 1)
    west, north, corner, d_in, lines, _ = lax.optimization_barrier((west, north, corner, d_in, lines, message))
    over = rel_table.shape[2] // lons - feat
    groups = feat // 128
    tail = lines[heads:].reshape(slots - heads, groups, 128)[:, :, :over].transpose(1, 0, 2)
    grad_table = jnp.concatenate([lines[:heads], tail.reshape(heads, over)], axis=1)[None]
    back = jnp.concatenate(
        [jnp.concatenate([corner, west], axis=2), jnp.concatenate([north, d_in[:stay, :, :half_rows]], axis=2)],
        axis=0,
    ).transpose(1, 2, 0, 3)
    grad_fields = (cotangent.astype(F32) + back.astype(F32)).astype(BF16)
    return (grad_fields, grad_query, grad_key, grad_value, grad_out, grad_table, grad_gain)


def solution(mesh):
    return jax.shard_map(
        local,
        mesh=mesh,
        in_specs=(
            P(None, "lat", "lon", None),
            P(None, "lat", "lon", None),
            P(),
            P("lat", "lon"),
            P("lat", "lon"),
            P("lat", "lon"),
            P("lat", "lon"),
            P("lat", None, None),
        ),
        out_specs=(
            P(None, "lat", "lon", None),
            P("lat", "lon"),
            P("lat", "lon"),
            P("lat", "lon"),
            P("lat", "lon"),
            P("lat", None, "lon"),
            P(),
        ),
        check_vma=False,
    )
```
